32 devices in a mesh: orb: 8 (over z, core), vec: 4 (over y, x).
Axes of the slice: x: 2, y: 2, z: 4, core: 2. Of those that a mesh axis runs over, the one named last changes fastest.
Arguments:
- orbitals: bfloat16 [8, 96, 9216], P('orb'), may hold values from -6 to 6
- energies: float32 [8], P('orb'), may hold values from -1 to 0
- trial_potential: bfloat16 [4, 96, 9216], P('vec', 'orb'), may hold values from -6 to 6
- local_potential: bfloat16 [96, 9216], P('orb'), may hold values from 0.5 to 2
Outputs:
- ortho: float32 [4, 96, 9216], P('vec', 'orb')
- factor: float32 [4, 4], replicated
The draws below stay inside these ranges and needn't reach their ends.
All inputs are finite; a program needn't handle non-finite values.
Results may differ from the reference program's by a relative error of at most 0.0003.
Values may be sent and summed in bfloat16 or wider, within the bound.
No kernel may reach another device: no remote copies, remote signals or barrier semaphores. Data moves between devices by JAX's collectives and lax.ppermute only.
A program may use at most 64 MiB of HBM per device.

```python
import jax
import jax.numpy as jnp
from jax import lax

NZ = 96
NY = 96
NX = 96
NYX = 9216
STEPS = 4
NORB = 8
NV = 4


def level_of(own_key, dims, cuts, least, largest):
    loudness = 1.0
    for position, shards_of in cuts:
        steps = jax.random.uniform(jax.random.fold_in(jax.random.fold_in(own_key, 6), position), (shards_of,), jnp.float32, least / len(cuts), largest / len(cuts))
        loudness = loudness * jnp.repeat(jnp.exp(steps), dims[position] // shards_of).reshape((-1,) + (1,) * (len(dims) - 1 - position))
    return loudness


def normal_values(rng, shape, width, bound, split=(), kind=jnp.bfloat16):
    drawn = jax.random.normal(rng, shape, jnp.float32) * width
    if len(split) > 0:
        drawn = level_of(rng, shape, split, -0.22, 0.18) * drawn
    return jnp.clip(drawn, min=-bound, max=bound).astype(kind)


def setup_inputs(seed: int = 0) -> dict:
    seeds = jax.random.split(jax.random.key(seed), 5)
    orbitals = normal_values(seeds[0], (NORB, NZ, NYX), 1.0, 6.0, ((0, 8),))
    energies = jnp.clip(-1.0 + 1.0 * jax.random.uniform(seeds[1], (NORB,), jnp.float32) ** level_of(seeds[1], (NORB,), ((0, 8),), -0.2, 0.2), -1.0, 0.0)
    trial_potential = normal_values(seeds[2], (NV, NZ, NYX), 1.0, 6.0, ((0, 4), (1, 8)))
    local_potential = jnp.clip(0.5 + 1.5 * jax.random.uniform(seeds[3], (NZ, NYX), jnp.float32) ** level_of(seeds[3], (NZ, NYX), ((0, 8),), -0.2, 0.2), 0.5, 2.0).astype(jnp.bfloat16)
    return {"orbitals": orbitals, "energies": energies, "trial_potential": trial_potential, "local_potential": local_potential}


def neighbours(field):
    depth, flat = field.shape
    zero_plane = jnp.zeros((1, flat), field.dtype)
    total = jnp.concatenate([zero_plane, field[:-1]], 0) + jnp.concatenate([field[1:], zero_plane], 0)
    zero_rows = jnp.zeros((depth, NX), field.dtype)
    total = total + jnp.concatenate([zero_rows, field[:, :-NX]], 1) + jnp.concatenate([field[:, NX:], zero_rows], 1)
    column = jnp.arange(flat) % NX
    zero_col = jnp.zeros((depth, 1), field.dtype)
    left = jnp.concatenate([zero_col, field[:, :-1]], 1) * (column > 0).astype(field.dtype)
    right = jnp.concatenate([field[:, 1:], zero_col], 1) * (column < NX - 1).astype(field.dtype)
    return total + left + right

def solve(psi, perturb, potential, energy):
    diag = 3.25 + potential - energy
    source = -perturb * psi
    answer = jnp.zeros_like(psi)
    for step in range(STEPS):
        weight = 1.0 / (1.0 + 0.8 * jnp.cos(jnp.pi * (2 * step + 1) / (2 * STEPS)))
        applied = diag * answer - 0.5 * neighbours(answer)
        answer = answer + weight * (source - applied) / diag
    return answer

def sine_basis(count):
    index = jnp.arange(count, dtype=jnp.float32) + 1.0
    return jnp.sqrt(2.0 / (count + 1)) * jnp.sin(jnp.pi * index[:, None] * index[None, :] / (count + 1))

def eigen_values(count):
    index = jnp.arange(count, dtype=jnp.float32) + 1.0
    return 2.0 - 2.0 * jnp.cos(jnp.pi * index / (count + 1))

def transform(cube):
    high = lax.Precision.HIGHEST
    cube = jnp.einsum('zyx,cx->zyc', cube, sine_basis(NX), precision=high)
    cube = jnp.einsum('zyc,by->zbc', cube, sine_basis(NY), precision=high)
    return jnp.einsum('zbc,az->abc', cube, sine_basis(NZ), precision=high)

def coulomb(field):
    cube = transform(field.reshape(NZ, NY, NX))
    denom = eigen_values(NZ)[:, None, None] + eigen_values(NY)[None, :, None] + eigen_values(NX)[None, None, :]
    cube = cube * (jnp.sqrt(4.0 * jnp.pi) / jnp.sqrt(denom))
    return transform(cube).reshape(NZ, NYX)

def reference(orbitals, energies, trial_potential, local_potential):
    potential = local_potential.astype(jnp.float32)

    def one_vector(vector):
        perturb = vector.astype(jnp.float32)

        def add_orbital(index, total):
            psi = lax.dynamic_index_in_dim(orbitals, index, 0, keepdims=False).astype(jnp.float32)
            return total + psi * solve(psi, perturb, potential, energies[index])
        chi = lax.fori_loop(0, NORB, add_orbital, jnp.zeros((NZ, NYX), jnp.float32))
        return coulomb(chi * (4.0 / NORB))
    responses = lax.map(one_vector, trial_potential)
    flat = responses.reshape(NV, NZ * NYX)
    gram = jnp.dot(flat, flat.T, precision=lax.Precision.HIGHEST) / (NZ * NYX)
    lower = jnp.linalg.cholesky(gram)
    inverse = lax.linalg.triangular_solve(lower, jnp.eye(NV, dtype=jnp.float32), left_side=True, lower=True)
    ortho = jnp.dot(inverse, flat, precision=lax.Precision.HIGHEST)
    return (ortho.reshape(NV, NZ, NYX), lower.T)
```

```python
import functools
import math

import jax
import jax.numpy as jnp
import ml_dtypes
import numpy as np
from jax import lax
from jax.experimental import pallas as pl
from jax.experimental.pallas import tpu as pltpu
from jax.sharding import PartitionSpec as P

NZ = 96
NY = 96
NX = 96
STEPS = 4

BF16 = jnp.bfloat16
F32 = jnp.float32
LANES = 128
WEIGHTS = [1.0 / (1.0 + 0.8 * math.cos(math.pi * (2 * s + 1) / (2 * STEPS))) for s in range(STEPS)]


def neighbours(field):
    depth, flat = field.shape
    zero_plane = jnp.zeros((1, flat), field.dtype)
    total = jnp.concatenate([zero_plane, field[:-1]], 0) + jnp.concatenate(
        [field[1:], zero_plane], 0
    )
    zero_rows = jnp.zeros((depth, NX), field.dtype)
    total = (
        total
        + jnp.concatenate([zero_rows, field[:, :-NX]], 1)
        + jnp.concatenate([field[:, NX:], zero_rows], 1)
    )
    column = jnp.arange(flat) % NX
    zero_col = jnp.zeros((depth, 1), field.dtype)
    left = jnp.concatenate([zero_col, field[:, :-1]], 1) * (column > 0).astype(field.dtype)
    right = jnp.concatenate([field[:, 1:], zero_col], 1) * (column < NX - 1).astype(field.dtype)
    return total + left + right


def solve(psi, perturb, potential, energy):
    diag = 3.25 + potential - energy
    source = -perturb * psi
    answer = jnp.zeros_like(psi)
    for step in range(STEPS):
        weight = 1.0 / (1.0 + 0.8 * jnp.cos(jnp.pi * (2 * step + 1) / (2 * STEPS)))
        applied = diag * answer - 0.5 * neighbours(answer)
        answer = answer + weight * (source - applied) / diag
    return answer


def sine_basis(count):
    index = jnp.arange(count, dtype=jnp.float32) + 1.0
    return jnp.sqrt(2.0 / (count + 1)) * jnp.sin(
        jnp.pi * index[:, None] * index[None, :] / (count + 1)
    )


def eigen_of(position, count):
    return 2.0 - 2.0 * jnp.cos(jnp.pi * (position.astype(jnp.float32) + 1.0) / (count + 1))


def planes(field):
    high = lax.Precision.HIGHEST
    depth = field.shape[0]
    cube = field.reshape(depth, NY, NX)
    cube = jnp.einsum("zyx,cx->zyc", cube, sine_basis(NX), precision=high)
    cube = jnp.einsum("zyc,by->zbc", cube, sine_basis(NY), precision=high)
    return cube.reshape(depth, NY * NX)


def scale_columns(columns, start):
    high = lax.Precision.HIGHEST
    width = columns.shape[1]
    position = start + jnp.arange(width)
    denom = (
        eigen_of(jnp.arange(NZ), NZ)[:, None]
        + eigen_of(position // NX, NY)[None, :]
        + eigen_of(position % NX, NX)[None, :]
    )
    basis = sine_basis(NZ)
    spectral = jnp.dot(basis, columns, precision=high) * (jnp.sqrt(4.0 * jnp.pi) / jnp.sqrt(denom))
    return jnp.dot(basis, spectral, precision=high)


def coulomb_slab(slab):
    columns = lax.all_to_all(planes(slab), "orb", split_axis=1, concat_axis=0, tiled=True)
    scaled = scale_columns(columns, lax.axis_index("orb") * columns.shape[1])
    back = lax.all_to_all(scaled, "orb", split_axis=0, concat_axis=1, tiled=True)
    return planes(back)


def factorize(partial_gram):
    lower = jnp.linalg.cholesky(partial_gram / (NZ * NY * NX))
    inverse = lax.linalg.triangular_solve(
        lower, jnp.eye(lower.shape[0], dtype=jnp.float32), left_side=True, lower=True
    )
    return (lower, inverse)


def general_body(orbitals, energies, trial_potential, local_potential):
    high = lax.Precision.HIGHEST
    depth = local_potential.shape[0]
    plane_cells = local_potential.shape[1]
    vector_slab = trial_potential.reshape(depth, plane_cells)
    perturb_full, potential_full = (
        lax.all_gather(vector_slab, "orb", axis=0, tiled=True),
        lax.all_gather(local_potential, "orb", axis=0, tiled=True),
    )
    perturb = perturb_full.astype(jnp.float32)
    potential = potential_full.astype(jnp.float32)
    weight = 4.0 / (orbitals.shape[0] * lax.axis_size("orb"))
    psi = orbitals[0].astype(jnp.float32)
    partial_value = psi * solve(psi, perturb, potential, energies[0])
    partial_value = partial_value * weight
    slab = lax.psum_scatter(partial_value, "orb", scatter_dimension=0, tiled=True)
    slab = coulomb_slab(slab)
    mine = slab.reshape(1, depth, plane_cells)
    gathered = lax.all_gather(mine, "vec", axis=0, tiled=True)
    flat = gathered.reshape(gathered.shape[0], depth * plane_cells)
    partial_gram = jnp.dot(flat, flat.T, precision=high)
    lower, inverse = factorize(lax.psum(partial_gram, "orb"))
    row = lax.dynamic_slice_in_dim(inverse, lax.axis_index("vec"), 1, 0)
    ortho = jnp.dot(row, flat, precision=high).reshape(1, depth, plane_cells)
    return (ortho, lower.T)


TILES = 3
GROUP = 4
SUB = 8
ROWS = GROUP * SUB
WTILES = TILES * SUB
HALO = STEPS - 1


def fits(orb, vec, norb, nv):
    return (
        norb == orb
        and nv == vec
        and orb % 2 == 0
        and NZ % orb == 0
        and NZ // orb >= 4
        and NZ // orb % 2 == 0
        and NY == vec * (ROWS - 2 * GROUP)
        and NY == TILES * ROWS
        and vec * ROWS == LANES
        and NX * GROUP == TILES * LANES
        and NX % (orb * vec) == 0
        and NZ % (orb * vec) == 0
        and STEPS <= GROUP
    )


def split(x):
    high = x.astype(BF16)
    return high, (x - high.astype(F32)).astype(BF16)


def np_split(x):
    x = np.asarray(x, np.float64)
    high = x.astype(ml_dtypes.bfloat16)
    return np.stack([high, (x - high.astype(np.float64)).astype(ml_dtypes.bfloat16)])


def dot3(a, b, dims):
    one = functools.partial(
        lax.dot_general, dimension_numbers=(dims, ((), ())), preferred_element_type=F32
    )
    return one(a[0], b[0]) + (one(a[0], b[1]) + one(a[1], b[0]))


def np_basis(count):
    index = np.arange(count, dtype=np.float64) + 1.0
    return np.sqrt(2.0 / (count + 1)) * np.sin(np.pi * np.outer(index, index) / (count + 1))


def np_eigen(count):
    return 4.0 * np.sin(np.pi * (np.arange(count, dtype=np.float64) + 1.0) / (2 * (count + 1))) ** 2


def to_rows(tiles):
    lane = lax.broadcasted_iota(jnp.int32, tiles[0].shape, 1)
    a, b, c = tiles
    return [
        a,
        pltpu.roll(jnp.where(lane >= 96, a, b), 32, 1),
        pltpu.roll(jnp.where(lane >= 64, b, c), 64, 1),
        pltpu.roll(c, 96, 1),
    ]


def to_tiles(rows):
    lane = lax.broadcasted_iota(jnp.int32, rows[0].shape, 1)
    r1, r2 = pltpu.roll(rows[1], 96, 1), pltpu.roll(rows[2], 64, 1)
    return [
        jnp.where(lane < 96, rows[0], r1),
        jnp.where(lane < 64, r1, r2),
        jnp.where(lane < 32, r2, pltpu.roll(rows[3], 32, 1)),
    ]


def first_tile(strip):
    return strip * (WTILES - 2 * TILES) - TILES


def tile_lanes(strip, t):
    tile = jnp.clip(first_tile(strip) + t, 0, NY * NX // LANES - 1)
    return pl.ds(pl.multiple_of(tile * LANES, LANES), LANES)


def pack_planes(src, plane, out, pairs):
    def one(pair, carry):
        for i in range(TILES):
            top = pl.multiple_of((plane + 2 * pair) * WTILES + i * SUB, SUB)
            low = pl.multiple_of((plane + 2 * pair + 1) * WTILES + i * SUB, SUB)
            block = jnp.concatenate([src[pl.ds(top, SUB), :], src[pl.ds(low, SUB), :]], 0)
            out[pair, i] = block.astype(BF16)
        return carry

    lax.fori_loop(0, pairs, one, 0)


def orbital_windows_kernel(orb, energy_ref, psi_ref, *refs):
    outs, planes_ref = refs[:-1], refs[-1]
    chips = orb // 2
    slab = NZ // chips
    chip = lax.axis_index("orb") // 2
    strip = lax.axis_index("vec")
    zero = jnp.zeros((HALO * WTILES, LANES), F32)
    planes_ref[: HALO * WTILES, :] = zero
    planes_ref[(NZ + HALO) * WTILES :, :] = zero
    for t in range(WTILES):
        row = HALO * WTILES + (t % TILES) * SUB + t // TILES
        planes_ref[pl.ds(row, NZ, WTILES), :] = psi_ref[0, :, tile_lanes(strip, t)].astype(F32)
    energy = jnp.full((1, LANES), energy_ref[0], F32)
    high = energy.astype(BF16).astype(F32)
    middle = (energy - high).astype(BF16).astype(F32)
    low = energy - high - middle
    lane = lax.broadcasted_iota(jnp.int32, (1, LANES), 1)
    for at in range(chips):
        row = at * slab * WTILES
        held = planes_ref[row : row + 1, :]
        held = jnp.where(lane == 0, high, jnp.where(lane == 1, middle, jnp.where(lane == 2, low, held)))
        planes_ref[row : row + 1, :] = held
    for shift in range(chips):
        pack_planes(planes_ref, ((chip + shift) % chips) * slab, outs[shift], (slab + 2 * HALO) // 2)


def orbital_windows(orbitals, energies, orb):
    chips = orb // 2
    pairs = (NZ // chips + 2 * HALO) // 2
    return pl.pallas_call(
        functools.partial(orbital_windows_kernel, orb),
        out_shape=[jax.ShapeDtypeStruct((pairs, TILES, 2 * SUB, LANES), BF16)] * chips,
        in_specs=[
            pl.BlockSpec(memory_space=pltpu.SMEM),
            pl.BlockSpec(memory_space=pltpu.VMEM),
        ],
        out_specs=[pl.BlockSpec(memory_space=pltpu.VMEM)] * chips,
        scratch_shapes=[pltpu.VMEM(((NZ + 2 * HALO) * WTILES, LANES), F32)],
        compiler_params=pltpu.CompilerParams(vmem_limit_bytes=24 << 20),
        name="orbital_windows",
    )(energies, orbitals)


def potential_windows_kernel(vec, v_ref, pot_ref, halo_ref, *refs):
    outs, planes_ref = refs[:-1], refs[-1]
    core = lax.axis_index("orb") % 2
    strip = lax.axis_index("vec")
    depth = v_ref.shape[1]
    half = depth + GROUP
    own = (1 - core) * GROUP
    other = core * depth
    for n in range(vec + 1):
        src, part, to = (v_ref.at[0], 0, lax.rem(strip + n, vec)) if n < vec else (pot_ref, GROUP, strip)
        for t in range(WTILES):
            row = (n * half) * WTILES + (t % TILES) * SUB + t // TILES
            lanes = tile_lanes(to, t)
            planes_ref[pl.ds(row + own * WTILES, depth, WTILES), :] = src[:, lanes].astype(F32)
            edge = halo_ref[:, lanes].astype(F32)[part : part + GROUP]
            planes_ref[pl.ds(row + other * WTILES, GROUP, WTILES), :] = edge
        pack_planes(planes_ref, n * half, outs[n], half // 2)


def potential_windows(trial, potential, halo, vec):
    half = potential.shape[0] + GROUP
    return pl.pallas_call(
        functools.partial(potential_windows_kernel, vec),
        out_shape=[jax.ShapeDtypeStruct((half // 2, TILES, 2 * SUB, LANES), BF16)] * (vec + 1),
        in_specs=[pl.BlockSpec(memory_space=pltpu.VMEM)] * 3,
        out_specs=[pl.BlockSpec(memory_space=pltpu.VMEM)] * (vec + 1),
        scratch_shapes=[pltpu.VMEM(((vec + 1) * half * WTILES, LANES), F32)],
        compiler_params=pltpu.CompilerParams(vmem_limit_bytes=24 << 20),
        name="potential_windows",
    )(trial, potential, halo)


def potential_rows_kernel(vec, mine_ref, other_ref, v_ref, d_ref):
    core = lax.axis_index("orb") % 2
    strip = lax.axis_index("vec")
    pairs = mine_ref.shape[1]
    for src, first in ((mine_ref, core * pairs), (other_ref, (1 - core) * pairs)):

        def one(pair, carry, src=src, first=first):
            plane = 2 * (first + pair)
            for n in range(vec + 1):
                rows = to_rows([src[n, pair, i].astype(F32) for i in range(TILES)])
                for zz in range(2):
                    for i in range(GROUP):
                        row = rows[i][zz * SUB : (zz + 1) * SUB]
                        if n < vec:
                            v_ref[lax.rem(strip - n + vec, vec), plane + zz, i] = row
                        else:
                            d_ref[plane + zz, i] = 3.25 + row
            return carry

        lax.fori_loop(0, pairs, one, 0)


def potential_rows(mine, other, vec):
    planes = 4 * mine.shape[1]
    return pl.pallas_call(
        functools.partial(potential_rows_kernel, vec),
        out_shape=[
            jax.ShapeDtypeStruct((vec, planes, GROUP, SUB, LANES), F32),
            jax.ShapeDtypeStruct((planes, GROUP, SUB, LANES), F32),
        ],
        in_specs=[pl.BlockSpec(memory_space=pltpu.VMEM)] * 2,
        out_specs=[pl.BlockSpec(memory_space=pltpu.VMEM)] * 2,
        compiler_params=pltpu.CompilerParams(vmem_limit_bytes=24 << 20),
        name="potential_rows",
    )(mine, other)


def solve_kernel(vec, first, last, *refs):
    psi_ref, v_ref, d_ref = refs[:3]
    refs = refs[3:]
    sum_ref = None if first else refs[0]
    outs = refs[0 if first else 1 : -5]
    psi_s, h_s, c_s, u_a, u_b = refs[-5:]
    planes = d_ref.shape[0]
    depth = (planes - 2 * GROUP) // 2
    core = lax.axis_index("orb") % 2
    top = (lax.axis_index("orb") // 2) * 2 * depth - GROUP
    top_row = lax.axis_index("vec") * (ROWS - 2 * GROUP) - GROUP
    lane = lax.broadcasted_iota(jnp.int32, (SUB, LANES), 1)
    group = lax.broadcasted_iota(jnp.int32, (SUB, LANES), 0)
    inside = []
    for i in range(GROUP):
        y = top_row + group * GROUP + i
        inside.append(jnp.where((y >= 0) & (y < NY) & (lane < NX), 0.5, 0.0))
    block = psi_ref[0, 0].astype(F32)
    energy = block[0:1, 0:1] + block[0:1, 1:2] + block[0:1, 2:3]

    def begin(pair, carry):
        rows = to_rows([psi_ref[pair, i].astype(F32) for i in range(TILES)])
        for zz in range(2):
            w = GROUP - HALO + 2 * pair + zz
            z = top + w
            there = jnp.where((z >= 0) & (z < NZ), 1.0, 0.0)
            for i in range(GROUP):
                psi = rows[i][zz * SUB : (zz + 1) * SUB]
                h = inside[i] * there / (d_ref[w, i] - energy)
                psi_s[w, i] = psi
                h_s[w, i] = h
                scaled = -2.0 * psi * h
                for k in range(vec):
                    c = scaled * v_ref[k, w, i]
                    c_s[k, w, i] = c
                    u_a[k, w, i] = WEIGHTS[0] * c
        return carry

    lax.fori_loop(0, psi_ref.shape[0], begin, 0)

    def stepped(src, k, w, weight):
        u = [src[k, w, i] for i in range(GROUP)]
        new = []
        for i in range(GROUP):
            north = u[i - 1] if i > 0 else pltpu.roll(u[GROUP - 1], 1, 0)
            south = u[i + 1] if i < GROUP - 1 else pltpu.roll(u[0], SUB - 1, 0)
            near = (src[k, w - 1, i] + src[k, w + 1, i]) + (north + south)
            near = near + (pltpu.roll(u[i], 1, 1) + pltpu.roll(u[i], LANES - 1, 1))
            new.append((1.0 - weight) * u[i] + weight * (c_s[k, w, i] + h_s[w, i] * near))
        return new

    src, dst = u_a, u_b
    for step in range(1, STEPS - 1):
        low = GROUP - HALO + step

        def middle(w, carry, src=src, dst=dst, step=step):
            for k in range(vec):
                for i, new in enumerate(stepped(src, k, w, WEIGHTS[step])):
                    dst[k, w, i] = new
            return carry

        lax.fori_loop(low, planes - low, middle, 0)
        src, dst = dst, src

    def end(p, carry, out, start, src=src):
        w = GROUP + start + p
        for k in range(vec):
            for i, new in enumerate(stepped(src, k, w, WEIGHTS[STEPS - 1])):
                rows = pl.ds(k * ROWS + i * SUB, SUB)
                total = psi_s[w, i] * new
                if not first:
                    total = total + sum_ref[start + p, rows, :]
                out[p, rows, :] = total
        return carry

    if last:
        lax.fori_loop(0, depth, functools.partial(end, out=outs[1], start=(1 - core) * depth), 0)
        lax.fori_loop(0, depth, functools.partial(end, out=outs[0], start=core * depth), 0)
    else:
        lax.fori_loop(0, 2 * depth, functools.partial(end, out=outs[0], start=0), 0)


def solve_window(psi, v, d, total, vec, last):
    planes = d.shape[0]
    depth = (planes - 2 * GROUP) // 2
    first = total is None
    if last:
        outs = [jax.ShapeDtypeStruct((depth, LANES, LANES), F32)] * 2
    else:
        outs = [jax.ShapeDtypeStruct((2 * depth, LANES, LANES), F32)]
    args = (psi, v, d) if first else (psi, v, d, total)
    rows = (planes, GROUP, SUB, LANES)
    got = pl.pallas_call(
        functools.partial(solve_kernel, vec, first, last),
        out_shape=outs,
        in_specs=[pl.BlockSpec(memory_space=pltpu.VMEM)] * len(args),
        out_specs=[pl.BlockSpec(memory_space=pltpu.VMEM)] * len(outs),
        scratch_shapes=[pltpu.VMEM(rows, F32)] * 2 + [pltpu.VMEM((vec, *rows), F32)] * 3,
        compiler_params=pltpu.CompilerParams(vmem_limit_bytes=32 << 20),
        name="solve_window",
    )(*args)
    return got if last else got[0]


def forward_x_kernel(ndev, basis_ref, own_ref, other_ref, out_ref):
    depth = own_ref.shape[0]
    parts = NX // ndev
    rows = out_ref.shape[0] // ndev
    basis = (basis_ref[0], basis_ref[1])
    for z in range(depth):
        chi = split(own_ref[z] + other_ref[z])
        got = dot3(basis, chi, ((1,), (1,)))
        for part in range(parts):
            out_ref[pl.ds(part * depth + z, ndev, rows), :] = got[part * ndev : (part + 1) * ndev]
    for row in range(parts * depth, rows):
        out_ref[pl.ds(row, ndev, rows), :] = jnp.zeros((ndev, LANES), F32)


def forward_x(own, other, basis, ndev):
    rows = -(-(NX // ndev) * own.shape[0] // SUB) * SUB
    out = pl.pallas_call(
        functools.partial(forward_x_kernel, ndev),
        out_shape=jax.ShapeDtypeStruct((ndev * rows, LANES), F32),
        in_specs=[pl.BlockSpec(memory_space=pltpu.VMEM)] * 3,
        out_specs=pl.BlockSpec(memory_space=pltpu.VMEM),
        compiler_params=pltpu.CompilerParams(vmem_limit_bytes=24 << 20),
        name="forward_x",
    )(basis, own, other)
    return out.reshape(ndev, rows, LANES)


def spectral_kernel(orb, vec, mux_ref, muzy_ref, wy_ref, kz_ref, kzb_ref, wyb_ref, got_ref, out_ref):
    ndev = orb * vec
    parts = NX // ndev
    me = lax.axis_index("orb") * vec + lax.axis_index("vec")
    rows = got_ref.shape[1]
    x = jnp.concatenate(
        [
            jnp.concatenate([got_ref[o * vec + v] for o in range(orb)], 0)
            for v in range(vec)
        ],
        1,
    )
    mm = ((1,), (0,))
    t = dot3(split(x), (wy_ref[0], wy_ref[1]), mm)
    t = dot3((kz_ref[0], kz_ref[1]), split(t), mm)
    scale = jnp.concatenate(
        [
            math.sqrt(4.0 * math.pi) / jnp.sqrt(muzy_ref[...] + mux_ref[part * ndev + me])
            for part in range(parts)
        ],
        0,
    )
    fields = [t[:, k * LANES : (k + 1) * LANES] * scale for k in range(vec)]
    lane = lax.broadcasted_iota(jnp.int32, (1, LANES), 1)
    gram = jnp.zeros((1, LANES), F32)
    for k in range(vec):
        for l in range(k + 1):
            entry = jnp.sum(jnp.sum(fields[k] * fields[l], axis=0, keepdims=True), axis=1, keepdims=True)
            gram = jnp.where(lane == k * vec + l, entry, gram)
    t = jnp.concatenate(fields, 1)
    t = dot3((kzb_ref[0], kzb_ref[1]), split(t), mm)
    t = dot3(split(t), (wyb_ref[0], wyb_ref[1]), mm)
    rows = out_ref.shape[0] // ndev
    groups = t.shape[0] // ndev
    for r in range(groups):
        for yt in range(TILES):
            out_ref[pl.ds(r * TILES + yt, ndev, rows), :] = t[
                r * ndev : (r + 1) * ndev, yt * LANES : (yt + 1) * LANES
            ]
    out_ref[pl.ds(groups * TILES, ndev, rows), :] = jnp.broadcast_to(gram, (ndev, LANES))


def spectral(got, orb, vec):
    ndev = orb * vec
    parts, zs = NX // ndev, NZ // ndev
    depth = NZ // orb
    strip = ROWS - 2 * GROUP
    rows_in = got.shape[1]
    rows_out = -(-(parts * zs * TILES + 1) // SUB) * SUB
    sy, sz = np_basis(NY), np_basis(NZ)
    wy = np.zeros((vec, vec, GROUP, SUB, vec, LANES))
    wyb = np.zeros((vec, LANES, TILES, vec, GROUP, SUB))
    for k in range(vec):
        for i in range(GROUP):
            for g in range(SUB):
                for v in range(vec):
                    row = v * strip - GROUP + GROUP * g + i
                    if v * strip <= row < (v + 1) * strip:
                        wy[v, k, i, g, k, :NY] = sy[row]
                for yt in range(TILES):
                    wyb[k, :NY, yt, k, i, g] = sy[yt * ROWS + GROUP * g + i]
    wy = wy.reshape(vec * LANES, vec * LANES)
    wyb = wyb.reshape(vec * LANES, TILES * LANES)
    kz = np.zeros((parts, NZ, orb, rows_in))
    kzb = np.zeros((zs, parts, ndev, parts, NZ))
    for part in range(parts):
        for o in range(orb):
            kz[part, :, o, part * depth : (part + 1) * depth] = sz[:, o * depth : (o + 1) * depth]
        for z in range(zs):
            kzb[z, part, :, part, :] = sz[z::zs]
    kz = kz.reshape(parts * NZ, orb * rows_in)
    kzb = kzb.reshape(zs * parts * ndev, parts * NZ)
    muzy = np.ones((NZ, LANES), np.float32)
    muzy[:, :NY] = np_eigen(NZ)[:, None] + np_eigen(NY)[None, :]
    mux = np_eigen(NX).astype(np.float32)
    out = pl.pallas_call(
        functools.partial(spectral_kernel, orb, vec),
        out_shape=jax.ShapeDtypeStruct((ndev * rows_out, LANES), F32),
        in_specs=[pl.BlockSpec(memory_space=pltpu.SMEM)] + [pl.BlockSpec(memory_space=pltpu.VMEM)] * 6,
        out_specs=pl.BlockSpec(memory_space=pltpu.VMEM),
        compiler_params=pltpu.CompilerParams(vmem_limit_bytes=32 << 20),
        name="spectral",
    )(mux, muzy, np_split(wy), np_split(kz), np_split(kzb), np_split(wyb), got)
    return out.reshape(ndev, rows_out, LANES)


def back_kernel(ndev, vec, basis_ref, got_ref, factor_ref, *outs):
    parts, zs = NX // ndev, NZ // ndev
    rows = got_ref.shape[0] // ndev
    strip = lax.axis_index("vec")
    basis = (basis_ref[0], basis_ref[1])
    gram = jnp.sum(got_ref[pl.ds(zs * parts * TILES, ndev, rows), :], axis=0, keepdims=True)
    gram = gram / (NZ * NY * NX)
    entry = lambda k, l: gram[:, k * vec + l : k * vec + l + 1]
    lower = [[None] * vec for _ in range(vec)]
    inverse = [[jnp.zeros((1, 1), F32)] * vec for _ in range(vec)]
    for l in range(vec):
        pivot = entry(l, l)
        for m in range(l):
            pivot = pivot - lower[l][m] * lower[l][m]
        lower[l][l] = jnp.sqrt(pivot)
        inverse[l][l] = 1.0 / lower[l][l]
        for k in range(l + 1, vec):
            value = entry(k, l)
            for m in range(l):
                value = value - lower[k][m] * lower[l][m]
            lower[k][l] = value * inverse[l][l]
    for l in range(vec):
        for k in range(l + 1, vec):
            value = lower[k][l] * inverse[l][l]
            for m in range(l + 1, k):
                value = value + lower[k][m] * inverse[m][l]
            inverse[k][l] = -value * inverse[k][k]
    at_row = lax.broadcasted_iota(jnp.int32, (vec, vec), 0)
    at_col = lax.broadcasted_iota(jnp.int32, (vec, vec), 1)
    factor = jnp.zeros((vec, vec), F32)
    for k in range(vec):
        for l in range(k + 1):
            factor = jnp.where((at_row == l) & (at_col == k), lower[k][l], factor)
    factor_ref[...] = factor
    coefficients = []
    for s in range(vec):
        to = lax.rem(strip + s, vec)
        line = []
        for k in range(vec):
            value = inverse[0][k]
            for m in range(1, vec):
                value = jnp.where(to == m, inverse[m][k], value)
            line.append(value)
        coefficients.append(line)
    for z in range(zs):
        for yt in range(TILES):
            x = jnp.concatenate(
                [
                    got_ref[pl.ds((z * parts + part) * TILES + yt, ndev, rows), :]
                    for part in range(parts)
                ],
                0,
            )
            y = dot3(split(x), basis, ((0,), (0,)))
            for s in range(vec):
                mixed = coefficients[s][0] * y[:ROWS]
                for k in range(1, vec):
                    mixed = mixed + coefficients[s][k] * y[k * ROWS : (k + 1) * ROWS]
                tiles = to_tiles([mixed[i * SUB : (i + 1) * SUB] for i in range(GROUP)])
                for i in range(TILES):
                    outs[s][z, (yt * TILES + i) * SUB : (yt * TILES + i + 1) * SUB, :] = tiles[i]


def back(got, basis, ndev, vec):
    zs = NZ // ndev
    tiles = NY * NX // LANES
    return pl.pallas_call(
        functools.partial(back_kernel, ndev, vec),
        out_shape=[jax.ShapeDtypeStruct((vec, vec), F32)]
        + [jax.ShapeDtypeStruct((zs, tiles, LANES), F32)] * vec,
        in_specs=[pl.BlockSpec(memory_space=pltpu.VMEM)] * 2,
        out_specs=[pl.BlockSpec(memory_space=pltpu.VMEM)] * (vec + 1),
        compiler_params=pltpu.CompilerParams(vmem_limit_bytes=24 << 20),
        name="back",
    )(basis, got.reshape(-1, LANES))


def assemble_kernel(vec, *refs):
    gots, out_ref, all_ref = refs[:vec], refs[vec], refs[vec + 1]
    strip = lax.axis_index("vec")
    zs, tiles = gots[0].shape[:2]
    depth = zs * vec
    for s in range(vec):
        first = lax.rem(strip - s + vec, vec) * zs
        for z in range(zs):
            start = pl.multiple_of((first + z) * tiles, SUB)
            all_ref[pl.ds(start, tiles), :] = gots[s][z]
    for yt in range(TILES):
        for i in range(TILES):
            for g in range(SUB):
                row = (yt * TILES + i) * SUB + g
                tile = yt * WTILES + g * TILES + i
                out_ref[0, :, tile * LANES : (tile + 1) * LANES] = all_ref[pl.ds(row, depth, tiles), :]


def assemble(gots, vec):
    zs, tiles = gots[0].shape[:2]
    return pl.pallas_call(
        functools.partial(assemble_kernel, vec),
        out_shape=jax.ShapeDtypeStruct((1, zs * vec, tiles * LANES), F32),
        in_specs=[pl.BlockSpec(memory_space=pltpu.VMEM)] * vec,
        out_specs=pl.BlockSpec(memory_space=pltpu.VMEM),
        scratch_shapes=[pltpu.VMEM((zs * vec * tiles, LANES), F32)],
        compiler_params=pltpu.CompilerParams(vmem_limit_bytes=24 << 20),
        name="assemble",
    )(*gots)


def swap_cores(x, orb):
    return lax.ppermute(x, "orb", [(o, o ^ 1) for o in range(orb)])


def shift(x, axis, count):
    n = lax.axis_size(axis)
    return lax.ppermute(x, axis, [(i, (i + count) % n) for i in range(n)])


def responses(orbitals, energies, trial_potential, local_potential):
    orb, vec = lax.axis_size("orb"), lax.axis_size("vec")
    core = lax.axis_index("orb") % 2
    depth = local_potential.shape[0]
    chips = orb // 2
    edges = [
        jnp.concatenate([trial_potential[0, at : at + GROUP], local_potential[at : at + GROUP]], 0)
        for at in (0, depth - GROUP)
    ]
    edge = jnp.where(core == 0, edges[0], edges[1])
    pairs = [(o, o + 1) for o in range(1, orb - 1, 2)] + [(o + 1, o) for o in range(1, orb - 1, 2)]
    halo = lax.ppermute(edge, "orb", pairs)
    windows = orbital_windows(orbitals, energies, orb)
    psis = [windows[0]]
    for r in range(1, chips):
        perm = [(2 * a + c, 2 * ((a + r) % chips) + c) for a in range(chips) for c in range(2)]
        psis.append(lax.ppermute(windows[r], "orb", perm))
    parts = potential_windows(trial_potential, local_potential, halo, vec)
    mine = jnp.stack([parts[0]] + [shift(parts[n], "vec", n) for n in range(1, vec)] + [parts[vec]])
    v, d = potential_rows(mine, swap_cores(mine, orb), vec)
    total = None
    for r in range(chips):
        total = solve_window(psis[r], v, d, total, vec, r == chips - 1)
    return total[0], swap_cores(total[1], orb)


def block_body(orbitals, energies, trial_potential, local_potential):
    orb, vec = lax.axis_size("orb"), lax.axis_size("vec")
    ndev = orb * vec
    both = ("orb", "vec")
    own, other = responses(orbitals, energies, trial_potential, local_potential)
    sx = np_basis(NX)
    padded = np.zeros((NX, LANES))
    padded[:, :NX] = sx
    sent = forward_x(own, other, np_split(padded * (4.0 / orb)), ndev)
    got = lax.all_to_all(sent, both, 0, 0, tiled=True)
    sent = spectral(got, orb, vec)
    got = lax.all_to_all(sent, both, 0, 0, tiled=True)
    factor, *slots = back(got, np_split(padded), ndev, vec)
    gots = [slots[0]] + [shift(slots[s], "vec", s) for s in range(1, vec)]
    return assemble(gots, vec), factor


def solution(mesh):
    orb, vec = mesh.shape["orb"], mesh.shape["vec"]
    placed = (P("orb", None, None), P("orb"), P("vec", "orb", None), P("orb", None))

    def body(orbitals, energies, trial_potential, local_potential):
        one = orbitals.shape[0] == 1 and trial_potential.shape[0] == 1
        plan = block_body if one and fits(orb, vec, orb, vec) else general_body
        return plan(orbitals, energies, trial_potential, local_potential)

    return jax.shard_map(
        body, mesh=mesh, in_specs=placed, out_specs=(P("vec", "orb", None), P()), check_vma=False
    )
```

```python
import functools
import math

import jax
import jax.numpy as jnp
import ml_dtypes
import numpy as np
from jax import lax
from jax.experimental import pallas as pl
from jax.experimental.pallas import tpu as pltpu
from jax.sharding import PartitionSpec as P

NZ = 96
NY = 96
NX = 96
STEPS = 4

BF16 = jnp.bfloat16
F32 = jnp.float32
LANES = 128
WEIGHTS = [1.0 / (1.0 + 0.8 * math.cos(math.pi * (2 * s + 1) / (2 * STEPS))) for s in range(STEPS)]


def neighbours(field):
    depth, flat = field.shape
    zero_plane = jnp.zeros((1, flat), field.dtype)
    total = jnp.concatenate([zero_plane, field[:-1]], 0) + jnp.concatenate(
        [field[1:], zero_plane], 0
    )
    zero_rows = jnp.zeros((depth, NX), field.dtype)
    total = (
        total
        + jnp.concatenate([zero_rows, field[:, :-NX]], 1)
        + jnp.concatenate([field[:, NX:], zero_rows], 1)
    )
    column = jnp.arange(flat) % NX
    zero_col = jnp.zeros((depth, 1), field.dtype)
    left = jnp.concatenate([zero_col, field[:, :-1]], 1) * (column > 0).astype(field.dtype)
    right = jnp.concatenate([field[:, 1:], zero_col], 1) * (column < NX - 1).astype(field.dtype)
    return total + left + right


def solve(psi, perturb, potential, energy):
    diag = 3.25 + potential - energy
    source = -perturb * psi
    answer = jnp.zeros_like(psi)
    for step in range(STEPS):
        weight = 1.0 / (1.0 + 0.8 * jnp.cos(jnp.pi * (2 * step + 1) / (2 * STEPS)))
        applied = diag * answer - 0.5 * neighbours(answer)
        answer = answer + weight * (source - applied) / diag
    return answer


def sine_basis(count):
    index = jnp.arange(count, dtype=jnp.float32) + 1.0
    return jnp.sqrt(2.0 / (count + 1)) * jnp.sin(
        jnp.pi * index[:, None] * index[None, :] / (count + 1)
    )


def eigen_of(position, count):
    return 2.0 - 2.0 * jnp.cos(jnp.pi * (position.astype(jnp.float32) + 1.0) / (count + 1))


def planes(field):
    high = lax.Precision.HIGHEST
    depth = field.shape[0]
    cube = field.reshape(depth, NY, NX)
    cube = jnp.einsum("zyx,cx->zyc", cube, sine_basis(NX), precision=high)
    cube = jnp.einsum("zyc,by->zbc", cube, sine_basis(NY), precision=high)
    return cube.reshape(depth, NY * NX)


def scale_columns(columns, start):
    high = lax.Precision.HIGHEST
    width = columns.shape[1]
    position = start + jnp.arange(width)
    denom = (
        eigen_of(jnp.arange(NZ), NZ)[:, None]
        + eigen_of(position // NX, NY)[None, :]
        + eigen_of(position % NX, NX)[None, :]
    )
    basis = sine_basis(NZ)
    spectral = jnp.dot(basis, columns, precision=high) * (jnp.sqrt(4.0 * jnp.pi) / jnp.sqrt(denom))
    return jnp.dot(basis, spectral, precision=high)


def coulomb_slab(slab):
    columns = lax.all_to_all(planes(slab), "orb", split_axis=1, concat_axis=0, tiled=True)
    scaled = scale_columns(columns, lax.axis_index("orb") * columns.shape[1])
    back = lax.all_to_all(scaled, "orb", split_axis=0, concat_axis=1, tiled=True)
    return planes(back)


def factorize(partial_gram):
    lower = jnp.linalg.cholesky(partial_gram / (NZ * NY * NX))
    inverse = lax.linalg.triangular_solve(
        lower, jnp.eye(lower.shape[0], dtype=jnp.float32), left_side=True, lower=True
    )
    return (lower, inverse)


def general_body(orbitals, energies, trial_potential, local_potential):
    high = lax.Precision.HIGHEST
    depth = local_potential.shape[0]
    plane_cells = local_potential.shape[1]
    vector_slab = trial_potential.reshape(depth, plane_cells)
    perturb_full, potential_full = (
        lax.all_gather(vector_slab, "orb", axis=0, tiled=True),
        lax.all_gather(local_potential, "orb", axis=0, tiled=True),
    )
    perturb = perturb_full.astype(jnp.float32)
    potential = potential_full.astype(jnp.float32)
    weight = 4.0 / (orbitals.shape[0] * lax.axis_size("orb"))
    psi = orbitals[0].astype(jnp.float32)
    partial_value = psi * solve(psi, perturb, potential, energies[0])
    partial_value = partial_value * weight
    slab = lax.psum_scatter(partial_value, "orb", scatter_dimension=0, tiled=True)
    slab = coulomb_slab(slab)
    mine = slab.reshape(1, depth, plane_cells)
    gathered = lax.all_gather(mine, "vec", axis=0, tiled=True)
    flat = gathered.reshape(gathered.shape[0], depth * plane_cells)
    partial_gram = jnp.dot(flat, flat.T, precision=high)
    lower, inverse = factorize(lax.psum(partial_gram, "orb"))
    row = lax.dynamic_slice_in_dim(inverse, lax.axis_index("vec"), 1, 0)
    ortho = jnp.dot(row, flat, precision=high).reshape(1, depth, plane_cells)
    return (ortho, lower.T)


TILES = 3
GROUP = 4
SUB = 8
ROWS = GROUP * SUB
WTILES = TILES * SUB
HALO = STEPS - 1


def fits(orb, vec, norb, nv):
    return (
        norb == orb
        and nv == vec
        and orb % 2 == 0
        and NZ % orb == 0
        and NZ // orb >= 4
        and NZ // orb % 2 == 0
        and NY == vec * (ROWS - 2 * GROUP)
        and NY == TILES * ROWS
        and vec * ROWS == LANES
        and NX * GROUP == TILES * LANES
        and NX % (orb * vec) == 0
        and NZ % (orb * vec) == 0
        and STEPS <= GROUP
    )


def split(x):
    high = x.astype(BF16)
    return high, (x - high.astype(F32)).astype(BF16)


def np_split(x):
    x = np.asarray(x, np.float64)
    high = x.astype(ml_dtypes.bfloat16)
    return np.stack([high, (x - high.astype(np.float64)).astype(ml_dtypes.bfloat16)])


def dot3(a, b, dims):
    one = functools.partial(
        lax.dot_general, dimension_numbers=(dims, ((), ())), preferred_element_type=F32
    )
    return one(a[0], b[0]) + (one(a[0], b[1]) + one(a[1], b[0]))


def np_basis(count):
    index = np.arange(count, dtype=np.float64) + 1.0
    return np.sqrt(2.0 / (count + 1)) * np.sin(np.pi * np.outer(index, index) / (count + 1))


def np_eigen(count):
    return 4.0 * np.sin(np.pi * (np.arange(count, dtype=np.float64) + 1.0) / (2 * (count + 1))) ** 2


def to_rows(tiles):
    lane = lax.broadcasted_iota(jnp.int32, tiles[0].shape, 1)
    a, b, c = tiles
    return [
        a,
        pltpu.roll(jnp.where(lane >= 96, a, b), 32, 1),
        pltpu.roll(jnp.where(lane >= 64, b, c), 64, 1),
        pltpu.roll(c, 96, 1),
    ]


def to_tiles(rows):
    lane = lax.broadcasted_iota(jnp.int32, rows[0].shape, 1)
    r1, r2 = pltpu.roll(rows[1], 96, 1), pltpu.roll(rows[2], 64, 1)
    return [
        jnp.where(lane < 96, rows[0], r1),
        jnp.where(lane < 64, r1, r2),
        jnp.where(lane < 32, r2, pltpu.roll(rows[3], 32, 1)),
    ]


def first_tile(strip):
    return strip * (WTILES - 2 * TILES) - TILES


def tile_lanes(strip, t):
    tile = jnp.clip(first_tile(strip) + t, 0, NY * NX // LANES - 1)
    return pl.ds(pl.multiple_of(tile * LANES, LANES), LANES)


def pack_planes(src, plane, out, pairs):
    def one(pair, carry):
        for i in range(TILES):
            top = pl.multiple_of((plane + 2 * pair) * WTILES + i * SUB, SUB)
            low = pl.multiple_of((plane + 2 * pair + 1) * WTILES + i * SUB, SUB)
            block = jnp.concatenate([src[pl.ds(top, SUB), :], src[pl.ds(low, SUB), :]], 0)
            out[pair, i] = block.astype(BF16)
        return carry

    lax.fori_loop(0, pairs, one, 0)


def orbital_windows_kernel(orb, energy_ref, psi_ref, *refs):
    outs, planes_ref = refs[:-1], refs[-1]
    chips = orb // 2
    slab = NZ // chips
    chip = lax.axis_index("orb") // 2
    strip = lax.axis_index("vec")
    zero = jnp.zeros((HALO * WTILES, LANES), F32)
    planes_ref[: HALO * WTILES, :] = zero
    planes_ref[(NZ + HALO) * WTILES :, :] = zero
    for t in range(WTILES):
        row = HALO * WTILES + (t % TILES) * SUB + t // TILES
        planes_ref[pl.ds(row, NZ, WTILES), :] = psi_ref[0, :, tile_lanes(strip, t)].astype(F32)
    energy = jnp.full((1, LANES), energy_ref[0], F32)
    high = energy.astype(BF16).astype(F32)
    middle = (energy - high).astype(BF16).astype(F32)
    low = energy - high - middle
    lane = lax.broadcasted_iota(jnp.int32, (1, LANES), 1)
    for at in range(chips):
        row = at * slab * WTILES
        held = planes_ref[row : row + 1, :]
        held = jnp.where(lane == 0, high, jnp.where(lane == 1, middle, jnp.where(lane == 2, low, held)))
        planes_ref[row : row + 1, :] = held
    for shift in range(chips):
        pack_planes(planes_ref, ((chip + shift) % chips) * slab, outs[shift], (slab + 2 * HALO) // 2)


def orbital_windows(orbitals, energies, orb):
    chips = orb // 2
    pairs = (NZ // chips + 2 * HALO) // 2
    return pl.pallas_call(
        functools.partial(orbital_windows_kernel, orb),
        out_shape=[jax.ShapeDtypeStruct((pairs, TILES, 2 * SUB, LANES), BF16)] * chips,
        in_specs=[
            pl.BlockSpec(memory_space=pltpu.SMEM),
            pl.BlockSpec(memory_space=pltpu.VMEM),
        ],
        out_specs=[pl.BlockSpec(memory_space=pltpu.VMEM)] * chips,
        scratch_shapes=[pltpu.VMEM(((NZ + 2 * HALO) * WTILES, LANES), F32)],
        compiler_params=pltpu.CompilerParams(vmem_limit_bytes=24 << 20),
        name="orbital_windows",
    )(energies, orbitals)


def potential_windows_kernel(vec, v_ref, pot_ref, halo_ref, *refs):
    outs, planes_ref = refs[:-1], refs[-1]
    core = lax.axis_index("orb") % 2
    strip = lax.axis_index("vec")
    depth = v_ref.shape[1]
    half = depth + GROUP
    own = (1 - core) * GROUP
    other = core * depth
    for n in range(vec + 1):
        src, part, to = (v_ref.at[0], 0, lax.rem(strip + n, vec)) if n < vec else (pot_ref, GROUP, strip)
        for t in range(WTILES):
            row = (n * half) * WTILES + (t % TILES) * SUB + t // TILES
            lanes = tile_lanes(to, t)
            planes_ref[pl.ds(row + own * WTILES, depth, WTILES), :] = src[:, lanes].astype(F32)
            edge = halo_ref[:, lanes].astype(F32)[part : part + GROUP]
            planes_ref[pl.ds(row + other * WTILES, GROUP, WTILES), :] = edge
        pack_planes(planes_ref, n * half, outs[n], half // 2)


def potential_windows(trial, potential, halo, vec):
    half = potential.shape[0] + GROUP
    return pl.pallas_call(
        functools.partial(potential_windows_kernel, vec),
        out_shape=[jax.ShapeDtypeStruct((half // 2, TILES, 2 * SUB, LANES), BF16)] * (vec + 1),
        in_specs=[pl.BlockSpec(memory_space=pltpu.VMEM)] * 3,
        out_specs=[pl.BlockSpec(memory_space=pltpu.VMEM)] * (vec + 1),
        scratch_shapes=[pltpu.VMEM(((vec + 1) * half * WTILES, LANES), F32)],
        compiler_params=pltpu.CompilerParams(vmem_limit_bytes=24 << 20),
        name="potential_windows",
    )(trial, potential, halo)


def potential_rows_kernel(vec, mine_ref, other_ref, v_ref, d_ref):
    core = lax.axis_index("orb") % 2
    strip = lax.axis_index("vec")
    pairs = mine_ref.shape[1]
    for src, first in ((mine_ref, core * pairs), (other_ref, (1 - core) * pairs)):

        def one(pair, carry, src=src, first=first):
            plane = 2 * (first + pair)
            for n in range(vec + 1):
                rows = to_rows([src[n, pair, i].astype(F32) for i in range(TILES)])
                for zz in range(2):
                    block = jnp.concatenate([rows[i][zz * SUB : (zz + 1) * SUB] for i in range(GROUP)], 0)
                    if n < vec:
                        k = lax.rem(strip - n + vec, vec)
                        v_ref[plane + zz, pl.ds(pl.multiple_of(k * ROWS, ROWS), ROWS), :] = block
                    else:
                        d_ref[plane + zz] = 3.25 + block
            return carry

        lax.fori_loop(0, pairs, one, 0)


def potential_rows(mine, other, vec):
    planes = 4 * mine.shape[1]
    return pl.pallas_call(
        functools.partial(potential_rows_kernel, vec),
        out_shape=[
            jax.ShapeDtypeStruct((planes, vec * ROWS, LANES), F32),
            jax.ShapeDtypeStruct((planes, ROWS, LANES), F32),
        ],
        in_specs=[pl.BlockSpec(memory_space=pltpu.VMEM)] * 2,
        out_specs=[pl.BlockSpec(memory_space=pltpu.VMEM)] * 2,
        compiler_params=pltpu.CompilerParams(vmem_limit_bytes=24 << 20),
        name="potential_rows",
    )(mine, other)


def solve_kernel(vec, first, last, *refs):
    psi_ref, v_ref, d_ref = refs[:3]
    refs = refs[3:]
    sum_ref = None if first else refs[0]
    outs = refs[0 if first else 1 : -5]
    psi_s, h_s, c_s, u_a, u_b = refs[-5:]
    planes = d_ref.shape[0]
    depth = (planes - 2 * GROUP) // 2
    core = lax.axis_index("orb") % 2
    top = (lax.axis_index("orb") // 2) * 2 * depth - GROUP
    top_row = lax.axis_index("vec") * (ROWS - 2 * GROUP) - GROUP
    lane = lax.broadcasted_iota(jnp.int32, (SUB, LANES), 1)
    group = lax.broadcasted_iota(jnp.int32, (SUB, LANES), 0)
    inside = []
    for i in range(GROUP):
        y = top_row + group * GROUP + i
        inside.append(jnp.where((y >= 0) & (y < NY) & (lane < NX), 0.5, 0.0))
    inside = jnp.concatenate(inside, 0)
    block = psi_ref[0, 0].astype(F32)
    energy = block[0:1, 0:1] + block[0:1, 1:2] + block[0:1, 2:3]
    at = lax.broadcasted_iota(jnp.int32, (2 * LANES, LANES), 0) % LANES
    to = lax.broadcasted_iota(jnp.int32, (2 * LANES, LANES), 1)
    beside = jnp.where((at == to - 1) | (at == to + 1), 1.0, 0.0).astype(BF16)

    def begin(pair, carry):
        rows = to_rows([psi_ref[pair, i].astype(F32) for i in range(TILES)])
        for zz in range(2):
            w = GROUP - HALO + 2 * pair + zz
            z = top + w
            there = jnp.where((z >= 0) & (z < NZ), 1.0, 0.0)
            psi = jnp.concatenate([rows[i][zz * SUB : (zz + 1) * SUB] for i in range(GROUP)], 0)
            h = inside * there / (d_ref[w] - energy)
            psi_s[w] = psi
            h_s[w] = h
            scaled = -2.0 * psi * h
            for k in range(vec):
                rows_k = pl.ds(k * ROWS, ROWS)
                c = scaled * v_ref[w, rows_k, :]
                c_s[w, rows_k, :] = c
                u_a[w, rows_k, :] = WEIGHTS[0] * c
        return carry

    lax.fori_loop(0, psi_ref.shape[0], begin, 0, unroll=5)

    def stepped(src, w, weight):
        u = src[w]
        high, low = split(u)
        x = jnp.dot(jnp.concatenate([high, low], 1), beside, preferred_element_type=F32)
        near = x + (src[w - 1] + src[w + 1])
        h = h_s[w]
        new = []
        for k in range(vec):
            rows = [u[k * ROWS + i * SUB : k * ROWS + (i + 1) * SUB] for i in range(GROUP)]
            north = jnp.concatenate([pltpu.roll(rows[-1], 1, 0)] + rows[:-1], 0)
            south = jnp.concatenate(rows[1:] + [pltpu.roll(rows[0], SUB - 1, 0)], 0)
            at_k = slice(k * ROWS, (k + 1) * ROWS)
            total = near[at_k] + (north + south)
            change = c_s[w, at_k, :] + h * total
            new.append((1.0 - weight) * u[at_k] + weight * change)
        return new

    src, dst = u_a, u_b
    for step in range(1, STEPS - 1):
        low = GROUP - HALO + step

        def middle(w, carry, src=src, dst=dst, step=step):
            dst[w] = jnp.concatenate(stepped(src, w, WEIGHTS[step]), 0)
            return carry

        lax.fori_loop(low, planes - low, middle, 0, unroll=True)
        src, dst = dst, src

    def end(p, carry, out, start, src=src):
        w = GROUP + start + p
        psi = psi_s[w]
        total = jnp.concatenate([psi * new for new in stepped(src, w, WEIGHTS[STEPS - 1])], 0)
        if not first:
            total = total + sum_ref[start + p]
        out[p] = total
        return carry

    if last:
        lax.fori_loop(0, depth, functools.partial(end, out=outs[1], start=(1 - core) * depth), 0, unroll=True)
        lax.fori_loop(0, depth, functools.partial(end, out=outs[0], start=core * depth), 0, unroll=True)
    else:
        lax.fori_loop(0, 2 * depth, functools.partial(end, out=outs[0], start=0), 0, unroll=True)


def solve_window(psi, v, d, total, vec, last):
    planes = d.shape[0]
    depth = (planes - 2 * GROUP) // 2
    first = total is None
    if last:
        outs = [jax.ShapeDtypeStruct((depth, LANES, LANES), F32)] * 2
    else:
        outs = [jax.ShapeDtypeStruct((2 * depth, LANES, LANES), F32)]
    args = (psi, v, d) if first else (psi, v, d, total)
    got = pl.pallas_call(
        functools.partial(solve_kernel, vec, first, last),
        out_shape=outs,
        in_specs=[pl.BlockSpec(memory_space=pltpu.VMEM)] * len(args),
        out_specs=[pl.BlockSpec(memory_space=pltpu.VMEM)] * len(outs),
        scratch_shapes=[pltpu.VMEM((planes, ROWS, LANES), F32)] * 2
        + [pltpu.VMEM((planes, vec * ROWS, LANES), F32)] * 3,
        compiler_params=pltpu.CompilerParams(vmem_limit_bytes=32 << 20),
        name="solve_window",
    )(*args)
    return got if last else got[0]


def forward_x_kernel(ndev, basis_ref, own_ref, other_ref, out_ref):
    depth = own_ref.shape[0]
    parts = NX // ndev
    rows = out_ref.shape[0] // ndev
    basis = (basis_ref[0], basis_ref[1])
    for z in range(depth):
        chi = split(own_ref[z] + other_ref[z])
        got = dot3(basis, chi, ((1,), (1,)))
        for part in range(parts):
            out_ref[pl.ds(part * depth + z, ndev, rows), :] = got[part * ndev : (part + 1) * ndev]
    for row in range(parts * depth, rows):
        out_ref[pl.ds(row, ndev, rows), :] = jnp.zeros((ndev, LANES), F32)


def forward_x(own, other, basis, ndev):
    rows = -(-(NX // ndev) * own.shape[0] // SUB) * SUB
    out = pl.pallas_call(
        functools.partial(forward_x_kernel, ndev),
        out_shape=jax.ShapeDtypeStruct((ndev * rows, LANES), F32),
        in_specs=[pl.BlockSpec(memory_space=pltpu.VMEM)] * 3,
        out_specs=pl.BlockSpec(memory_space=pltpu.VMEM),
        compiler_params=pltpu.CompilerParams(vmem_limit_bytes=24 << 20),
        name="forward_x",
    )(basis, own, other)
    return out.reshape(ndev, rows, LANES)


def spectral_kernel(orb, vec, mux_ref, muzy_ref, wy_ref, kz_ref, kzb_ref, wyb_ref, got_ref, out_ref):
    ndev = orb * vec
    parts = NX // ndev
    me = lax.axis_index("orb") * vec + lax.axis_index("vec")
    rows = got_ref.shape[1]
    x = jnp.concatenate(
        [
            jnp.concatenate([got_ref[o * vec + v] for o in range(orb)], 0)
            for v in range(vec)
        ],
        1,
    )
    mm = ((1,), (0,))
    t = dot3(split(x), (wy_ref[0], wy_ref[1]), mm)
    t = dot3((kz_ref[0], kz_ref[1]), split(t), mm)
    scale = jnp.concatenate(
        [
            math.sqrt(4.0 * math.pi) / jnp.sqrt(muzy_ref[...] + mux_ref[part * ndev + me])
            for part in range(parts)
        ],
        0,
    )
    fields = [t[:, k * LANES : (k + 1) * LANES] * scale for k in range(vec)]
    lane = lax.broadcasted_iota(jnp.int32, (1, LANES), 1)
    gram = jnp.zeros((1, LANES), F32)
    for k in range(vec):
        for l in range(k + 1):
            entry = jnp.sum(jnp.sum(fields[k] * fields[l], axis=0, keepdims=True), axis=1, keepdims=True)
            gram = jnp.where(lane == k * vec + l, entry, gram)
    t = jnp.concatenate(fields, 1)
    t = dot3((kzb_ref[0], kzb_ref[1]), split(t), mm)
    t = dot3(split(t), (wyb_ref[0], wyb_ref[1]), mm)
    rows = out_ref.shape[0] // ndev
    groups = t.shape[0] // ndev
    for r in range(groups):
        for yt in range(TILES):
            out_ref[pl.ds(r * TILES + yt, ndev, rows), :] = t[
                r * ndev : (r + 1) * ndev, yt * LANES : (yt + 1) * LANES
            ]
    out_ref[pl.ds(groups * TILES, ndev, rows), :] = jnp.broadcast_to(gram, (ndev, LANES))


def spectral(got, orb, vec):
    ndev = orb * vec
    parts, zs = NX // ndev, NZ // ndev
    depth = NZ // orb
    strip = ROWS - 2 * GROUP
    rows_in = got.shape[1]
    rows_out = -(-(parts * zs * TILES + 1) // SUB) * SUB
    sy, sz = np_basis(NY), np_basis(NZ)
    wy = np.zeros((vec, vec, GROUP, SUB, vec, LANES))
    wyb = np.zeros((vec, LANES, TILES, vec, GROUP, SUB))
    for k in range(vec):
        for i in range(GROUP):
            for g in range(SUB):
                for v in range(vec):
                    row = v * strip - GROUP + GROUP * g + i
                    if v * strip <= row < (v + 1) * strip:
                        wy[v, k, i, g, k, :NY] = sy[row]
                for yt in range(TILES):
                    wyb[k, :NY, yt, k, i, g] = sy[yt * ROWS + GROUP * g + i]
    wy = wy.reshape(vec * LANES, vec * LANES)
    wyb = wyb.reshape(vec * LANES, TILES * LANES)
    kz = np.zeros((parts, NZ, orb, rows_in))
    kzb = np.zeros((zs, parts, ndev, parts, NZ))
    for part in range(parts):
        for o in range(orb):
            kz[part, :, o, part * depth : (part + 1) * depth] = sz[:, o * depth : (o + 1) * depth]
        for z in range(zs):
            kzb[z, part, :, part, :] = sz[z::zs]
    kz = kz.reshape(parts * NZ, orb * rows_in)
    kzb = kzb.reshape(zs * parts * ndev, parts * NZ)
    muzy = np.ones((NZ, LANES), np.float32)
    muzy[:, :NY] = np_eigen(NZ)[:, None] + np_eigen(NY)[None, :]
    mux = np_eigen(NX).astype(np.float32)
    out = pl.pallas_call(
        functools.partial(spectral_kernel, orb, vec),
        out_shape=jax.ShapeDtypeStruct((ndev * rows_out, LANES), F32),
        in_specs=[pl.BlockSpec(memory_space=pltpu.SMEM)] + [pl.BlockSpec(memory_space=pltpu.VMEM)] * 6,
        out_specs=pl.BlockSpec(memory_space=pltpu.VMEM),
        compiler_params=pltpu.CompilerParams(vmem_limit_bytes=32 << 20),
        name="spectral",
    )(mux, muzy, np_split(wy), np_split(kz), np_split(kzb), np_split(wyb), got)
    return out.reshape(ndev, rows_out, LANES)


def back_kernel(ndev, vec, basis_ref, got_ref, factor_ref, *outs):
    parts, zs = NX // ndev, NZ // ndev
    rows = got_ref.shape[0] // ndev
    strip = lax.axis_index("vec")
    basis = (basis_ref[0], basis_ref[1])
    gram = jnp.sum(got_ref[pl.ds(zs * parts * TILES, ndev, rows), :], axis=0, keepdims=True)
    gram = gram / (NZ * NY * NX)
    entry = lambda k, l: gram[:, k * vec + l : k * vec + l + 1]
    lower = [[None] * vec for _ in range(vec)]
    inverse = [[jnp.zeros((1, 1), F32)] * vec for _ in range(vec)]
    for l in range(vec):
        pivot = entry(l, l)
        for m in range(l):
            pivot = pivot - lower[l][m] * lower[l][m]
        lower[l][l] = jnp.sqrt(pivot)
        inverse[l][l] = 1.0 / lower[l][l]
        for k in range(l + 1, vec):
            value = entry(k, l)
            for m in range(l):
                value = value - lower[k][m] * lower[l][m]
            lower[k][l] = value * inverse[l][l]
    for l in range(vec):
        for k in range(l + 1, vec):
            value = lower[k][l] * inverse[l][l]
            for m in range(l + 1, k):
                value = value + lower[k][m] * inverse[m][l]
            inverse[k][l] = -value * inverse[k][k]
    at_row = lax.broadcasted_iota(jnp.int32, (vec, vec), 0)
    at_col = lax.broadcasted_iota(jnp.int32, (vec, vec), 1)
    factor = jnp.zeros((vec, vec), F32)
    for k in range(vec):
        for l in range(k + 1):
            factor = jnp.where((at_row == l) & (at_col == k), lower[k][l], factor)
    factor_ref[...] = factor
    coefficients = []
    for s in range(vec):
        to = lax.rem(strip + s, vec)
        line = []
        for k in range(vec):
            value = inverse[0][k]
            for m in range(1, vec):
                value = jnp.where(to == m, inverse[m][k], value)
            line.append(value)
        coefficients.append(line)
    for z in range(zs):
        for yt in range(TILES):
            x = jnp.concatenate(
                [
                    got_ref[pl.ds((z * parts + part) * TILES + yt, ndev, rows), :]
                    for part in range(parts)
                ],
                0,
            )
            y = dot3(split(x), basis, ((0,), (0,)))
            for s in range(vec):
                mixed = coefficients[s][0] * y[:ROWS]
                for k in range(1, vec):
                    mixed = mixed + coefficients[s][k] * y[k * ROWS : (k + 1) * ROWS]
                tiles = to_tiles([mixed[i * SUB : (i + 1) * SUB] for i in range(GROUP)])
                for i in range(TILES):
                    outs[s][z, (yt * TILES + i) * SUB : (yt * TILES + i + 1) * SUB, :] = tiles[i]


def back(got, basis, ndev, vec):
    zs = NZ // ndev
    tiles = NY * NX // LANES
    return pl.pallas_call(
        functools.partial(back_kernel, ndev, vec),
        out_shape=[jax.ShapeDtypeStruct((vec, vec), F32)]
        + [jax.ShapeDtypeStruct((zs, tiles, LANES), F32)] * vec,
        in_specs=[pl.BlockSpec(memory_space=pltpu.VMEM)] * 2,
        out_specs=[pl.BlockSpec(memory_space=pltpu.VMEM)] * (vec + 1),
        compiler_params=pltpu.CompilerParams(vmem_limit_bytes=24 << 20),
        name="back",
    )(basis, got.reshape(-1, LANES))


def assemble_kernel(vec, *refs):
    gots, out_ref, all_ref = refs[:vec], refs[vec], refs[vec + 1]
    strip = lax.axis_index("vec")
    zs, tiles = gots[0].shape[:2]
    depth = zs * vec
    for s in range(vec):
        first = lax.rem(strip - s + vec, vec) * zs
        for z in range(zs):
            start = pl.multiple_of((first + z) * tiles, SUB)
            all_ref[pl.ds(start, tiles), :] = gots[s][z]
    for yt in range(TILES):
        for i in range(TILES):
            for g in range(SUB):
                row = (yt * TILES + i) * SUB + g
                tile = yt * WTILES + g * TILES + i
                out_ref[0, :, tile * LANES : (tile + 1) * LANES] = all_ref[pl.ds(row, depth, tiles), :]


def assemble(gots, vec):
    zs, tiles = gots[0].shape[:2]
    return pl.pallas_call(
        functools.partial(assemble_kernel, vec),
        out_shape=jax.ShapeDtypeStruct((1, zs * vec, tiles * LANES), F32),
        in_specs=[pl.BlockSpec(memory_space=pltpu.VMEM)] * vec,
        out_specs=pl.BlockSpec(memory_space=pltpu.VMEM),
        scratch_shapes=[pltpu.VMEM((zs * vec * tiles, LANES), F32)],
        compiler_params=pltpu.CompilerParams(vmem_limit_bytes=24 << 20),
        name="assemble",
    )(*gots)


def swap_cores(x, orb):
    return lax.ppermute(x, "orb", [(o, o ^ 1) for o in range(orb)])


def shift(x, axis, count):
    n = lax.axis_size(axis)
    return lax.ppermute(x, axis, [(i, (i + count) % n) for i in range(n)])


def responses(orbitals, energies, trial_potential, local_potential):
    orb, vec = lax.axis_size("orb"), lax.axis_size("vec")
    core = lax.axis_index("orb") % 2
    depth = local_potential.shape[0]
    chips = orb // 2
    edges = [
        jnp.concatenate([trial_potential[0, at : at + GROUP], local_potential[at : at + GROUP]], 0)
        for at in (0, depth - GROUP)
    ]
    edge = jnp.where(core == 0, edges[0], edges[1])
    pairs = [(o, o + 1) for o in range(1, orb - 1, 2)] + [(o + 1, o) for o in range(1, orb - 1, 2)]
    halo = lax.ppermute(edge, "orb", pairs)
    windows = orbital_windows(orbitals, energies, orb)
    psis = [windows[0]]
    for r in range(1, chips):
        perm = [(2 * a + c, 2 * ((a + r) % chips) + c) for a in range(chips) for c in range(2)]
        psis.append(lax.ppermute(windows[r], "orb", perm))
    parts = potential_windows(trial_potential, local_potential, halo, vec)
    mine = jnp.stack([parts[0]] + [shift(parts[n], "vec", n) for n in range(1, vec)] + [parts[vec]])
    v, d = potential_rows(mine, swap_cores(mine, orb), vec)
    total = None
    for r in range(chips):
        total = solve_window(psis[r], v, d, total, vec, r == chips - 1)
    return total[0], swap_cores(total[1], orb)


def block_body(orbitals, energies, trial_potential, local_potential):
    orb, vec = lax.axis_size("orb"), lax.axis_size("vec")
    ndev = orb * vec
    both = ("orb", "vec")
    own, other = responses(orbitals, energies, trial_potential, local_potential)
    sx = np_basis(NX)
    padded = np.zeros((NX, LANES))
    padded[:, :NX] = sx
    sent = forward_x(own, other, np_split(padded * (4.0 / orb)), ndev)
    got = lax.all_to_all(sent, both, 0, 0, tiled=True)
    sent = spectral(got, orb, vec)
    got = lax.all_to_all(sent, both, 0, 0, tiled=True)
    factor, *slots = back(got, np_split(padded), ndev, vec)
    gots = [slots[0]] + [shift(slots[s], "vec", s) for s in range(1, vec)]
    return assemble(gots, vec), factor


def solution(mesh):
    orb, vec = mesh.shape["orb"], mesh.shape["vec"]
    placed = (P("orb", None, None), P("orb"), P("vec", "orb", None), P("orb", None))

    def body(orbitals, energies, trial_potential, local_potential):
        one = orbitals.shape[0] == 1 and trial_potential.shape[0] == 1
        plan = block_body if one and fits(orb, vec, orb, vec) else general_body
        return plan(orbitals, energies, trial_potential, local_potential)

    return jax.shard_map(
        body, mesh=mesh, in_specs=placed, out_specs=(P("vec", "orb", None), P()), check_vma=False
    )
```

```python
import functools
import math

import jax
import jax.numpy as jnp
import ml_dtypes
import numpy as np
from jax import lax
from jax.experimental import pallas as pl
from jax.experimental.pallas import tpu as pltpu
from jax.sharding import PartitionSpec as P

NZ = 96
NY = 96
NX = 96
STEPS = 4

BF16 = jnp.bfloat16
F32 = jnp.float32
LANES = 128
WEIGHTS = [1.0 / (1.0 + 0.8 * math.cos(math.pi * (2 * s + 1) / (2 * STEPS))) for s in range(STEPS)]


def neighbours(field):
    depth, flat = field.shape
    zero_plane = jnp.zeros((1, flat), field.dtype)
    total = jnp.concatenate([zero_plane, field[:-1]], 0) + jnp.concatenate(
        [field[1:], zero_plane], 0
    )
    zero_rows = jnp.zeros((depth, NX), field.dtype)
    total = (
        total
        + jnp.concatenate([zero_rows, field[:, :-NX]], 1)
        + jnp.concatenate([field[:, NX:], zero_rows], 1)
    )
    column = jnp.arange(flat) % NX
    zero_col = jnp.zeros((depth, 1), field.dtype)
    left = jnp.concatenate([zero_col, field[:, :-1]], 1) * (column > 0).astype(field.dtype)
    right = jnp.concatenate([field[:, 1:], zero_col], 1) * (column < NX - 1).astype(field.dtype)
    return total + left + right


def solve(psi, perturb, potential, energy):
    diag = 3.25 + potential - energy
    source = -perturb * psi
    answer = jnp.zeros_like(psi)
    for step in range(STEPS):
        weight = 1.0 / (1.0 + 0.8 * jnp.cos(jnp.pi * (2 * step + 1) / (2 * STEPS)))
        applied = diag * answer - 0.5 * neighbours(answer)
        answer = answer + weight * (source - applied) / diag
    return answer


def sine_basis(count):
    index = jnp.arange(count, dtype=jnp.float32) + 1.0
    return jnp.sqrt(2.0 / (count + 1)) * jnp.sin(
        jnp.pi * index[:, None] * index[None, :] / (count + 1)
    )


def eigen_of(position, count):
    return 2.0 - 2.0 * jnp.cos(jnp.pi * (position.astype(jnp.float32) + 1.0) / (count + 1))


def planes(field):
    high = lax.Precision.HIGHEST
    depth = field.shape[0]
    cube = field.reshape(depth, NY, NX)
    cube = jnp.einsum("zyx,cx->zyc", cube, sine_basis(NX), precision=high)
    cube = jnp.einsum("zyc,by->zbc", cube, sine_basis(NY), precision=high)
    return cube.reshape(depth, NY * NX)


def scale_columns(columns, start):
    high = lax.Precision.HIGHEST
    width = columns.shape[1]
    position = start + jnp.arange(width)
    denom = (
        eigen_of(jnp.arange(NZ), NZ)[:, None]
        + eigen_of(position // NX, NY)[None, :]
        + eigen_of(position % NX, NX)[None, :]
    )
    basis = sine_basis(NZ)
    spectral = jnp.dot(basis, columns, precision=high) * (jnp.sqrt(4.0 * jnp.pi) / jnp.sqrt(denom))
    return jnp.dot(basis, spectral, precision=high)


def coulomb_slab(slab):
    columns = lax.all_to_all(planes(slab), "orb", split_axis=1, concat_axis=0, tiled=True)
    scaled = scale_columns(columns, lax.axis_index("orb") * columns.shape[1])
    back = lax.all_to_all(scaled, "orb", split_axis=0, concat_axis=1, tiled=True)
    return planes(back)


def factorize(partial_gram):
    lower = jnp.linalg.cholesky(partial_gram / (NZ * NY * NX))
    inverse = lax.linalg.triangular_solve(
        lower, jnp.eye(lower.shape[0], dtype=jnp.float32), left_side=True, lower=True
    )
    return (lower, inverse)


def general_body(orbitals, energies, trial_potential, local_potential):
    high = lax.Precision.HIGHEST
    depth = local_potential.shape[0]
    plane_cells = local_potential.shape[1]
    vector_slab = trial_potential.reshape(depth, plane_cells)
    perturb_full, potential_full = (
        lax.all_gather(vector_slab, "orb", axis=0, tiled=True),
        lax.all_gather(local_potential, "orb", axis=0, tiled=True),
    )
    perturb = perturb_full.astype(jnp.float32)
    potential = potential_full.astype(jnp.float32)
    weight = 4.0 / (orbitals.shape[0] * lax.axis_size("orb"))
    psi = orbitals[0].astype(jnp.float32)
    partial_value = psi * solve(psi, perturb, potential, energies[0])
    partial_value = partial_value * weight
    slab = lax.psum_scatter(partial_value, "orb", scatter_dimension=0, tiled=True)
    slab = coulomb_slab(slab)
    mine = slab.reshape(1, depth, plane_cells)
    gathered = lax.all_gather(mine, "vec", axis=0, tiled=True)
    flat = gathered.reshape(gathered.shape[0], depth * plane_cells)
    partial_gram = jnp.dot(flat, flat.T, precision=high)
    lower, inverse = factorize(lax.psum(partial_gram, "orb"))
    row = lax.dynamic_slice_in_dim(inverse, lax.axis_index("vec"), 1, 0)
    ortho = jnp.dot(row, flat, precision=high).reshape(1, depth, plane_cells)
    return (ortho, lower.T)


TILES = 3
GROUP = 4
SUB = NY // GROUP
PLANE = TILES * SUB
EDGE = 4
TAIL = 32


def fits(orb, vec):
    ndev = orb * vec
    return (
        orb % 2 == 0
        and NZ % ndev == 0
        and NX % ndev == 0
        and NY % GROUP == 0
        and NX * GROUP == TILES * LANES
        and NZ // orb % GROUP == 0
        and (2 * (NZ // orb) + 2 * EDGE) % (2 * vec) == 0
        and NX // ndev == TILES
        and NX // ndev * NY == 2 * LANES + TAIL
        and vec * TAIL == LANES
        and GROUP * TAIL == LANES
        and STEPS <= EDGE
    )


def split(x):
    high = x.astype(BF16)
    return high, (x - high.astype(F32)).astype(BF16)


def np_split(x):
    x = np.asarray(x, np.float64)
    high = x.astype(ml_dtypes.bfloat16)
    return np.stack([high, (x - high.astype(np.float64)).astype(ml_dtypes.bfloat16)])


def dot3(a, b, dims=((1,), (0,))):
    one = functools.partial(
        lax.dot_general, dimension_numbers=(dims, ((), ())), preferred_element_type=F32
    )
    return one(a[0], b[0]) + (one(a[0], b[1]) + one(a[1], b[0]))


def np_basis(count):
    index = np.arange(count, dtype=np.float64) + 1.0
    return np.sqrt(2.0 / (count + 1)) * np.sin(np.pi * np.outer(index, index) / (count + 1))


def np_eigen(count):
    return 4.0 * np.sin(np.pi * (np.arange(count, dtype=np.float64) + 1.0) / (2 * (count + 1))) ** 2


def row_order():
    return np.array([GROUP * g + i for i in range(GROUP) for g in range(SUB)])


def to_rows(tiles):
    lane = lax.broadcasted_iota(jnp.int32, tiles[0].shape, 1)
    a, b, c = tiles
    return [
        a,
        pltpu.roll(jnp.where(lane >= 96, a, b), 32, 1),
        pltpu.roll(jnp.where(lane >= 64, b, c), 64, 1),
        pltpu.roll(c, 96, 1),
    ]


def to_tiles(rows):
    lane = lax.broadcasted_iota(jnp.int32, rows[0].shape, 1)
    r1, r2 = pltpu.roll(rows[1], 96, 1), pltpu.roll(rows[2], 64, 1)
    return [
        jnp.where(lane < 96, rows[0], r1),
        jnp.where(lane < 64, r1, r2),
        jnp.where(lane < 32, r2, pltpu.roll(rows[3], 32, 1)),
    ]


VMEM = pl.BlockSpec(memory_space=pltpu.VMEM)
SMEM = pl.BlockSpec(memory_space=pltpu.SMEM)
HBM = pl.BlockSpec(memory_space=pltpu.HBM)


def limit(mib):
    return pltpu.CompilerParams(vmem_limit_bytes=mib << 20)


def pack_planes(src, plane, out, pairs, to=()):
    for pair in range(pairs):
        for i in range(TILES):
            top = pl.multiple_of((plane + 2 * pair) * PLANE + i * SUB, 8)
            low = pl.multiple_of((plane + 2 * pair + 1) * PLANE + i * SUB, 8)
            block = jnp.concatenate([src[pl.ds(top, SUB), :], src[pl.ds(low, SUB), :]], 0)
            out[(*to, pair, i)] = block.astype(BF16)


def windows_kernel(orb, vec, energy_ref, psi_any, v_any, pot_any, *refs):
    outs, (planes_ref, more_ref, psi_ref, v_ref, pot_ref, sem) = refs[:-6], refs[-6:]
    chips = orb // 2
    depth = v_ref.shape[0]
    slab = 2 * depth
    piece = (slab + 2 * EDGE) // vec
    chip = lax.axis_index("orb") // 2
    core = lax.axis_index("orb") % 2
    line = lax.axis_index("vec")
    copies = [
        pltpu.make_async_copy(v_any.at[0], v_ref, sem.at[0]),
        pltpu.make_async_copy(pot_any, pot_ref, sem.at[1]),
        pltpu.make_async_copy(psi_any.at[0], psi_ref, sem.at[2]),
    ]
    for copy in copies:
        copy.start()
    own_ref, edge_ref, *psi_outs = outs
    for n, src in enumerate((v_ref, pot_ref)):
        copies[n].wait()
        for t in range(PLANE):
            row = n * depth * PLANE + (t % TILES) * SUB + t // TILES
            more_ref[pl.ds(row, depth, PLANE), :] = src[:, t * LANES : (t + 1) * LANES].astype(F32)
        pack_planes(more_ref, n * depth, own_ref, depth // 2, (n,))
        pack_planes(more_ref, n * depth + core * (depth - EDGE), edge_ref, EDGE // 2, (n,))
    zero = jnp.zeros((EDGE * PLANE, LANES), F32)
    planes_ref[: EDGE * PLANE, :] = zero
    planes_ref[(NZ + EDGE) * PLANE :, :] = zero
    copies[2].wait()
    for t in range(PLANE):
        row = EDGE * PLANE + (t % TILES) * SUB + t // TILES
        planes_ref[pl.ds(row, NZ, PLANE), :] = psi_ref[:, t * LANES : (t + 1) * LANES].astype(F32)
    energy = jnp.full((1, LANES), energy_ref[0], F32)
    high = energy.astype(BF16).astype(F32)
    middle = (energy - high).astype(BF16).astype(F32)
    low = energy - high - middle
    lane = lax.broadcasted_iota(jnp.int32, (1, LANES), 1)
    held = jnp.where(lane == 0, high, jnp.where(lane == 1, middle, low))
    for shift in range(1, chips):
        first = ((chip + shift) % chips) * slab
        pack_planes(planes_ref, first + line * piece, psi_outs[vec + shift - 1], piece // 2)

        @pl.when(line == 0)
        def _():
            start = pl.multiple_of(first * PLANE, 8)
            block = planes_ref[pl.ds(start, SUB), :]
            top = jnp.where(lax.broadcasted_iota(jnp.int32, block.shape, 0) == 0, held, block)
            both = jnp.concatenate([top, planes_ref[pl.ds(start + PLANE, SUB), :]], 0)
            psi_outs[vec + shift - 1][0, 0] = both.astype(BF16)

    for s in range(vec):
        number = (line - s + vec) % vec
        pack_planes(planes_ref, chip * slab + number * piece, psi_outs[s], piece // 2)

        @pl.when(number == 0)
        def _():
            start = pl.multiple_of(chip * slab * PLANE, 8)
            block = planes_ref[pl.ds(start, SUB), :]
            top = jnp.where(lax.broadcasted_iota(jnp.int32, block.shape, 0) == 0, held, block)
            both = jnp.concatenate([top, planes_ref[pl.ds(start + PLANE, SUB), :]], 0)
            psi_outs[s][0, 0] = both.astype(BF16)


def windows(orbitals, energies, trial, potential, orb, vec):
    chips = orb // 2
    depth = potential.shape[0]
    block = (TILES, 2 * SUB, LANES)
    pairs = (2 * depth + 2 * EDGE) // vec // 2
    outs = [jax.ShapeDtypeStruct((2, depth // 2, *block), BF16), jax.ShapeDtypeStruct((2, EDGE // 2, *block), BF16)]
    outs += [jax.ShapeDtypeStruct((pairs, *block), BF16)] * (vec + chips - 1)
    inputs = [pltpu.with_memory_space_constraint(x, pltpu.HBM) for x in (orbitals, trial, potential)]
    own, edge, *psis = pl.pallas_call(
        functools.partial(windows_kernel, orb, vec),
        out_shape=outs,
        in_specs=[SMEM] + [HBM] * 3,
        out_specs=[VMEM] * len(outs),
        scratch_shapes=[
            pltpu.VMEM(((NZ + 2 * EDGE) * PLANE, LANES), F32),
            pltpu.VMEM((2 * depth * PLANE, LANES), F32),
            pltpu.VMEM((NZ, PLANE * LANES), BF16),
            pltpu.VMEM((depth, PLANE * LANES), BF16),
            pltpu.VMEM((depth, PLANE * LANES), BF16),
            pltpu.SemaphoreType.DMA((3,)),
        ],
        compiler_params=limit(32),
        name="windows",
    )(energies, *inputs)
    return own, edge, psis[:vec], psis[vec:]


def rows_of(refs, pair):
    rows = to_rows([ref.astype(F32) for ref in refs])
    return [jnp.concatenate([r[zz * SUB : (zz + 1) * SUB] for r in rows], 0) for zz in range(2)]


def potential_rows_kernel(own_ref, other_ref, near_ref, far_ref, v_ref, d_ref):
    core = lax.axis_index("orb") % 2
    pairs, edge = own_ref.shape[1], near_ref.shape[1]
    spans = (
        (own_ref, edge + core * pairs),
        (other_ref, edge + (1 - core) * pairs),
        (near_ref, core * (2 * pairs + edge)),
        (far_ref, (1 - core) * (2 * pairs + edge)),
    )
    for src, first in spans:
        for pair in range(src.shape[1]):
            plane = 2 * (first + pair)
            for n, out in enumerate((v_ref, d_ref)):
                for zz, rows in enumerate(rows_of([src[n, pair, i] for i in range(TILES)], pair)):
                    out[plane + zz] = rows if n == 0 else 3.25 + rows


def potential_rows(own, other, near, far):
    planes = 4 * (own.shape[1] + near.shape[1])
    return pl.pallas_call(
        potential_rows_kernel,
        out_shape=[jax.ShapeDtypeStruct((planes, NY, LANES), F32)] * 2,
        in_specs=[VMEM] * 4,
        out_specs=[VMEM] * 2,
        compiler_params=limit(24),
        name="potential_rows",
    )(own, other, near, far)


def solve_kernel(vec, which, first, last, *refs):
    psi_refs, (v_ref, d_ref) = [ref.at[which] for ref in refs[:vec]], refs[vec : vec + 2]
    refs = refs[vec + 2 :]
    sum_ref = None if first else refs[0]
    outs = refs[0 if first else 1 : -5]
    psi_s, h_s, c_s, u_a, u_b = refs[-5:]
    planes = d_ref.shape[0]
    depth = (planes - 2 * EDGE) // 2
    pairs = psi_refs[0].shape[0]
    core = lax.axis_index("orb") % 2
    line = lax.axis_index("vec")
    top = (lax.axis_index("orb") // 2) * 2 * depth - EDGE
    half = jnp.where(lax.broadcasted_iota(jnp.int32, (NY, LANES), 1) < NX, 0.5, 0.0)
    group = lax.broadcasted_iota(jnp.int32, (SUB, LANES), 0)
    numbers = [lax.rem(line - s + vec, vec) for s in range(vec)]
    energy = jnp.zeros((1, 1), F32)
    for number, psi_ref in zip(numbers, psi_refs):
        block = psi_ref[0, 0][:8].astype(F32)
        energy = jnp.where(number == 0, block[0:1, 0:1] + block[0:1, 1:2] + block[0:1, 2:3], energy)
    at = lax.broadcasted_iota(jnp.int32, (2 * LANES, LANES), 0) % LANES
    to = lax.broadcasted_iota(jnp.int32, (2 * LANES, LANES), 1)
    beside = jnp.where((at == to - 1) | (at == to + 1), 1.0, 0.0).astype(BF16)

    for number, psi_ref in zip(numbers, psi_refs):
        for pair in range(pairs):
            for zz, psi in enumerate(rows_of([psi_ref[pair, i] for i in range(TILES)], pair)):
                w = number * 2 * pairs + 2 * pair + zz
                there = jnp.where((top + w >= 0) & (top + w < NZ), 1.0, 0.0)
                h = half * there / (d_ref[w] - energy)
                c = -2.0 * psi * h * v_ref[w]
                psi_s[w] = psi
                h_s[w] = h
                c_s[w] = c
                u_a[w] = WEIGHTS[0] * c

    def stepped(src, w, weight):
        u = src[w]
        high, low = split(u)
        x = jnp.dot(jnp.concatenate([high, low], 1), beside, preferred_element_type=F32)
        rows = [u[i * SUB : (i + 1) * SUB] for i in range(GROUP)]
        before = jnp.where(group == 0, 0.0, pltpu.roll(rows[-1], 1, 0))
        behind = jnp.where(group == SUB - 1, 0.0, pltpu.roll(rows[0], SUB - 1, 0))
        north = jnp.concatenate([before] + rows[:-1], 0)
        south = jnp.concatenate(rows[1:] + [behind], 0)
        near = (x + (src[w - 1] + src[w + 1])) + (north + south)
        return (1.0 - weight) * u + weight * (c_s[w] + h_s[w] * near)

    src, dst = u_a, u_b
    for step in range(1, STEPS - 1):
        low = EDGE - STEPS + 1 + step

        def middle(w, carry, src=src, dst=dst, step=step):
            dst[w] = stepped(src, w, WEIGHTS[step])
            return carry

        lax.fori_loop(low, planes - low, middle, 0, unroll=True)
        src, dst = dst, src

    def end(p, carry, out, start, src=src):
        w = EDGE + start + p
        total = psi_s[w] * stepped(src, w, WEIGHTS[STEPS - 1])
        if not first:
            total = total + sum_ref[start + p]
        out[p] = total
        return carry

    if last:
        lax.fori_loop(0, depth, functools.partial(end, out=outs[1], start=(1 - core) * depth), 0, unroll=True)
        lax.fori_loop(0, depth, functools.partial(end, out=outs[0], start=core * depth), 0, unroll=True)
    else:
        lax.fori_loop(0, 2 * depth, functools.partial(end, out=outs[0], start=0), 0, unroll=True)


def solve_window(psis, which, v, d, total, last):
    planes = d.shape[0]
    depth = (planes - 2 * EDGE) // 2
    first = total is None
    if last:
        outs = [jax.ShapeDtypeStruct((depth, NY, LANES), F32)] * 2
    else:
        outs = [jax.ShapeDtypeStruct((2 * depth, NY, LANES), F32)]
    args = (*psis, v, d) if first else (*psis, v, d, total)
    got = pl.pallas_call(
        functools.partial(solve_kernel, len(psis), which, first, last),
        out_shape=outs,
        in_specs=[VMEM] * len(args),
        out_specs=[VMEM] * len(outs),
        scratch_shapes=[pltpu.VMEM((planes, NY, LANES), F32)] * 5,
        compiler_params=limit(32),
        name="solve_window",
    )(*args)
    return got if last else got[0]


def forward_kernel(ndev, basis_ref, weights_ref, own_ref, other_ref, out_ref):
    depth = own_ref.shape[0]
    rows = out_ref.shape[0] // ndev
    basis = (basis_ref[0], basis_ref[1])
    pad = jnp.zeros((LANES - NY, LANES), F32)
    blocks = []
    for z in range(depth):
        chi = split(jnp.concatenate([own_ref[z] + other_ref[z], pad], 0))
        got = dot3(basis, chi, ((1,), (1,)))
        blocks.append(jnp.concatenate([got[p * ndev : (p + 1) * ndev] for p in range(TILES)], 1))
    t = dot3(split(jnp.concatenate(blocks, 0)), (weights_ref[0], weights_ref[1]))
    for z in range(depth):
        for tile in range(2):
            out_ref[pl.ds(tile * depth + z, ndev, rows), :] = t[
                z * ndev : (z + 1) * ndev, tile * LANES : (tile + 1) * LANES
            ]
    for quad in range(depth // GROUP):
        tail = t[quad * GROUP * ndev : (quad * GROUP + 1) * ndev, 2 * LANES :]
        for z in range(1, GROUP):
            at = quad * GROUP + z
            tail = tail + pltpu.roll(t[at * ndev : (at + 1) * ndev, 2 * LANES :], z * TAIL, 1)
        out_ref[pl.ds(2 * depth + quad, ndev, rows), :] = tail
    for row in range(2 * depth + depth // GROUP, rows):
        out_ref[pl.ds(row, ndev, rows), :] = jnp.zeros((ndev, LANES), F32)


def y_weights():
    sy = np_basis(NY)[row_order()]
    weights = np.zeros((TILES, LANES, TILES * LANES))
    for part in range(TILES):
        weights[part, :NY, part * NY : (part + 1) * NY] = sy
    return weights.reshape(TILES * LANES, TILES * LANES)


def x_basis():
    padded = np.zeros((NX, LANES))
    padded[:, :NX] = np_basis(NX)
    return padded


def forward(own, other, ndev, scale):
    depth = own.shape[0]
    rows = -(-(2 * depth + depth // GROUP) // 8) * 8
    out = pl.pallas_call(
        functools.partial(forward_kernel, ndev),
        out_shape=jax.ShapeDtypeStruct((ndev * rows, LANES), F32),
        in_specs=[VMEM] * 4,
        out_specs=VMEM,
        compiler_params=limit(24),
        name="forward",
    )(np_split(x_basis() * scale), np_split(y_weights()), own, other)
    return out.reshape(ndev, rows, LANES)


def spectral_kernel(orb, vec, mux_ref, muz_ref, muy_ref, kz_ref, kzb_ref, got_ref, out_ref):
    ndev = orb * vec
    me = lax.axis_index("orb") * vec + lax.axis_index("vec")
    x = jnp.concatenate(
        [jnp.concatenate([got_ref[o * vec + k] for o in range(orb)], 0) for k in range(vec)], 1
    )
    t = dot3((kz_ref[0], kz_ref[1]), split(x))
    lane = lax.broadcasted_iota(jnp.int32, (NZ, LANES), 1)
    mux = [mux_ref[part * ndev + me] for part in range(TILES)]
    by_tile = (
        jnp.where(lane < NY, mux[0], mux[1]),
        jnp.where(lane < 2 * NY - LANES, mux[1], mux[2]),
        jnp.full((NZ, LANES), mux[2], F32),
    )
    scales = [
        math.sqrt(4.0 * math.pi) / jnp.sqrt(muz_ref[...] + (muy_ref[tile : tile + 1] + by_tile[tile]))
        for tile in range(TILES)
    ]
    fields = []
    for k in range(vec):
        tk = t[:, k * LANES : (k + 1) * LANES]
        tail = jnp.zeros((NZ, LANES), F32)
        for z in range(GROUP):
            mine = (lane >= z * TAIL) & (lane < (z + 1) * TAIL)
            tail = jnp.where(mine, tk[(2 + z) * NZ : (3 + z) * NZ], tail)
        tail = tail + pltpu.roll(tail, 2 * TAIL, 1)
        tail = tail + pltpu.roll(tail, TAIL, 1)
        fields.append((tk[:NZ] * scales[0], tk[NZ : 2 * NZ] * scales[1], tail * scales[2]))
    row = lax.broadcasted_iota(jnp.int32, (1, LANES), 1)
    gram = jnp.zeros((1, LANES), F32)
    for k in range(vec):
        for l in range(k + 1):
            f, g = fields[k], fields[l]
            terms = f[0] * g[0] + f[1] * g[1] + jnp.where(lane < TAIL, f[2] * g[2], 0.0)
            entry = jnp.sum(jnp.sum(terms, axis=0, keepdims=True), axis=1, keepdims=True)
            gram = jnp.where(row == k * vec + l, entry, gram)
    tails = fields[0][2]
    for k in range(1, vec):
        tails = jnp.where((lane >= k * TAIL) & (lane < (k + 1) * TAIL), fields[k][2], tails)
    t = jnp.concatenate([field[tile] for field in fields for tile in range(2)] + [tails], 1)
    t = dot3((kzb_ref[0], kzb_ref[1]), split(t))
    rows = out_ref.shape[0] // ndev
    zs, tiles = NZ // ndev, t.shape[1] // LANES
    for z in range(zs):
        for tile in range(tiles):
            out_ref[pl.ds(z * tiles + tile, ndev, rows), :] = t[
                z * ndev : (z + 1) * ndev, tile * LANES : (tile + 1) * LANES
            ]
    out_ref[pl.ds(zs * tiles, ndev, rows), :] = jnp.broadcast_to(gram, (ndev, LANES))


def spectral(got, orb, vec):
    ndev = orb * vec
    depth, zs = NZ // orb, NZ // ndev
    rows_in = got.shape[1]
    rows_out = -(-(zs * (2 * vec + 1) + 1) // 8) * 8
    sz = np_basis(NZ)
    kz = np.zeros((2 + GROUP, NZ, orb, rows_in))
    for o in range(orb):
        mine = sz[:, o * depth : (o + 1) * depth]
        for tile in range(2):
            kz[tile, :, o, tile * depth : (tile + 1) * depth] = mine
        for z in range(GROUP):
            kz[2 + z, :, o, 2 * depth : 2 * depth + depth // GROUP] = mine[:, z::GROUP]
    kzb = np.concatenate([sz[z::zs] for z in range(zs)])
    muy = np.tile(np_eigen(NY), TILES)
    muy = np.stack([muy[:LANES], muy[LANES : 2 * LANES], np.tile(muy[2 * LANES : 2 * LANES + TAIL], vec)])
    muz = np.broadcast_to(np_eigen(NZ)[:, None], (NZ, LANES))
    f32 = lambda x: np.ascontiguousarray(x, np.float32)
    out = pl.pallas_call(
        functools.partial(spectral_kernel, orb, vec),
        out_shape=jax.ShapeDtypeStruct((ndev * rows_out, LANES), F32),
        in_specs=[SMEM] + [VMEM] * 5,
        out_specs=VMEM,
        compiler_params=limit(32),
        name="spectral",
    )(
        f32(np_eigen(NX)),
        f32(muz),
        f32(muy),
        np_split(kz.reshape((2 + GROUP) * NZ, orb * rows_in)),
        np_split(kzb),
        got,
    )
    return out.reshape(ndev, rows_out, LANES)


def factors(gram, vec):
    entry = lambda k, l: gram[:, k * vec + l : k * vec + l + 1]
    lower = [[None] * vec for _ in range(vec)]
    inverse = [[jnp.zeros((1, 1), F32)] * vec for _ in range(vec)]
    for l in range(vec):
        pivot = entry(l, l)
        for m in range(l):
            pivot = pivot - lower[l][m] * lower[l][m]
        lower[l][l] = jnp.sqrt(pivot)
        inverse[l][l] = 1.0 / lower[l][l]
        for k in range(l + 1, vec):
            value = entry(k, l)
            for m in range(l):
                value = value - lower[k][m] * lower[l][m]
            lower[k][l] = value * inverse[l][l]
    for l in range(vec):
        for k in range(l + 1, vec):
            value = lower[k][l] * inverse[l][l]
            for m in range(l + 1, k):
                value = value + lower[k][m] * inverse[m][l]
            inverse[k][l] = -value * inverse[k][k]
    return lower, inverse


def back_kernel(ndev, vec, basis_ref, weights_ref, got_ref, factor_ref, *outs):
    zs = NZ // ndev
    tiles = 2 * vec + 1
    rows = got_ref.shape[0] // ndev
    line = lax.axis_index("vec")
    basis = (basis_ref[0], basis_ref[1])
    gram = jnp.sum(got_ref[pl.ds(zs * tiles, ndev, rows), :], axis=0, keepdims=True) / (NZ * NY * NX)
    lower, inverse = factors(gram, vec)
    at_row = lax.broadcasted_iota(jnp.int32, (vec, vec), 0)
    at_col = lax.broadcasted_iota(jnp.int32, (vec, vec), 1)
    factor = jnp.zeros((vec, vec), F32)
    for k in range(vec):
        for l in range(k + 1):
            factor = jnp.where((at_row == l) & (at_col == k), lower[k][l], factor)
    factor_ref[...] = factor
    coefficients = []
    for s in range(vec):
        to = lax.rem(line + s, vec)
        entries = []
        for k in range(vec):
            value = inverse[0][k]
            for m in range(1, vec):
                value = jnp.where(to == m, inverse[m][k], value)
            entries.append(value)
        coefficients.append(entries)
    column = lambda tile: split(
        jnp.concatenate([got_ref[pl.ds(z * tiles + tile, ndev, rows), :] for z in range(zs)], 0)
    )
    tails = column(2 * vec)
    fields = []
    for k in range(vec):
        parts = [column(2 * k), column(2 * k + 1), tails]
        t = tuple(jnp.concatenate([part[n] for part in parts], 1) for n in range(2))
        y = dot3(t, (weights_ref[0, k], weights_ref[1, k]))
        field = []
        for z in range(zs):
            block = jnp.concatenate(
                [y[z * ndev : (z + 1) * ndev, p * LANES : (p + 1) * LANES] for p in range(TILES)], 0
            )
            field.append(dot3(split(block), basis, ((0,), (0,)))[:NY])
        fields.append(field)
    for s in range(vec):
        for z in range(zs):
            mixed = coefficients[s][0] * fields[0][z]
            for k in range(1, vec):
                mixed = mixed + coefficients[s][k] * fields[k][z]
            got = to_tiles([mixed[i * SUB : (i + 1) * SUB] for i in range(GROUP)])
            for i in range(TILES):
                outs[s][pl.ds(z * PLANE + i, SUB, TILES), :] = got[i]


def back(got, ndev, vec):
    zs = NZ // ndev
    one = y_weights().T
    weights = np.zeros((vec, *one.shape))
    for k in range(vec):
        weights[k, : 2 * LANES] = one[: 2 * LANES]
        weights[k, 2 * LANES + k * TAIL : 2 * LANES + (k + 1) * TAIL] = one[2 * LANES : 2 * LANES + TAIL]
    return pl.pallas_call(
        functools.partial(back_kernel, ndev, vec),
        out_shape=[jax.ShapeDtypeStruct((vec, vec), F32)]
        + [jax.ShapeDtypeStruct((zs * PLANE, LANES), F32)] * vec,
        in_specs=[VMEM] * 3,
        out_specs=[VMEM] * (vec + 1),
        compiler_params=limit(24),
        name="back",
    )(np_split(x_basis()), np_split(weights), got.reshape(-1, LANES))


def assemble_kernel(vec, *refs):
    gots, out_ref = refs[:vec], refs[vec]
    line = lax.axis_index("vec")
    rows = gots[0].shape[0]
    for s in range(vec):
        start = pl.multiple_of(lax.rem(line - s + vec, vec) * rows, 8)
        out_ref[pl.ds(start, rows), :] = gots[s][...]


def assemble(gots):
    vec = len(gots)
    rows = gots[0].shape[0] * vec
    out = pl.pallas_call(
        functools.partial(assemble_kernel, vec),
        out_shape=jax.ShapeDtypeStruct((rows, LANES), F32),
        in_specs=[VMEM] * vec,
        out_specs=VMEM,
        compiler_params=limit(24),
        name="assemble",
    )(*gots)
    return out.reshape(1, rows // PLANE, PLANE * LANES)


def gather_kernel(n, *refs):
    for i in range(n):
        refs[-1][i] = refs[i][...]


def gather(pieces, done=()):
    n = len(pieces)
    return pl.pallas_call(
        functools.partial(gather_kernel, n),
        out_shape=jax.ShapeDtypeStruct((n, *pieces[0].shape), pieces[0].dtype),
        in_specs=[VMEM] * (n + len(done)),
        out_specs=VMEM,
        compiler_params=limit(24),
        name="gather",
    )(*pieces, *done)


def swap_cores(x, orb):
    return lax.ppermute(x, "orb", [(o, o ^ 1) for o in range(orb)])


def shift(x, axis, count):
    n = lax.axis_size(axis)
    return lax.ppermute(x, axis, [(i, (i + count) % n) for i in range(n)])


def responses(orbitals, energies, trial_potential, local_potential):
    orb, vec = lax.axis_size("orb"), lax.axis_size("vec")
    chips = orb // 2
    own, edge, psi, pieces = windows(orbitals, energies, trial_potential, local_potential, orb, vec)
    adjacent = [(o, o + 1) for o in range(1, orb - 1, 2)] + [(o + 1, o) for o in range(1, orb - 1, 2)]
    same_core = [(o, o + 2) for o in range(1, orb - 2, 2)] + [(o, o - 2) for o in range(2, orb, 2)]
    v, d = potential_rows(
        own, swap_cores(own, orb), lax.ppermute(edge, "orb", adjacent), lax.ppermute(edge, "orb", same_core)
    )
    order = sorted(range(1, chips), key=lambda r: min(r, chips - r))
    arrived = []
    for r in order:
        perm = [(2 * a + c, 2 * ((a + r) % chips) + c) for a in range(chips) for c in range(2)]
        arrived.append(lax.ppermute(pieces[r - 1], "orb", perm))
    total = solve_window([p[None] for p in psi], 0, v, d, None, False)
    done, number = (), 1
    while arrived:
        held, arrived = arrived[:2], arrived[2:]
        held = gather(held, done)
        done = (total,)
        psi = [held] + [shift(held, "vec", n) for n in range(1, vec)]
        for which in range(held.shape[0]):
            number += 1
            total = solve_window(psi, which, v, d, total, number == chips)
    return total[0], swap_cores(total[1], orb)


def slab_body(orbitals, energies, trial_potential, local_potential):
    orb, vec = lax.axis_size("orb"), lax.axis_size("vec")
    ndev = orb * vec
    both = ("orb", "vec")
    own, other = responses(orbitals, energies, trial_potential, local_potential)
    got = lax.all_to_all(forward(own, other, ndev, 4.0 / orb), both, 0, 0, tiled=True)
    got = lax.all_to_all(spectral(got, orb, vec), both, 0, 0, tiled=True)
    factor, *slots = back(got, ndev, vec)
    gots = [slots[0]] + [shift(slots[s], "vec", s) for s in range(1, vec)]
    return assemble(gots), factor


def solution(mesh):
    orb, vec = mesh.shape["orb"], mesh.shape["vec"]
    placed = (P("orb", None, None), P("orb"), P("vec", "orb", None), P("orb", None))

    def body(orbitals, energies, trial_potential, local_potential):
        one = orbitals.shape[0] == 1 and trial_potential.shape[0] == 1
        plan = slab_body if one and fits(orb, vec) else general_body
        return plan(orbitals, energies, trial_potential, local_potential)

    return jax.shard_map(
        body, mesh=mesh, in_specs=placed, out_specs=(P("vec", "orb", None), P()), check_vma=False
    )
```

```python
import functools
import math

import jax
import jax.numpy as jnp
import ml_dtypes
import numpy as np
from jax import lax
from jax.experimental import pallas as pl
from jax.experimental.pallas import tpu as pltpu
from jax.sharding import PartitionSpec as P

NZ = 96
NY = 96
NX = 96
STEPS = 4

BF16 = jnp.bfloat16
F32 = jnp.float32
LANES = 128
WEIGHTS = [1.0 / (1.0 + 0.8 * math.cos(math.pi * (2 * s + 1) / (2 * STEPS))) for s in range(STEPS)]


def neighbours(field):
    depth, flat = field.shape
    zero_plane = jnp.zeros((1, flat), field.dtype)
    total = jnp.concatenate([zero_plane, field[:-1]], 0) + jnp.concatenate(
        [field[1:], zero_plane], 0
    )
    zero_rows = jnp.zeros((depth, NX), field.dtype)
    total = (
        total
        + jnp.concatenate([zero_rows, field[:, :-NX]], 1)
        + jnp.concatenate([field[:, NX:], zero_rows], 1)
    )
    column = jnp.arange(flat) % NX
    zero_col = jnp.zeros((depth, 1), field.dtype)
    left = jnp.concatenate([zero_col, field[:, :-1]], 1) * (column > 0).astype(field.dtype)
    right = jnp.concatenate([field[:, 1:], zero_col], 1) * (column < NX - 1).astype(field.dtype)
    return total + left + right


def solve(psi, perturb, potential, energy):
    diag = 3.25 + potential - energy
    source = -perturb * psi
    answer = jnp.zeros_like(psi)
    for step in range(STEPS):
        weight = 1.0 / (1.0 + 0.8 * jnp.cos(jnp.pi * (2 * step + 1) / (2 * STEPS)))
        applied = diag * answer - 0.5 * neighbours(answer)
        answer = answer + weight * (source - applied) / diag
    return answer


def sine_basis(count):
    index = jnp.arange(count, dtype=jnp.float32) + 1.0
    return jnp.sqrt(2.0 / (count + 1)) * jnp.sin(
        jnp.pi * index[:, None] * index[None, :] / (count + 1)
    )


def eigen_of(position, count):
    return 2.0 - 2.0 * jnp.cos(jnp.pi * (position.astype(jnp.float32) + 1.0) / (count + 1))


def planes(field):
    high = lax.Precision.HIGHEST
    depth = field.shape[0]
    cube = field.reshape(depth, NY, NX)
    cube = jnp.einsum("zyx,cx->zyc", cube, sine_basis(NX), precision=high)
    cube = jnp.einsum("zyc,by->zbc", cube, sine_basis(NY), precision=high)
    return cube.reshape(depth, NY * NX)


def scale_columns(columns, start):
    high = lax.Precision.HIGHEST
    width = columns.shape[1]
    position = start + jnp.arange(width)
    denom = (
        eigen_of(jnp.arange(NZ), NZ)[:, None]
        + eigen_of(position // NX, NY)[None, :]
        + eigen_of(position % NX, NX)[None, :]
    )
    basis = sine_basis(NZ)
    spectral = jnp.dot(basis, columns, precision=high) * (jnp.sqrt(4.0 * jnp.pi) / jnp.sqrt(denom))
    return jnp.dot(basis, spectral, precision=high)


def coulomb_slab(slab):
    columns = lax.all_to_all(planes(slab), "orb", split_axis=1, concat_axis=0, tiled=True)
    scaled = scale_columns(columns, lax.axis_index("orb") * columns.shape[1])
    back = lax.all_to_all(scaled, "orb", split_axis=0, concat_axis=1, tiled=True)
    return planes(back)


def factorize(partial_gram):
    lower = jnp.linalg.cholesky(partial_gram / (NZ * NY * NX))
    inverse = lax.linalg.triangular_solve(
        lower, jnp.eye(lower.shape[0], dtype=jnp.float32), left_side=True, lower=True
    )
    return (lower, inverse)


def general_body(orbitals, energies, trial_potential, local_potential):
    high = lax.Precision.HIGHEST
    depth = local_potential.shape[0]
    plane_cells = local_potential.shape[1]
    vector_slab = trial_potential.reshape(depth, plane_cells)
    perturb_full, potential_full = (
        lax.all_gather(vector_slab, "orb", axis=0, tiled=True),
        lax.all_gather(local_potential, "orb", axis=0, tiled=True),
    )
    perturb = perturb_full.astype(jnp.float32)
    potential = potential_full.astype(jnp.float32)
    weight = 4.0 / (orbitals.shape[0] * lax.axis_size("orb"))
    psi = orbitals[0].astype(jnp.float32)
    partial_value = psi * solve(psi, perturb, potential, energies[0])
    partial_value = partial_value * weight
    slab = lax.psum_scatter(partial_value, "orb", scatter_dimension=0, tiled=True)
    slab = coulomb_slab(slab)
    mine = slab.reshape(1, depth, plane_cells)
    gathered = lax.all_gather(mine, "vec", axis=0, tiled=True)
    flat = gathered.reshape(gathered.shape[0], depth * plane_cells)
    partial_gram = jnp.dot(flat, flat.T, precision=high)
    lower, inverse = factorize(lax.psum(partial_gram, "orb"))
    row = lax.dynamic_slice_in_dim(inverse, lax.axis_index("vec"), 1, 0)
    ortho = jnp.dot(row, flat, precision=high).reshape(1, depth, plane_cells)
    return (ortho, lower.T)


TILES = 3
GROUP = 4
SUB = 8
ROWS = GROUP * SUB
WTILES = TILES * SUB
HALO = STEPS - 1


def fits(orb, vec, norb, nv):
    return (
        norb == orb
        and nv == vec
        and orb % 2 == 0
        and NZ % orb == 0
        and NZ // orb >= 4
        and NZ // orb % 2 == 0
        and NY == vec * (ROWS - 2 * GROUP)
        and NY == TILES * ROWS
        and vec * ROWS == LANES
        and NX * GROUP == TILES * LANES
        and NX % (orb * vec) == 0
        and NZ % (orb * vec) == 0
        and STEPS <= GROUP
    )


def split(x):
    high = x.astype(BF16)
    return high, (x - high.astype(F32)).astype(BF16)


def np_split(x):
    x = np.asarray(x, np.float64)
    high = x.astype(ml_dtypes.bfloat16)
    return np.stack([high, (x - high.astype(np.float64)).astype(ml_dtypes.bfloat16)])


def dot3(a, b, dims):
    one = functools.partial(
        lax.dot_general, dimension_numbers=(dims, ((), ())), preferred_element_type=F32
    )
    return one(a[0], b[0]) + (one(a[0], b[1]) + one(a[1], b[0]))


def np_basis(count):
    index = np.arange(count, dtype=np.float64) + 1.0
    return np.sqrt(2.0 / (count + 1)) * np.sin(np.pi * np.outer(index, index) / (count + 1))


def np_eigen(count):
    return 4.0 * np.sin(np.pi * (np.arange(count, dtype=np.float64) + 1.0) / (2 * (count + 1))) ** 2


def to_rows(tiles):
    lane = lax.broadcasted_iota(jnp.int32, tiles[0].shape, 1)
    a, b, c = tiles
    return [
        a,
        pltpu.roll(jnp.where(lane >= 96, a, b), 32, 1),
        pltpu.roll(jnp.where(lane >= 64, b, c), 64, 1),
        pltpu.roll(c, 96, 1),
    ]


def to_tiles(rows):
    lane = lax.broadcasted_iota(jnp.int32, rows[0].shape, 1)
    r1, r2 = pltpu.roll(rows[1], 96, 1), pltpu.roll(rows[2], 64, 1)
    return [
        jnp.where(lane < 96, rows[0], r1),
        jnp.where(lane < 64, r1, r2),
        jnp.where(lane < 32, r2, pltpu.roll(rows[3], 32, 1)),
    ]


def first_tile(strip):
    return strip * (WTILES - 2 * TILES) - TILES


def window_start(strip):
    return jnp.clip(first_tile(strip), 0, NY * NX // LANES - WTILES)


def tile_lanes(strip, t, start=0):
    tile = jnp.clip(first_tile(strip) + t, 0, NY * NX // LANES - 1) - start
    return pl.ds(pl.multiple_of(tile * LANES, LANES), LANES)


def pack_planes(src, plane, out, pairs):
    def one(pair, carry):
        for i in range(TILES):
            top = pl.multiple_of((plane + 2 * pair) * WTILES + i * SUB, SUB)
            low = pl.multiple_of((plane + 2 * pair + 1) * WTILES + i * SUB, SUB)
            block = jnp.concatenate([src[pl.ds(top, SUB), :], src[pl.ds(low, SUB), :]], 0)
            out[pair, i] = block.astype(BF16)
        return carry

    lax.fori_loop(0, pairs, one, 0)


def windows_kernel(orb, vec, energy_ref, psi_any, v_any, pot_any, *refs):
    outs, (planes_ref, more_ref, psi_ref, v_ref, pot_ref, sem) = refs[:-6], refs[-6:]
    chips = orb // 2
    slab = NZ // chips
    depth = v_ref.shape[0]
    chip = lax.axis_index("orb") // 2
    strip = lax.axis_index("vec")
    start = window_start(strip)
    lanes = pl.ds(pl.multiple_of(start * LANES, LANES), WTILES * LANES)
    copies = [
        pltpu.make_async_copy(v_any.at[0], v_ref, sem.at[0]),
        pltpu.make_async_copy(pot_any.at[:, lanes], pot_ref, sem.at[1]),
        pltpu.make_async_copy(psi_any.at[0, :, lanes], psi_ref, sem.at[2]),
    ]
    for copy in copies:
        copy.start()
    for copy in copies:
        copy.wait()
    for n in range(vec + 1):
        for t in range(WTILES):
            row = (n * depth) * WTILES + (t % TILES) * SUB + t // TILES
            if n < vec:
                tile = v_ref[:, tile_lanes(lax.rem(strip + n, vec), t)]
            else:
                tile = pot_ref[:, tile_lanes(strip, t, start)]
            more_ref[pl.ds(row, depth, WTILES), :] = tile.astype(F32)
        pack_planes(more_ref, n * depth, outs[chips + n], depth // 2)
    zero = jnp.zeros((HALO * WTILES, LANES), F32)
    planes_ref[: HALO * WTILES, :] = zero
    planes_ref[(NZ + HALO) * WTILES :, :] = zero
    for t in range(WTILES):
        row = HALO * WTILES + (t % TILES) * SUB + t // TILES
        planes_ref[pl.ds(row, NZ, WTILES), :] = psi_ref[:, tile_lanes(strip, t, start)].astype(F32)
    energy = jnp.full((1, LANES), energy_ref[0], F32)
    high = energy.astype(BF16).astype(F32)
    middle = (energy - high).astype(BF16).astype(F32)
    low = energy - high - middle
    lane = lax.broadcasted_iota(jnp.int32, (1, LANES), 1)
    for at in range(chips):
        row = at * slab * WTILES
        held = planes_ref[row : row + 1, :]
        held = jnp.where(lane == 0, high, jnp.where(lane == 1, middle, jnp.where(lane == 2, low, held)))
        planes_ref[row : row + 1, :] = held
    for shift in range(chips):
        pack_planes(planes_ref, ((chip + shift) % chips) * slab, outs[shift], (slab + 2 * HALO) // 2)


def windows(orbitals, energies, trial, potential, orb, vec):
    chips = orb // 2
    depth = potential.shape[0]
    block = (TILES, 2 * SUB, LANES)
    pairs = (NZ // chips + 2 * HALO) // 2
    outs = [jax.ShapeDtypeStruct((pairs, *block), BF16)] * chips
    outs += [jax.ShapeDtypeStruct((depth // 2, *block), BF16)] * (vec + 1)
    got = pl.pallas_call(
        functools.partial(windows_kernel, orb, vec),
        out_shape=outs,
        in_specs=[pl.BlockSpec(memory_space=pltpu.SMEM)] + [pl.BlockSpec(memory_space=pltpu.HBM)] * 3,
        out_specs=[pl.BlockSpec(memory_space=pltpu.VMEM)] * len(outs),
        scratch_shapes=[
            pltpu.VMEM(((NZ + 2 * HALO) * WTILES, LANES), F32),
            pltpu.VMEM(((vec + 1) * depth * WTILES, LANES), F32),
            pltpu.VMEM((NZ, WTILES * LANES), BF16),
            pltpu.VMEM((depth, NY * NX), BF16),
            pltpu.VMEM((depth, WTILES * LANES), BF16),
            pltpu.SemaphoreType.DMA((3,)),
        ],
        compiler_params=pltpu.CompilerParams(vmem_limit_bytes=24 << 20),
        name="windows",
    )(energies, *(pltpu.with_memory_space_constraint(x, pltpu.HBM) for x in (orbitals, trial, potential)))
    return list(got[:chips]), list(got[chips:])


def edges_kernel(n, parts_and_more, *refs):
    parts, (own_ref, edge_ref) = refs[:n], refs[parts_and_more:]
    core = lax.axis_index("orb") % 2
    first = core * (own_ref.shape[1] - edge_ref.shape[1])
    for i, part in enumerate(parts):
        own_ref[i] = part[...]
        edge_ref[i] = part[pl.ds(first, edge_ref.shape[1])]


def edges(parts, arrived):
    pairs, *block = parts[0].shape
    n = len(parts)
    more = n + len(arrived)
    return pl.pallas_call(
        functools.partial(edges_kernel, n, more),
        out_shape=[
            jax.ShapeDtypeStruct((n, pairs, *block), BF16),
            jax.ShapeDtypeStruct((n, GROUP // 2, *block), BF16),
        ],
        in_specs=[pl.BlockSpec(memory_space=pltpu.VMEM)] * more,
        out_specs=[pl.BlockSpec(memory_space=pltpu.VMEM)] * 2,
        compiler_params=pltpu.CompilerParams(vmem_limit_bytes=24 << 20),
        name="edges",
    )(*parts, *arrived)


def with_edge_kernel(n, own_ref, edge_ref, *refs):
    out_ref = refs[n]
    core = lax.axis_index("orb") % 2
    pairs, edge = own_ref.shape[1], edge_ref.shape[1]
    out_ref[:, pl.ds((1 - core) * edge, pairs)] = own_ref[...]
    out_ref[:, pl.ds(core * pairs, edge)] = edge_ref[...]


def with_edge(own, edge, arrived):
    n, pairs, *block = own.shape
    return pl.pallas_call(
        functools.partial(with_edge_kernel, len(arrived)),
        out_shape=jax.ShapeDtypeStruct((n, pairs + edge.shape[1], *block), own.dtype),
        in_specs=[pl.BlockSpec(memory_space=pltpu.VMEM)] * (2 + len(arrived)),
        out_specs=pl.BlockSpec(memory_space=pltpu.VMEM),
        compiler_params=pltpu.CompilerParams(vmem_limit_bytes=24 << 20),
        name="with_edge",
    )(own, edge, *arrived)


def potential_rows_kernel(vec, n, mine_ref, other_ref, *refs):
    v_ref, d_ref = refs[n:]
    core = lax.axis_index("orb") % 2
    strip = lax.axis_index("vec")
    pairs = mine_ref.shape[1]
    for src, first in ((mine_ref, core * pairs), (other_ref, (1 - core) * pairs)):

        def one(pair, carry, src=src, first=first):
            plane = 2 * (first + pair)
            for n in range(vec + 1):
                rows = to_rows([src[n, pair, i].astype(F32) for i in range(TILES)])
                for zz in range(2):
                    block = jnp.concatenate([rows[i][zz * SUB : (zz + 1) * SUB] for i in range(GROUP)], 0)
                    if n < vec:
                        k = lax.rem(strip - n + vec, vec)
                        v_ref[plane + zz, pl.ds(pl.multiple_of(k * ROWS, ROWS), ROWS), :] = block
                    else:
                        d_ref[plane + zz] = 3.25 + block
            return carry

        lax.fori_loop(0, pairs, one, 0, unroll=True)


def potential_rows(mine, other, vec, arrived):
    planes = 4 * mine.shape[1]
    return pl.pallas_call(
        functools.partial(potential_rows_kernel, vec, len(arrived)),
        out_shape=[
            jax.ShapeDtypeStruct((planes, vec * ROWS, LANES), F32),
            jax.ShapeDtypeStruct((planes, ROWS, LANES), F32),
        ],
        in_specs=[pl.BlockSpec(memory_space=pltpu.VMEM)] * (2 + len(arrived)),
        out_specs=[pl.BlockSpec(memory_space=pltpu.VMEM)] * 2,
        compiler_params=pltpu.CompilerParams(vmem_limit_bytes=24 << 20),
        name="potential_rows",
    )(mine, other, *arrived)


def solve_kernel(vec, first, last, *refs):
    psi_ref, v_ref, d_ref = refs[:3]
    refs = refs[3:]
    sum_ref = None if first else refs[0]
    outs = refs[0 if first else 1 : -5]
    psi_s, h_s, c_s, u_a, u_b = refs[-5:]
    planes = d_ref.shape[0]
    depth = (planes - 2 * GROUP) // 2
    core = lax.axis_index("orb") % 2
    top = (lax.axis_index("orb") // 2) * 2 * depth - GROUP
    top_row = lax.axis_index("vec") * (ROWS - 2 * GROUP) - GROUP
    lane = lax.broadcasted_iota(jnp.int32, (SUB, LANES), 1)
    group = lax.broadcasted_iota(jnp.int32, (SUB, LANES), 0)
    inside = []
    for i in range(GROUP):
        y = top_row + group * GROUP + i
        inside.append(jnp.where((y >= 0) & (y < NY) & (lane < NX), 0.5, 0.0))
    inside = jnp.concatenate(inside, 0)
    block = psi_ref[0, 0].astype(F32)
    energy = block[0:1, 0:1] + block[0:1, 1:2] + block[0:1, 2:3]
    at = lax.broadcasted_iota(jnp.int32, (2 * LANES, LANES), 0) % LANES
    to = lax.broadcasted_iota(jnp.int32, (2 * LANES, LANES), 1)
    beside = jnp.where((at == to - 1) | (at == to + 1), 1.0, 0.0).astype(BF16)

    def begin(pair, carry):
        rows = to_rows([psi_ref[pair, i].astype(F32) for i in range(TILES)])
        for zz in range(2):
            w = GROUP - HALO + 2 * pair + zz
            z = top + w
            there = jnp.where((z >= 0) & (z < NZ), 1.0, 0.0)
            psi = jnp.concatenate([rows[i][zz * SUB : (zz + 1) * SUB] for i in range(GROUP)], 0)
            h = inside * there / (d_ref[w] - energy)
            psi_s[w] = psi
            h_s[w] = h
            scaled = -2.0 * psi * h
            for k in range(vec):
                rows_k = pl.ds(k * ROWS, ROWS)
                c = scaled * v_ref[w, rows_k, :]
                c_s[w, rows_k, :] = c
                u_a[w, rows_k, :] = WEIGHTS[0] * c
        return carry

    lax.fori_loop(0, psi_ref.shape[0], begin, 0, unroll=5)

    def stepped(src, w, weight):
        u = src[w]
        high, low = split(u)
        x = jnp.dot(jnp.concatenate([high, low], 1), beside, preferred_element_type=F32)
        near = x + (src[w - 1] + src[w + 1])
        h = h_s[w]
        new = []
        for k in range(vec):
            rows = [u[k * ROWS + i * SUB : k * ROWS + (i + 1) * SUB] for i in range(GROUP)]
            north = jnp.concatenate([pltpu.roll(rows[-1], 1, 0)] + rows[:-1], 0)
            south = jnp.concatenate(rows[1:] + [pltpu.roll(rows[0], SUB - 1, 0)], 0)
            at_k = slice(k * ROWS, (k + 1) * ROWS)
            total = near[at_k] + (north + south)
            change = c_s[w, at_k, :] + h * total
            new.append((1.0 - weight) * u[at_k] + weight * change)
        return new

    src, dst = u_a, u_b
    for step in range(1, STEPS - 1):
        low = GROUP - HALO + step

        def middle(w, carry, src=src, dst=dst, step=step):
            dst[w] = jnp.concatenate(stepped(src, w, WEIGHTS[step]), 0)
            return carry

        lax.fori_loop(low, planes - low, middle, 0, unroll=True)
        src, dst = dst, src

    def end(p, carry, out, start, src=src):
        w = GROUP + start + p
        psi = psi_s[w]
        total = jnp.concatenate([psi * new for new in stepped(src, w, WEIGHTS[STEPS - 1])], 0)
        if not first:
            total = total + sum_ref[start + p]
        out[p] = total
        return carry

    if last:
        lax.fori_loop(0, depth, functools.partial(end, out=outs[1], start=(1 - core) * depth), 0, unroll=True)
        lax.fori_loop(0, depth, functools.partial(end, out=outs[0], start=core * depth), 0, unroll=True)
    else:
        lax.fori_loop(0, 2 * depth, functools.partial(end, out=outs[0], start=0), 0, unroll=True)


def solve_window(psi, v, d, total, vec, last):
    planes = d.shape[0]
    depth = (planes - 2 * GROUP) // 2
    first = total is None
    if last:
        outs = [jax.ShapeDtypeStruct((depth, LANES, LANES), F32)] * 2
    else:
        outs = [jax.ShapeDtypeStruct((2 * depth, LANES, LANES), F32)]
    args = (psi, v, d) if first else (psi, v, d, total)
    got = pl.pallas_call(
        functools.partial(solve_kernel, vec, first, last),
        out_shape=outs,
        in_specs=[pl.BlockSpec(memory_space=pltpu.VMEM)] * len(args),
        out_specs=[pl.BlockSpec(memory_space=pltpu.VMEM)] * len(outs),
        scratch_shapes=[pltpu.VMEM((planes, ROWS, LANES), F32)] * 2
        + [pltpu.VMEM((planes, vec * ROWS, LANES), F32)] * 3,
        compiler_params=pltpu.CompilerParams(vmem_limit_bytes=32 << 20),
        name="solve_window",
    )(*args)
    return got if last else got[0]


def forward_x_kernel(ndev, basis_ref, own_ref, other_ref, out_ref):
    depth = own_ref.shape[0]
    parts = NX // ndev
    rows = out_ref.shape[0] // ndev
    basis = (basis_ref[0], basis_ref[1])
    for z in range(depth):
        chi = split(own_ref[z] + other_ref[z])
        got = dot3(basis, chi, ((1,), (1,)))
        for part in range(parts):
            out_ref[pl.ds(part * depth + z, ndev, rows), :] = got[part * ndev : (part + 1) * ndev]
    for row in range(parts * depth, rows):
        out_ref[pl.ds(row, ndev, rows), :] = jnp.zeros((ndev, LANES), F32)


def forward_x(own, other, basis, ndev):
    rows = -(-(NX // ndev) * own.shape[0] // SUB) * SUB
    out = pl.pallas_call(
        functools.partial(forward_x_kernel, ndev),
        out_shape=jax.ShapeDtypeStruct((ndev * rows, LANES), F32),
        in_specs=[pl.BlockSpec(memory_space=pltpu.VMEM)] * 3,
        out_specs=pl.BlockSpec(memory_space=pltpu.VMEM),
        compiler_params=pltpu.CompilerParams(vmem_limit_bytes=24 << 20),
        name="forward_x",
    )(basis, own, other)
    return out.reshape(ndev, rows, LANES)


def spectral_kernel(orb, vec, mux_ref, muzy_ref, wy_ref, kz_ref, kzb_ref, wyb_ref, got_ref, out_ref):
    ndev = orb * vec
    parts = NX // ndev
    me = lax.axis_index("orb") * vec + lax.axis_index("vec")
    rows = got_ref.shape[1]
    x = jnp.concatenate(
        [
            jnp.concatenate([got_ref[o * vec + v] for o in range(orb)], 0)
            for v in range(vec)
        ],
        1,
    )
    mm = ((1,), (0,))
    t = dot3(split(x), (wy_ref[0], wy_ref[1]), mm)
    t = dot3((kz_ref[0], kz_ref[1]), split(t), mm)
    scale = jnp.concatenate(
        [
            math.sqrt(4.0 * math.pi) / jnp.sqrt(muzy_ref[...] + mux_ref[part * ndev + me])
            for part in range(parts)
        ],
        0,
    )
    fields = [t[:, k * LANES : (k + 1) * LANES] * scale for k in range(vec)]
    lane = lax.broadcasted_iota(jnp.int32, (1, LANES), 1)
    gram = jnp.zeros((1, LANES), F32)
    for k in range(vec):
        for l in range(k + 1):
            entry = jnp.sum(jnp.sum(fields[k] * fields[l], axis=0, keepdims=True), axis=1, keepdims=True)
            gram = jnp.where(lane == k * vec + l, entry, gram)
    t = jnp.concatenate(fields, 1)
    t = dot3((kzb_ref[0], kzb_ref[1]), split(t), mm)
    t = dot3(split(t), (wyb_ref[0], wyb_ref[1]), mm)
    rows = out_ref.shape[0] // ndev
    groups = t.shape[0] // ndev
    for r in range(groups):
        for yt in range(TILES):
            out_ref[pl.ds(r * TILES + yt, ndev, rows), :] = t[
                r * ndev : (r + 1) * ndev, yt * LANES : (yt + 1) * LANES
            ]
    out_ref[pl.ds(groups * TILES, ndev, rows), :] = jnp.broadcast_to(gram, (ndev, LANES))


def spectral(got, orb, vec):
    ndev = orb * vec
    parts, zs = NX // ndev, NZ // ndev
    depth = NZ // orb
    strip = ROWS - 2 * GROUP
    rows_in = got.shape[1]
    rows_out = -(-(parts * zs * TILES + 1) // SUB) * SUB
    sy, sz = np_basis(NY), np_basis(NZ)
    wy = np.zeros((vec, vec, GROUP, SUB, vec, LANES))
    wyb = np.zeros((vec, LANES, TILES, vec, GROUP, SUB))
    for k in range(vec):
        for i in range(GROUP):
            for g in range(SUB):
                for v in range(vec):
                    row = v * strip - GROUP + GROUP * g + i
                    if v * strip <= row < (v + 1) * strip:
                        wy[v, k, i, g, k, :NY] = sy[row]
                for yt in range(TILES):
                    wyb[k, :NY, yt, k, i, g] = sy[yt * ROWS + GROUP * g + i]
    wy = wy.reshape(vec * LANES, vec * LANES)
    wyb = wyb.reshape(vec * LANES, TILES * LANES)
    kz = np.zeros((parts, NZ, orb, rows_in))
    kzb = np.zeros((zs, parts, ndev, parts, NZ))
    for part in range(parts):
        for o in range(orb):
            kz[part, :, o, part * depth : (part + 1) * depth] = sz[:, o * depth : (o + 1) * depth]
        for z in range(zs):
            kzb[z, part, :, part, :] = sz[z::zs]
    kz = kz.reshape(parts * NZ, orb * rows_in)
    kzb = kzb.reshape(zs * parts * ndev, parts * NZ)
    muzy = np.ones((NZ, LANES), np.float32)
    muzy[:, :NY] = np_eigen(NZ)[:, None] + np_eigen(NY)[None, :]
    mux = np_eigen(NX).astype(np.float32)
    out = pl.pallas_call(
        functools.partial(spectral_kernel, orb, vec),
        out_shape=jax.ShapeDtypeStruct((ndev * rows_out, LANES), F32),
        in_specs=[pl.BlockSpec(memory_space=pltpu.SMEM)] + [pl.BlockSpec(memory_space=pltpu.VMEM)] * 6,
        out_specs=pl.BlockSpec(memory_space=pltpu.VMEM),
        compiler_params=pltpu.CompilerParams(vmem_limit_bytes=32 << 20),
        name="spectral",
    )(mux, muzy, np_split(wy), np_split(kz), np_split(kzb), np_split(wyb), got)
    return out.reshape(ndev, rows_out, LANES)


def back_kernel(ndev, vec, basis_ref, got_ref, factor_ref, *outs):
    parts, zs = NX // ndev, NZ // ndev
    rows = got_ref.shape[0] // ndev
    strip = lax.axis_index("vec")
    basis = (basis_ref[0], basis_ref[1])
    gram = jnp.sum(got_ref[pl.ds(zs * parts * TILES, ndev, rows), :], axis=0, keepdims=True)
    gram = gram / (NZ * NY * NX)
    entry = lambda k, l: gram[:, k * vec + l : k * vec + l + 1]
    lower = [[None] * vec for _ in range(vec)]
    inverse = [[jnp.zeros((1, 1), F32)] * vec for _ in range(vec)]
    for l in range(vec):
        pivot = entry(l, l)
        for m in range(l):
            pivot = pivot - lower[l][m] * lower[l][m]
        lower[l][l] = jnp.sqrt(pivot)
        inverse[l][l] = 1.0 / lower[l][l]
        for k in range(l + 1, vec):
            value = entry(k, l)
            for m in range(l):
                value = value - lower[k][m] * lower[l][m]
            lower[k][l] = value * inverse[l][l]
    for l in range(vec):
        for k in range(l + 1, vec):
            value = lower[k][l] * inverse[l][l]
            for m in range(l + 1, k):
                value = value + lower[k][m] * inverse[m][l]
            inverse[k][l] = -value * inverse[k][k]
    at_row = lax.broadcasted_iota(jnp.int32, (vec, vec), 0)
    at_col = lax.broadcasted_iota(jnp.int32, (vec, vec), 1)
    factor = jnp.zeros((vec, vec), F32)
    for k in range(vec):
        for l in range(k + 1):
            factor = jnp.where((at_row == l) & (at_col == k), lower[k][l], factor)
    factor_ref[...] = factor
    coefficients = []
    for s in range(vec):
        to = lax.rem(strip + s, vec)
        line = []
        for k in range(vec):
            value = inverse[0][k]
            for m in range(1, vec):
                value = jnp.where(to == m, inverse[m][k], value)
            line.append(value)
        coefficients.append(line)
    for z in range(zs):
        for yt in range(TILES):
            x = jnp.concatenate(
                [
                    got_ref[pl.ds((z * parts + part) * TILES + yt, ndev, rows), :]
                    for part in range(parts)
                ],
                0,
            )
            y = dot3(split(x), basis, ((0,), (0,)))
            for s in range(vec):
                mixed = coefficients[s][0] * y[:ROWS]
                for k in range(1, vec):
                    mixed = mixed + coefficients[s][k] * y[k * ROWS : (k + 1) * ROWS]
                tiles = to_tiles([mixed[i * SUB : (i + 1) * SUB] for i in range(GROUP)])
                for i in range(TILES):
                    outs[s][pl.ds((z * TILES + yt) * WTILES + i, SUB, TILES), :] = tiles[i]


def back(got, basis, ndev, vec):
    zs = NZ // ndev
    tiles = NY * NX // LANES
    return pl.pallas_call(
        functools.partial(back_kernel, ndev, vec),
        out_shape=[jax.ShapeDtypeStruct((vec, vec), F32)]
        + [jax.ShapeDtypeStruct((zs * tiles, LANES), F32)] * vec,
        in_specs=[pl.BlockSpec(memory_space=pltpu.VMEM)] * 2,
        out_specs=[pl.BlockSpec(memory_space=pltpu.VMEM)] * (vec + 1),
        compiler_params=pltpu.CompilerParams(vmem_limit_bytes=24 << 20),
        name="back",
    )(basis, got.reshape(-1, LANES))


def assemble_kernel(vec, *refs):
    gots, out_ref = refs[:vec], refs[vec]
    line = lax.axis_index("vec")
    rows = gots[0].shape[0]
    for s in range(vec):
        start = pl.multiple_of(lax.rem(line - s + vec, vec) * rows, 8)
        out_ref[pl.ds(start, rows), :] = gots[s][...]


def assemble(gots):
    vec = len(gots)
    rows = gots[0].shape[0] * vec
    out = pl.pallas_call(
        functools.partial(assemble_kernel, vec),
        out_shape=jax.ShapeDtypeStruct((rows, LANES), F32),
        in_specs=[pl.BlockSpec(memory_space=pltpu.VMEM)] * vec,
        out_specs=pl.BlockSpec(memory_space=pltpu.VMEM),
        compiler_params=pltpu.CompilerParams(vmem_limit_bytes=24 << 20),
        name="assemble",
    )(*gots)
    return out.reshape(1, rows * LANES // (NY * NX), NY * NX)


def swap_cores(x, orb):
    return lax.ppermute(x, "orb", [(o, o ^ 1) for o in range(orb)])


def shift(x, axis, count):
    n = lax.axis_size(axis)
    return lax.ppermute(x, axis, [(i, (i + count) % n) for i in range(n)])


def responses(orbitals, energies, trial_potential, local_potential):
    orb, vec = lax.axis_size("orb"), lax.axis_size("vec")
    chips = orb // 2
    psis, parts = windows(orbitals, energies, trial_potential, local_potential, orb, vec)
    def to_chip(r):
        perm = [(2 * a + c, 2 * ((a + r) % chips) + c) for a in range(chips) for c in range(2)]
        return lax.ppermute(psis[r], "orb", perm)

    order = [1, *range(2, chips - 1), chips - 1]
    for r in order:
        psis[r] = to_chip(r)
    for n in range(1, vec):
        parts[n] = shift(parts[n], "vec", n)
    arrived = [psis[r] for r in order]
    own, edge = edges(parts, arrived[:-2])
    near = [(o, o + 1) for o in range(1, orb - 1, 2)] + [(o + 1, o) for o in range(1, orb - 1, 2)]
    edge = lax.ppermute(edge, "orb", near + [(0, 0), (orb - 1, orb - 1)])
    mine = with_edge(own, edge, arrived[-2:-1])
    v, d = potential_rows(mine, swap_cores(mine, orb), vec, [])
    total = None
    for r in [0] + order:
        total = solve_window(psis[r], v, d, total, vec, r == order[-1])
    return total[0], swap_cores(total[1], orb)


def block_body(orbitals, energies, trial_potential, local_potential):
    orb, vec = lax.axis_size("orb"), lax.axis_size("vec")
    ndev = orb * vec
    both = ("orb", "vec")
    own, other = responses(orbitals, energies, trial_potential, local_potential)
    sx = np_basis(NX)
    padded = np.zeros((NX, LANES))
    padded[:, :NX] = sx
    sent = forward_x(own, other, np_split(padded * (4.0 / orb)), ndev)
    got = lax.all_to_all(sent, both, 0, 0, tiled=True)
    sent = spectral(got, orb, vec)
    got = lax.all_to_all(sent, both, 0, 0, tiled=True)
    factor, *slots = back(got, np_split(padded), ndev, vec)
    gots = [slots[0]] + [shift(slots[s], "vec", s) for s in range(1, vec)]
    return assemble(gots), factor


def solution(mesh):
    orb, vec = mesh.shape["orb"], mesh.shape["vec"]
    placed = (P("orb", None, None), P("orb"), P("vec", "orb", None), P("orb", None))

    def body(orbitals, energies, trial_potential, local_potential):
        one = orbitals.shape[0] == 1 and trial_potential.shape[0] == 1
        plan = block_body if one and fits(orb, vec, orb, vec) else general_body
        return plan(orbitals, energies, trial_potential, local_potential)

    return jax.shard_map(
        body, mesh=mesh, in_specs=placed, out_specs=(P("vec", "orb", None), P()), check_vma=False
    )
```

```python
import functools
import math

import jax
import jax.numpy as jnp
import ml_dtypes
import numpy as np
from jax import lax
from jax.experimental import pallas as pl
from jax.experimental.pallas import tpu as pltpu
from jax.sharding import PartitionSpec as P

NZ = 96
NY = 96
NX = 96
STEPS = 4

BF16 = jnp.bfloat16
F32 = jnp.float32
LANES = 128
WEIGHTS = [1.0 / (1.0 + 0.8 * math.cos(math.pi * (2 * s + 1) / (2 * STEPS))) for s in range(STEPS)]

SCALES = [WEIGHTS[0]]
for weight_ in WEIGHTS[1:]:
    SCALES.append((1.0 - weight_) * SCALES[-1])
COEFFICIENTS = [None] + [
    (1.0, WEIGHTS[s] / SCALES[s], WEIGHTS[s] * SCALES[s - 1] / SCALES[s]) for s in range(1, STEPS)
]


def neighbours(field):
    depth, flat = field.shape
    zero_plane = jnp.zeros((1, flat), field.dtype)
    total = jnp.concatenate([zero_plane, field[:-1]], 0) + jnp.concatenate(
        [field[1:], zero_plane], 0
    )
    zero_rows = jnp.zeros((depth, NX), field.dtype)
    total = (
        total
        + jnp.concatenate([zero_rows, field[:, :-NX]], 1)
        + jnp.concatenate([field[:, NX:], zero_rows], 1)
    )
    column = jnp.arange(flat) % NX
    zero_col = jnp.zeros((depth, 1), field.dtype)
    left = jnp.concatenate([zero_col, field[:, :-1]], 1) * (column > 0).astype(field.dtype)
    right = jnp.concatenate([field[:, 1:], zero_col], 1) * (column < NX - 1).astype(field.dtype)
    return total + left + right


def solve(psi, perturb, potential, energy):
    diag = 3.25 + potential - energy
    source = -perturb * psi
    answer = jnp.zeros_like(psi)
    for step in range(STEPS):
        weight = 1.0 / (1.0 + 0.8 * jnp.cos(jnp.pi * (2 * step + 1) / (2 * STEPS)))
        applied = diag * answer - 0.5 * neighbours(answer)
        answer = answer + weight * (source - applied) / diag
    return answer


def sine_basis(count):
    index = jnp.arange(count, dtype=jnp.float32) + 1.0
    return jnp.sqrt(2.0 / (count + 1)) * jnp.sin(
        jnp.pi * index[:, None] * index[None, :] / (count + 1)
    )


def eigen_of(position, count):
    return 2.0 - 2.0 * jnp.cos(jnp.pi * (position.astype(jnp.float32) + 1.0) / (count + 1))


def planes(field):
    high = lax.Precision.HIGHEST
    depth = field.shape[0]
    cube = field.reshape(depth, NY, NX)
    cube = jnp.einsum("zyx,cx->zyc", cube, sine_basis(NX), precision=high)
    cube = jnp.einsum("zyc,by->zbc", cube, sine_basis(NY), precision=high)
    return cube.reshape(depth, NY * NX)


def scale_columns(columns, start):
    high = lax.Precision.HIGHEST
    width = columns.shape[1]
    position = start + jnp.arange(width)
    denom = (
        eigen_of(jnp.arange(NZ), NZ)[:, None]
        + eigen_of(position // NX, NY)[None, :]
        + eigen_of(position % NX, NX)[None, :]
    )
    basis = sine_basis(NZ)
    spectral = jnp.dot(basis, columns, precision=high) * (jnp.sqrt(4.0 * jnp.pi) / jnp.sqrt(denom))
    return jnp.dot(basis, spectral, precision=high)


def coulomb_slab(slab):
    columns = lax.all_to_all(planes(slab), "orb", split_axis=1, concat_axis=0, tiled=True)
    scaled = scale_columns(columns, lax.axis_index("orb") * columns.shape[1])
    back = lax.all_to_all(scaled, "orb", split_axis=0, concat_axis=1, tiled=True)
    return planes(back)


def factorize(partial_gram):
    lower = jnp.linalg.cholesky(partial_gram / (NZ * NY * NX))
    inverse = lax.linalg.triangular_solve(
        lower, jnp.eye(lower.shape[0], dtype=jnp.float32), left_side=True, lower=True
    )
    return (lower, inverse)


def general_body(orbitals, energies, trial_potential, local_potential):
    high = lax.Precision.HIGHEST
    depth = local_potential.shape[0]
    plane_cells = local_potential.shape[1]
    vector_slab = trial_potential.reshape(depth, plane_cells)
    perturb_full, potential_full = (
        lax.all_gather(vector_slab, "orb", axis=0, tiled=True),
        lax.all_gather(local_potential, "orb", axis=0, tiled=True),
    )
    perturb = perturb_full.astype(jnp.float32)
    potential = potential_full.astype(jnp.float32)
    weight = 4.0 / (orbitals.shape[0] * lax.axis_size("orb"))
    psi = orbitals[0].astype(jnp.float32)
    partial_value = psi * solve(psi, perturb, potential, energies[0])
    partial_value = partial_value * weight
    slab = lax.psum_scatter(partial_value, "orb", scatter_dimension=0, tiled=True)
    slab = coulomb_slab(slab)
    mine = slab.reshape(1, depth, plane_cells)
    gathered = lax.all_gather(mine, "vec", axis=0, tiled=True)
    flat = gathered.reshape(gathered.shape[0], depth * plane_cells)
    partial_gram = jnp.dot(flat, flat.T, precision=high)
    lower, inverse = factorize(lax.psum(partial_gram, "orb"))
    row = lax.dynamic_slice_in_dim(inverse, lax.axis_index("vec"), 1, 0)
    ortho = jnp.dot(row, flat, precision=high).reshape(1, depth, plane_cells)
    return (ortho, lower.T)


TILES = 3
GROUP = 4
SUB = 8
ROWS = GROUP * SUB
WTILES = TILES * SUB
HALO = STEPS - 1


def fits(orb, vec, norb, nv):
    return (
        norb == orb
        and nv == vec
        and orb % 2 == 0
        and NZ % orb == 0
        and NZ // orb >= 4
        and NZ // orb % 2 == 0
        and NY == vec * (ROWS - 2 * GROUP)
        and NY == TILES * ROWS
        and vec * ROWS == LANES
        and NX * GROUP == TILES * LANES
        and NX % (orb * vec) == 0
        and NZ % (orb * vec) == 0
        and STEPS <= GROUP
    )


def split(x):
    high = x.astype(BF16)
    return high, (x - high.astype(F32)).astype(BF16)


def np_split(x):
    x = np.asarray(x, np.float64)
    high = x.astype(ml_dtypes.bfloat16)
    return np.stack([high, (x - high.astype(np.float64)).astype(ml_dtypes.bfloat16)])


def dot3(a, b, dims):
    one = functools.partial(
        lax.dot_general, dimension_numbers=(dims, ((), ())), preferred_element_type=F32
    )
    return one(a[0], b[0]) + (one(a[0], b[1]) + one(a[1], b[0]))


def np_basis(count):
    index = np.arange(count, dtype=np.float64) + 1.0
    return np.sqrt(2.0 / (count + 1)) * np.sin(np.pi * np.outer(index, index) / (count + 1))


def np_eigen(count):
    return 4.0 * np.sin(np.pi * (np.arange(count, dtype=np.float64) + 1.0) / (2 * (count + 1))) ** 2


def to_rows(tiles):
    lane = lax.broadcasted_iota(jnp.int32, tiles[0].shape, 1)
    a, b, c = tiles
    return [
        a,
        pltpu.roll(jnp.where(lane >= 96, a, b), 32, 1),
        pltpu.roll(jnp.where(lane >= 64, b, c), 64, 1),
        pltpu.roll(c, 96, 1),
    ]


def to_tiles(rows):
    lane = lax.broadcasted_iota(jnp.int32, rows[0].shape, 1)
    r1, r2 = pltpu.roll(rows[1], 96, 1), pltpu.roll(rows[2], 64, 1)
    return [
        jnp.where(lane < 96, rows[0], r1),
        jnp.where(lane < 64, r1, r2),
        jnp.where(lane < 32, r2, pltpu.roll(rows[3], 32, 1)),
    ]


def first_tile(strip):
    return strip * (WTILES - 2 * TILES) - TILES


def window_start(strip):
    return jnp.clip(first_tile(strip), 0, NY * NX // LANES - WTILES)


def tile_lanes(strip, t, start=0):
    tile = jnp.clip(first_tile(strip) + t, 0, NY * NX // LANES - 1) - start
    return pl.ds(pl.multiple_of(tile * LANES, LANES), LANES)


def pack_planes(src, plane, out, pairs):
    def one(pair, carry):
        for i in range(TILES):
            top = pl.multiple_of((plane + 2 * pair) * WTILES + i * SUB, SUB)
            low = pl.multiple_of((plane + 2 * pair + 1) * WTILES + i * SUB, SUB)
            block = jnp.concatenate([src[pl.ds(top, SUB), :], src[pl.ds(low, SUB), :]], 0)
            out[pair, i] = block.astype(BF16)
        return carry

    lax.fori_loop(0, pairs, one, 0)


def windows_kernel(orb, vec, energy_ref, psi_any, v_any, pot_any, *refs):
    outs, (planes_ref, more_ref, psi_ref, v_ref, pot_ref, sem) = refs[:-6], refs[-6:]
    chips = orb // 2
    slab = NZ // chips
    depth = v_ref.shape[0]
    chip = lax.axis_index("orb") // 2
    strip = lax.axis_index("vec")
    start = window_start(strip)
    lanes = pl.ds(pl.multiple_of(start * LANES, LANES), WTILES * LANES)
    copies = [
        pltpu.make_async_copy(v_any.at[0], v_ref, sem.at[0]),
        pltpu.make_async_copy(pot_any.at[:, lanes], pot_ref, sem.at[1]),
        pltpu.make_async_copy(psi_any.at[0, :, lanes], psi_ref, sem.at[2]),
    ]
    for copy in copies:
        copy.start()
    for copy in copies:
        copy.wait()
    for n in range(vec + 1):
        for t in range(WTILES):
            row = (n * depth) * WTILES + (t % TILES) * SUB + t // TILES
            if n < vec:
                tile = v_ref[:, tile_lanes(lax.rem(strip + n, vec), t)]
            else:
                tile = pot_ref[:, tile_lanes(strip, t, start)]
            more_ref[pl.ds(row, depth, WTILES), :] = tile.astype(F32)
        pack_planes(more_ref, n * depth, outs[chips + n], depth // 2)
    zero = jnp.zeros((HALO * WTILES, LANES), F32)
    planes_ref[: HALO * WTILES, :] = zero
    planes_ref[(NZ + HALO) * WTILES :, :] = zero
    for t in range(WTILES):
        row = HALO * WTILES + (t % TILES) * SUB + t // TILES
        planes_ref[pl.ds(row, NZ, WTILES), :] = psi_ref[:, tile_lanes(strip, t, start)].astype(F32)
    energy = jnp.full((1, LANES), energy_ref[0], F32)
    high = energy.astype(BF16).astype(F32)
    middle = (energy - high).astype(BF16).astype(F32)
    low = energy - high - middle
    lane = lax.broadcasted_iota(jnp.int32, (1, LANES), 1)
    for at in range(chips):
        row = at * slab * WTILES
        held = planes_ref[row : row + 1, :]
        held = jnp.where(lane == 0, high, jnp.where(lane == 1, middle, jnp.where(lane == 2, low, held)))
        planes_ref[row : row + 1, :] = held
    for shift in range(chips):
        pack_planes(planes_ref, ((chip + shift) % chips) * slab, outs[shift], (slab + 2 * HALO) // 2)


def windows(orbitals, energies, trial, potential, orb, vec):
    chips = orb // 2
    depth = potential.shape[0]
    block = (TILES, 2 * SUB, LANES)
    pairs = (NZ // chips + 2 * HALO) // 2
    outs = [jax.ShapeDtypeStruct((pairs, *block), BF16)] * chips
    outs += [jax.ShapeDtypeStruct((depth // 2, *block), BF16)] * (vec + 1)
    got = pl.pallas_call(
        functools.partial(windows_kernel, orb, vec),
        out_shape=outs,
        in_specs=[pl.BlockSpec(memory_space=pltpu.SMEM)] + [pl.BlockSpec(memory_space=pltpu.HBM)] * 3,
        out_specs=[pl.BlockSpec(memory_space=pltpu.VMEM)] * len(outs),
        scratch_shapes=[
            pltpu.VMEM(((NZ + 2 * HALO) * WTILES, LANES), F32),
            pltpu.VMEM(((vec + 1) * depth * WTILES, LANES), F32),
            pltpu.VMEM((NZ, WTILES * LANES), BF16),
            pltpu.VMEM((depth, NY * NX), BF16),
            pltpu.VMEM((depth, WTILES * LANES), BF16),
            pltpu.SemaphoreType.DMA((3,)),
        ],
        compiler_params=pltpu.CompilerParams(vmem_limit_bytes=24 << 20),
        name="windows",
    )(energies, *(pltpu.with_memory_space_constraint(x, pltpu.HBM) for x in (orbitals, trial, potential)))
    return list(got[:chips]), list(got[chips:])


def edges_kernel(n, parts_and_more, *refs):
    parts, (own_ref, edge_ref) = refs[:n], refs[parts_and_more:]
    core = lax.axis_index("orb") % 2
    first = core * (own_ref.shape[1] - edge_ref.shape[1])
    for i, part in enumerate(parts):
        own_ref[i] = part[...]
        edge_ref[i] = part[pl.ds(first, edge_ref.shape[1])]


def edges(parts, arrived):
    pairs, *block = parts[0].shape
    n = len(parts)
    more = n + len(arrived)
    return pl.pallas_call(
        functools.partial(edges_kernel, n, more),
        out_shape=[
            jax.ShapeDtypeStruct((n, pairs, *block), BF16),
            jax.ShapeDtypeStruct((n, GROUP // 2, *block), BF16),
        ],
        in_specs=[pl.BlockSpec(memory_space=pltpu.VMEM)] * more,
        out_specs=[pl.BlockSpec(memory_space=pltpu.VMEM)] * 2,
        compiler_params=pltpu.CompilerParams(vmem_limit_bytes=24 << 20),
        name="edges",
    )(*parts, *arrived)


def with_edge_kernel(n, own_ref, edge_ref, *refs):
    out_ref = refs[n]
    core = lax.axis_index("orb") % 2
    pairs, edge = own_ref.shape[1], edge_ref.shape[1]
    out_ref[:, pl.ds((1 - core) * edge, pairs)] = own_ref[...]
    out_ref[:, pl.ds(core * pairs, edge)] = edge_ref[...]


def with_edge(own, edge, arrived):
    n, pairs, *block = own.shape
    return pl.pallas_call(
        functools.partial(with_edge_kernel, len(arrived)),
        out_shape=jax.ShapeDtypeStruct((n, pairs + edge.shape[1], *block), own.dtype),
        in_specs=[pl.BlockSpec(memory_space=pltpu.VMEM)] * (2 + len(arrived)),
        out_specs=pl.BlockSpec(memory_space=pltpu.VMEM),
        compiler_params=pltpu.CompilerParams(vmem_limit_bytes=24 << 20),
        name="with_edge",
    )(own, edge, *arrived)


def potential_rows_kernel(vec, n, mine_ref, other_ref, *refs):
    v_ref, d_ref = refs[n:]
    core = lax.axis_index("orb") % 2
    strip = lax.axis_index("vec")
    pairs = mine_ref.shape[1]
    for src, first in ((mine_ref, core * pairs), (other_ref, (1 - core) * pairs)):

        def one(pair, carry, src=src, first=first):
            plane = 2 * (first + pair)
            for n in range(vec + 1):
                rows = to_rows([src[n, pair, i].astype(F32) for i in range(TILES)])
                for zz in range(2):
                    block = jnp.concatenate([rows[i][zz * SUB : (zz + 1) * SUB] for i in range(GROUP)], 0)
                    if n < vec:
                        k = lax.rem(strip - n + vec, vec)
                        v_ref[plane + zz, pl.ds(pl.multiple_of(k * ROWS, ROWS), ROWS), :] = block
                    else:
                        d_ref[plane + zz] = 3.25 + block
            return carry

        lax.fori_loop(0, pairs, one, 0, unroll=True)


def potential_rows(mine, other, vec, arrived):
    planes = 4 * mine.shape[1]
    return pl.pallas_call(
        functools.partial(potential_rows_kernel, vec, len(arrived)),
        out_shape=[
            jax.ShapeDtypeStruct((planes, vec * ROWS, LANES), F32),
            jax.ShapeDtypeStruct((planes, ROWS, LANES), F32),
        ],
        in_specs=[pl.BlockSpec(memory_space=pltpu.VMEM)] * (2 + len(arrived)),
        out_specs=[pl.BlockSpec(memory_space=pltpu.VMEM)] * 2,
        compiler_params=pltpu.CompilerParams(vmem_limit_bytes=24 << 20),
        name="potential_rows",
    )(mine, other, *arrived)


def solve_kernel(vec, first, last, *refs):
    psi_ref, v_ref, d_ref = refs[:3]
    refs = refs[3:]
    sum_ref = None if first else refs[0]
    outs = refs[0 if first else 1 : -5]
    psi_s, h_s, c_s, u_a, u_b = refs[-5:]
    planes = d_ref.shape[0]
    depth = (planes - 2 * GROUP) // 2
    core = lax.axis_index("orb") % 2
    top = (lax.axis_index("orb") // 2) * 2 * depth - GROUP
    top_row = lax.axis_index("vec") * (ROWS - 2 * GROUP) - GROUP
    lane = lax.broadcasted_iota(jnp.int32, (SUB, LANES), 1)
    group = lax.broadcasted_iota(jnp.int32, (SUB, LANES), 0)
    inside = []
    for i in range(GROUP):
        y = top_row + group * GROUP + i
        inside.append(jnp.where((y >= 0) & (y < NY) & (lane < NX), 0.5, 0.0))
    inside = jnp.concatenate(inside, 0)
    block = psi_ref[0, 0].astype(F32)
    energy = block[0:1, 0:1] + block[0:1, 1:2] + block[0:1, 2:3]
    at = lax.broadcasted_iota(jnp.int32, (2 * LANES, LANES), 0) % LANES
    to = lax.broadcasted_iota(jnp.int32, (2 * LANES, LANES), 1)
    beside = jnp.where((at == to - 1) | (at == to + 1), 1.0, 0.0).astype(BF16)

    def begin(pair, carry):
        rows = to_rows([psi_ref[pair, i].astype(F32) for i in range(TILES)])
        for zz in range(2):
            w = GROUP - HALO + 2 * pair + zz
            z = top + w
            there = jnp.where((z >= 0) & (z < NZ), 1.0, 0.0)
            psi = jnp.concatenate([rows[i][zz * SUB : (zz + 1) * SUB] for i in range(GROUP)], 0)
            h = inside * there / (d_ref[w] - energy)
            psi_s[w] = SCALES[STEPS - 1] * psi
            h_s[w] = h
            scaled = -2.0 * psi * h
            for k in range(vec):
                rows_k = pl.ds(k * ROWS, ROWS)
                c_s[w, rows_k, :] = scaled * v_ref[w, rows_k, :]
        return carry

    lax.fori_loop(0, psi_ref.shape[0], begin, 0, unroll=5)

    def stepped(src, w, step):
        u = src[w]
        high, low = split(u)
        x = jnp.dot(jnp.concatenate([high, low], 1), beside, preferred_element_type=F32)
        near = x + (src[w - 1] + src[w + 1])
        own, given, around = COEFFICIENTS[step]
        h = around * h_s[w]
        new = []
        for k in range(vec):
            rows = [u[k * ROWS + i * SUB : k * ROWS + (i + 1) * SUB] for i in range(GROUP)]
            north = jnp.concatenate([pltpu.roll(rows[-1], 1, 0)] + rows[:-1], 0)
            south = jnp.concatenate(rows[1:] + [pltpu.roll(rows[0], SUB - 1, 0)], 0)
            at_k = slice(k * ROWS, (k + 1) * ROWS)
            change = h * (near[at_k] + (north + south))
            if src is c_s:
                new.append((own + given) * u[at_k] + change)
            else:
                new.append((u[at_k] + given * c_s[w, at_k, :]) + change)
        return new

    src, dst = c_s, u_a
    for step in range(1, STEPS - 1):
        low = GROUP - HALO + step

        def middle(w, carry, src=src, dst=dst, step=step):
            dst[w] = jnp.concatenate(stepped(src, w, step), 0)
            return carry

        lax.fori_loop(low, planes - low, middle, 0, unroll=True)
        src, dst = dst, (u_b if dst is u_a else u_a)

    def end(p, carry, out, start, src=src):
        w = GROUP + start + p
        psi = psi_s[w]
        total = jnp.concatenate([psi * new for new in stepped(src, w, STEPS - 1)], 0)
        if not first:
            total = total + sum_ref[start + p]
        out[p] = total
        return carry

    if last:
        lax.fori_loop(0, depth, functools.partial(end, out=outs[1], start=(1 - core) * depth), 0, unroll=True)
        lax.fori_loop(0, depth, functools.partial(end, out=outs[0], start=core * depth), 0, unroll=True)
    else:
        lax.fori_loop(0, 2 * depth, functools.partial(end, out=outs[0], start=0), 0, unroll=True)


def solve_window(psi, v, d, total, vec, last):
    planes = d.shape[0]
    depth = (planes - 2 * GROUP) // 2
    first = total is None
    if last:
        outs = [jax.ShapeDtypeStruct((depth, LANES, LANES), F32)] * 2
    else:
        outs = [jax.ShapeDtypeStruct((2 * depth, LANES, LANES), F32)]
    args = (psi, v, d) if first else (psi, v, d, total)
    got = pl.pallas_call(
        functools.partial(solve_kernel, vec, first, last),
        out_shape=outs,
        in_specs=[pl.BlockSpec(memory_space=pltpu.VMEM)] * len(args),
        out_specs=[pl.BlockSpec(memory_space=pltpu.VMEM)] * len(outs),
        scratch_shapes=[pltpu.VMEM((planes, ROWS, LANES), F32)] * 2
        + [pltpu.VMEM((planes, vec * ROWS, LANES), F32)] * 3,
        compiler_params=pltpu.CompilerParams(vmem_limit_bytes=32 << 20),
        name="solve_window",
    )(*args)
    return got if last else got[0]


def forward_x_kernel(ndev, basis_ref, own_ref, other_ref, out_ref):
    depth = own_ref.shape[0]
    parts = NX // ndev
    rows = out_ref.shape[0] // ndev
    basis = (basis_ref[0], basis_ref[1])
    for z in range(depth):
        chi = split(own_ref[z] + other_ref[z])
        got = dot3(basis, chi, ((1,), (1,)))
        for part in range(parts):
            out_ref[pl.ds(part * depth + z, ndev, rows), :] = got[part * ndev : (part + 1) * ndev]
    for row in range(parts * depth, rows):
        out_ref[pl.ds(row, ndev, rows), :] = jnp.zeros((ndev, LANES), F32)


def forward_x(own, other, basis, ndev):
    rows = -(-(NX // ndev) * own.shape[0] // SUB) * SUB
    out = pl.pallas_call(
        functools.partial(forward_x_kernel, ndev),
        out_shape=jax.ShapeDtypeStruct((ndev * rows, LANES), F32),
        in_specs=[pl.BlockSpec(memory_space=pltpu.VMEM)] * 3,
        out_specs=pl.BlockSpec(memory_space=pltpu.VMEM),
        compiler_params=pltpu.CompilerParams(vmem_limit_bytes=24 << 20),
        name="forward_x",
    )(basis, own, other)
    return out.reshape(ndev, rows, LANES)


def spectral_kernel(orb, vec, mux_ref, muzy_ref, wy_ref, kz_ref, kzb_ref, wyb_ref, got_ref, out_ref):
    ndev = orb * vec
    parts = NX // ndev
    me = lax.axis_index("orb") * vec + lax.axis_index("vec")
    rows = got_ref.shape[1]
    x = jnp.concatenate(
        [
            jnp.concatenate([got_ref[o * vec + v] for o in range(orb)], 0)
            for v in range(vec)
        ],
        1,
    )
    mm = ((1,), (0,))
    t = dot3(split(x), (wy_ref[0], wy_ref[1]), mm)
    t = dot3((kz_ref[0], kz_ref[1]), split(t), mm)
    scale = jnp.concatenate(
        [
            math.sqrt(4.0 * math.pi) / jnp.sqrt(muzy_ref[...] + mux_ref[part * ndev + me])
            for part in range(parts)
        ],
        0,
    )
    fields = [t[:, k * LANES : (k + 1) * LANES] * scale for k in range(vec)]
    lane = lax.broadcasted_iota(jnp.int32, (1, LANES), 1)
    gram = jnp.zeros((1, LANES), F32)
    for k in range(vec):
        for l in range(k + 1):
            entry = jnp.sum(jnp.sum(fields[k] * fields[l], axis=0, keepdims=True), axis=1, keepdims=True)
            gram = jnp.where(lane == k * vec + l, entry, gram)
    t = jnp.concatenate(fields, 1)
    t = dot3((kzb_ref[0], kzb_ref[1]), split(t), mm)
    t = dot3(split(t), (wyb_ref[0], wyb_ref[1]), mm)
    rows = out_ref.shape[0] // ndev
    groups = t.shape[0] // ndev
    for r in range(groups):
        for yt in range(TILES):
            out_ref[pl.ds(r * TILES + yt, ndev, rows), :] = t[
                r * ndev : (r + 1) * ndev, yt * LANES : (yt + 1) * LANES
            ]
    out_ref[pl.ds(groups * TILES, ndev, rows), :] = jnp.broadcast_to(gram, (ndev, LANES))


def spectral(got, orb, vec):
    ndev = orb * vec
    parts, zs = NX // ndev, NZ // ndev
    depth = NZ // orb
    strip = ROWS - 2 * GROUP
    rows_in = got.shape[1]
    rows_out = -(-(parts * zs * TILES + 1) // SUB) * SUB
    sy, sz = np_basis(NY), np_basis(NZ)
    wy = np.zeros((vec, vec, GROUP, SUB, vec, LANES))
    wyb = np.zeros((vec, LANES, TILES, vec, GROUP, SUB))
    for k in range(vec):
        for i in range(GROUP):
            for g in range(SUB):
                for v in range(vec):
                    row = v * strip - GROUP + GROUP * g + i
                    if v * strip <= row < (v + 1) * strip:
                        wy[v, k, i, g, k, :NY] = sy[row]
                for yt in range(TILES):
                    wyb[k, :NY, yt, k, i, g] = sy[yt * ROWS + GROUP * g + i]
    wy = wy.reshape(vec * LANES, vec * LANES)
    wyb = wyb.reshape(vec * LANES, TILES * LANES)
    kz = np.zeros((parts, NZ, orb, rows_in))
    kzb = np.zeros((zs, parts, ndev, parts, NZ))
    for part in range(parts):
        for o in range(orb):
            kz[part, :, o, part * depth : (part + 1) * depth] = sz[:, o * depth : (o + 1) * depth]
        for z in range(zs):
            kzb[z, part, :, part, :] = sz[z::zs]
    kz = kz.reshape(parts * NZ, orb * rows_in)
    kzb = kzb.reshape(zs * parts * ndev, parts * NZ)
    muzy = np.ones((NZ, LANES), np.float32)
    muzy[:, :NY] = np_eigen(NZ)[:, None] + np_eigen(NY)[None, :]
    mux = np_eigen(NX).astype(np.float32)
    out = pl.pallas_call(
        functools.partial(spectral_kernel, orb, vec),
        out_shape=jax.ShapeDtypeStruct((ndev * rows_out, LANES), F32),
        in_specs=[pl.BlockSpec(memory_space=pltpu.SMEM)] + [pl.BlockSpec(memory_space=pltpu.VMEM)] * 6,
        out_specs=pl.BlockSpec(memory_space=pltpu.VMEM),
        compiler_params=pltpu.CompilerParams(vmem_limit_bytes=32 << 20),
        name="spectral",
    )(mux, muzy, np_split(wy), np_split(kz), np_split(kzb), np_split(wyb), got)
    return out.reshape(ndev, rows_out, LANES)


def back_kernel(ndev, vec, basis_ref, got_ref, factor_ref, *outs):
    parts, zs = NX // ndev, NZ // ndev
    rows = got_ref.shape[0] // ndev
    strip = lax.axis_index("vec")
    basis = (basis_ref[0], basis_ref[1])
    gram = jnp.sum(got_ref[pl.ds(zs * parts * TILES, ndev, rows), :], axis=0, keepdims=True)
    gram = gram / (NZ * NY * NX)
    entry = lambda k, l: gram[:, k * vec + l : k * vec + l + 1]
    lower = [[None] * vec for _ in range(vec)]
    inverse = [[jnp.zeros((1, 1), F32)] * vec for _ in range(vec)]
    for l in range(vec):
        pivot = entry(l, l)
        for m in range(l):
            pivot = pivot - lower[l][m] * lower[l][m]
        lower[l][l] = jnp.sqrt(pivot)
        inverse[l][l] = 1.0 / lower[l][l]
        for k in range(l + 1, vec):
            value = entry(k, l)
            for m in range(l):
                value = value - lower[k][m] * lower[l][m]
            lower[k][l] = value * inverse[l][l]
    for l in range(vec):
        for k in range(l + 1, vec):
            value = lower[k][l] * inverse[l][l]
            for m in range(l + 1, k):
                value = value + lower[k][m] * inverse[m][l]
            inverse[k][l] = -value * inverse[k][k]
    at_row = lax.broadcasted_iota(jnp.int32, (vec, vec), 0)
    at_col = lax.broadcasted_iota(jnp.int32, (vec, vec), 1)
    factor = jnp.zeros((vec, vec), F32)
    for k in range(vec):
        for l in range(k + 1):
            factor = jnp.where((at_row == l) & (at_col == k), lower[k][l], factor)
    factor_ref[...] = factor
    coefficients = []
    for s in range(vec):
        to = lax.rem(strip + s, vec)
        line = []
        for k in range(vec):
            value = inverse[0][k]
            for m in range(1, vec):
                value = jnp.where(to == m, inverse[m][k], value)
            line.append(value)
        coefficients.append(line)
    for z in range(zs):
        for yt in range(TILES):
            x = jnp.concatenate(
                [
                    got_ref[pl.ds((z * parts + part) * TILES + yt, ndev, rows), :]
                    for part in range(parts)
                ],
                0,
            )
            y = dot3(split(x), basis, ((0,), (0,)))
            for s in range(vec):
                mixed = coefficients[s][0] * y[:ROWS]
                for k in range(1, vec):
                    mixed = mixed + coefficients[s][k] * y[k * ROWS : (k + 1) * ROWS]
                tiles = to_tiles([mixed[i * SUB : (i + 1) * SUB] for i in range(GROUP)])
                for i in range(TILES):
                    outs[s][pl.ds((z * TILES + yt) * WTILES + i, SUB, TILES), :] = tiles[i]


def back(got, basis, ndev, vec):
    zs = NZ // ndev
    tiles = NY * NX // LANES
    return pl.pallas_call(
        functools.partial(back_kernel, ndev, vec),
        out_shape=[jax.ShapeDtypeStruct((vec, vec), F32)]
        + [jax.ShapeDtypeStruct((zs * tiles, LANES), F32)] * vec,
        in_specs=[pl.BlockSpec(memory_space=pltpu.VMEM)] * 2,
        out_specs=[pl.BlockSpec(memory_space=pltpu.VMEM)] * (vec + 1),
        compiler_params=pltpu.CompilerParams(vmem_limit_bytes=24 << 20),
        name="back",
    )(basis, got.reshape(-1, LANES))


def assemble_kernel(vec, *refs):
    gots, out_ref = refs[:vec], refs[vec]
    line = lax.axis_index("vec")
    rows = gots[0].shape[0]
    for s in range(vec):
        start = pl.multiple_of(lax.rem(line - s + vec, vec) * rows, 8)
        out_ref[pl.ds(start, rows), :] = gots[s][...]


def assemble(gots):
    vec = len(gots)
    rows = gots[0].shape[0] * vec
    out = pl.pallas_call(
        functools.partial(assemble_kernel, vec),
        out_shape=jax.ShapeDtypeStruct((rows, LANES), F32),
        in_specs=[pl.BlockSpec(memory_space=pltpu.VMEM)] * vec,
        out_specs=pl.BlockSpec(memory_space=pltpu.VMEM),
        compiler_params=pltpu.CompilerParams(vmem_limit_bytes=24 << 20),
        name="assemble",
    )(*gots)
    return out.reshape(1, rows * LANES // (NY * NX), NY * NX)


def swap_cores(x, orb):
    return lax.ppermute(x, "orb", [(o, o ^ 1) for o in range(orb)])


def shift(x, axis, count):
    n = lax.axis_size(axis)
    return lax.ppermute(x, axis, [(i, (i + count) % n) for i in range(n)])


def responses(orbitals, energies, trial_potential, local_potential):
    orb, vec = lax.axis_size("orb"), lax.axis_size("vec")
    chips = orb // 2
    psis, parts = windows(orbitals, energies, trial_potential, local_potential, orb, vec)
    def to_chip(r):
        perm = [(2 * a + c, 2 * ((a + r) % chips) + c) for a in range(chips) for c in range(2)]
        return lax.ppermute(psis[r], "orb", perm)

    order = [1, chips - 1, *range(2, chips - 1)]
    for r in order:
        psis[r] = to_chip(r)
    for n in range(1, vec):
        parts[n] = shift(parts[n], "vec", n)
    arrived = [psis[r] for r in order]
    own, edge = edges(parts, [])
    near = [(o, o + 1) for o in range(1, orb - 1, 2)] + [(o + 1, o) for o in range(1, orb - 1, 2)]
    edge = lax.ppermute(edge, "orb", near + [(0, 0), (orb - 1, orb - 1)])
    mine = with_edge(own, edge, arrived[:2])
    v, d = potential_rows(mine, swap_cores(mine, orb), vec, [])
    total = None
    for r in [0] + order:
        total = solve_window(psis[r], v, d, total, vec, r == order[-1])
    return total[0], swap_cores(total[1], orb)


def block_body(orbitals, energies, trial_potential, local_potential):
    orb, vec = lax.axis_size("orb"), lax.axis_size("vec")
    ndev = orb * vec
    both = ("orb", "vec")
    own, other = responses(orbitals, energies, trial_potential, local_potential)
    sx = np_basis(NX)
    padded = np.zeros((NX, LANES))
    padded[:, :NX] = sx
    sent = forward_x(own, other, np_split(padded * (4.0 / orb)), ndev)
    got = lax.all_to_all(sent, both, 0, 0, tiled=True)
    sent = spectral(got, orb, vec)
    got = lax.all_to_all(sent, both, 0, 0, tiled=True)
    factor, *slots = back(got, np_split(padded), ndev, vec)
    gots = [slots[0]] + [shift(slots[s], "vec", s) for s in range(1, vec)]
    return assemble(gots), factor


def solution(mesh):
    orb, vec = mesh.shape["orb"], mesh.shape["vec"]
    placed = (P("orb", None, None), P("orb"), P("vec", "orb", None), P("orb", None))

    def body(orbitals, energies, trial_potential, local_potential):
        one = orbitals.shape[0] == 1 and trial_potential.shape[0] == 1
        plan = block_body if one and fits(orb, vec, orb, vec) else general_body
        return plan(orbitals, energies, trial_potential, local_potential)

    return jax.shard_map(
        body, mesh=mesh, in_specs=placed, out_specs=(P("vec", "orb", None), P()), check_vma=False
    )
```

```python
import functools
import math

import jax
import jax.numpy as jnp
import ml_dtypes
import numpy as np
from jax import lax
from jax.experimental import pallas as pl
from jax.experimental.pallas import tpu as pltpu
from jax.sharding import PartitionSpec as P

NZ = 96
NY = 96
NX = 96
STEPS = 4

BF16 = jnp.bfloat16
F32 = jnp.float32
LANES = 128
WEIGHTS = [1.0 / (1.0 + 0.8 * math.cos(math.pi * (2 * s + 1) / (2 * STEPS))) for s in range(STEPS)]

SCALES = [WEIGHTS[0]]
for weight_ in WEIGHTS[1:]:
    SCALES.append((1.0 - weight_) * SCALES[-1])
COEFFICIENTS = [None] + [
    (1.0, WEIGHTS[s] / SCALES[s], WEIGHTS[s] * SCALES[s - 1] / SCALES[s]) for s in range(1, STEPS)
]


def neighbours(field):
    depth, flat = field.shape
    zero_plane = jnp.zeros((1, flat), field.dtype)
    total = jnp.concatenate([zero_plane, field[:-1]], 0) + jnp.concatenate(
        [field[1:], zero_plane], 0
    )
    zero_rows = jnp.zeros((depth, NX), field.dtype)
    total = (
        total
        + jnp.concatenate([zero_rows, field[:, :-NX]], 1)
        + jnp.concatenate([field[:, NX:], zero_rows], 1)
    )
    column = jnp.arange(flat) % NX
    zero_col = jnp.zeros((depth, 1), field.dtype)
    left = jnp.concatenate([zero_col, field[:, :-1]], 1) * (column > 0).astype(field.dtype)
    right = jnp.concatenate([field[:, 1:], zero_col], 1) * (column < NX - 1).astype(field.dtype)
    return total + left + right


def solve(psi, perturb, potential, energy):
    diag = 3.25 + potential - energy
    source = -perturb * psi
    answer = jnp.zeros_like(psi)
    for step in range(STEPS):
        weight = 1.0 / (1.0 + 0.8 * jnp.cos(jnp.pi * (2 * step + 1) / (2 * STEPS)))
        applied = diag * answer - 0.5 * neighbours(answer)
        answer = answer + weight * (source - applied) / diag
    return answer


def sine_basis(count):
    index = jnp.arange(count, dtype=jnp.float32) + 1.0
    return jnp.sqrt(2.0 / (count + 1)) * jnp.sin(
        jnp.pi * index[:, None] * index[None, :] / (count + 1)
    )


def eigen_of(position, count):
    return 2.0 - 2.0 * jnp.cos(jnp.pi * (position.astype(jnp.float32) + 1.0) / (count + 1))


def planes(field):
    high = lax.Precision.HIGHEST
    depth = field.shape[0]
    cube = field.reshape(depth, NY, NX)
    cube = jnp.einsum("zyx,cx->zyc", cube, sine_basis(NX), precision=high)
    cube = jnp.einsum("zyc,by->zbc", cube, sine_basis(NY), precision=high)
    return cube.reshape(depth, NY * NX)


def scale_columns(columns, start):
    high = lax.Precision.HIGHEST
    width = columns.shape[1]
    position = start + jnp.arange(width)
    denom = (
        eigen_of(jnp.arange(NZ), NZ)[:, None]
        + eigen_of(position // NX, NY)[None, :]
        + eigen_of(position % NX, NX)[None, :]
    )
    basis = sine_basis(NZ)
    spectral = jnp.dot(basis, columns, precision=high) * (jnp.sqrt(4.0 * jnp.pi) / jnp.sqrt(denom))
    return jnp.dot(basis, spectral, precision=high)


def coulomb_slab(slab):
    columns = lax.all_to_all(planes(slab), "orb", split_axis=1, concat_axis=0, tiled=True)
    scaled = scale_columns(columns, lax.axis_index("orb") * columns.shape[1])
    back = lax.all_to_all(scaled, "orb", split_axis=0, concat_axis=1, tiled=True)
    return planes(back)


def factorize(partial_gram):
    lower = jnp.linalg.cholesky(partial_gram / (NZ * NY * NX))
    inverse = lax.linalg.triangular_solve(
        lower, jnp.eye(lower.shape[0], dtype=jnp.float32), left_side=True, lower=True
    )
    return (lower, inverse)


def general_body(orbitals, energies, trial_potential, local_potential):
    high = lax.Precision.HIGHEST
    depth = local_potential.shape[0]
    plane_cells = local_potential.shape[1]
    vector_slab = trial_potential.reshape(depth, plane_cells)
    perturb_full, potential_full = (
        lax.all_gather(vector_slab, "orb", axis=0, tiled=True),
        lax.all_gather(local_potential, "orb", axis=0, tiled=True),
    )
    perturb = perturb_full.astype(jnp.float32)
    potential = potential_full.astype(jnp.float32)
    weight = 4.0 / (orbitals.shape[0] * lax.axis_size("orb"))
    psi = orbitals[0].astype(jnp.float32)
    partial_value = psi * solve(psi, perturb, potential, energies[0])
    partial_value = partial_value * weight
    slab = lax.psum_scatter(partial_value, "orb", scatter_dimension=0, tiled=True)
    slab = coulomb_slab(slab)
    mine = slab.reshape(1, depth, plane_cells)
    gathered = lax.all_gather(mine, "vec", axis=0, tiled=True)
    flat = gathered.reshape(gathered.shape[0], depth * plane_cells)
    partial_gram = jnp.dot(flat, flat.T, precision=high)
    lower, inverse = factorize(lax.psum(partial_gram, "orb"))
    row = lax.dynamic_slice_in_dim(inverse, lax.axis_index("vec"), 1, 0)
    ortho = jnp.dot(row, flat, precision=high).reshape(1, depth, plane_cells)
    return (ortho, lower.T)


TILES = 3
GROUP = 4
SUB = 8
ROWS = GROUP * SUB
WTILES = TILES * SUB
HALO = STEPS - 1
TAILS = 4


def fits(orb, vec, norb, nv):
    return (
        norb == orb
        and nv == vec
        and orb % 2 == 0
        and NZ % orb == 0
        and NZ // orb >= 4
        and NZ // orb % 2 == 0
        and NY == vec * (ROWS - 2 * GROUP)
        and NY == TILES * ROWS
        and vec * ROWS == LANES
        and NX * GROUP == TILES * LANES
        and NX % (orb * vec) == 0
        and NZ % (orb * vec) == 0
        and STEPS <= GROUP
        and NZ // orb == TAILS * TILES
        and vec == GROUP
    )


def split(x):
    high = x.astype(BF16)
    return high, (x - high.astype(F32)).astype(BF16)


def np_split(x):
    x = np.asarray(x, np.float64)
    high = x.astype(ml_dtypes.bfloat16)
    return np.stack([high, (x - high.astype(np.float64)).astype(ml_dtypes.bfloat16)])


def dot3(a, b, dims):
    one = functools.partial(
        lax.dot_general, dimension_numbers=(dims, ((), ())), preferred_element_type=F32
    )
    return one(a[0], b[0]) + (one(a[0], b[1]) + one(a[1], b[0]))


def np_basis(count):
    index = np.arange(count, dtype=np.float64) + 1.0
    return np.sqrt(2.0 / (count + 1)) * np.sin(np.pi * np.outer(index, index) / (count + 1))


def np_eigen(count):
    return 4.0 * np.sin(np.pi * (np.arange(count, dtype=np.float64) + 1.0) / (2 * (count + 1))) ** 2


def to_rows(tiles):
    lane = lax.broadcasted_iota(jnp.int32, tiles[0].shape, 1)
    a, b, c = tiles
    return [
        a,
        pltpu.roll(jnp.where(lane >= 96, a, b), 32, 1),
        pltpu.roll(jnp.where(lane >= 64, b, c), 64, 1),
        pltpu.roll(c, 96, 1),
    ]


def to_tiles(rows):
    lane = lax.broadcasted_iota(jnp.int32, rows[0].shape, 1)
    r1, r2 = pltpu.roll(rows[1], 96, 1), pltpu.roll(rows[2], 64, 1)
    return [
        jnp.where(lane < 96, rows[0], r1),
        jnp.where(lane < 64, r1, r2),
        jnp.where(lane < 32, r2, pltpu.roll(rows[3], 32, 1)),
    ]


def first_tile(strip):
    return strip * (WTILES - 2 * TILES) - TILES


def window_start(strip):
    return jnp.clip(first_tile(strip), 0, NY * NX // LANES - WTILES)


def tile_lanes(strip, t, start=0):
    tile = jnp.clip(first_tile(strip) + t, 0, NY * NX // LANES - 1) - start
    return pl.ds(pl.multiple_of(tile * LANES, LANES), LANES)


def pack_planes(src, plane, out, pairs):
    def one(pair, carry):
        for i in range(TILES):
            top = pl.multiple_of((plane + 2 * pair) * WTILES + i * SUB, SUB)
            low = pl.multiple_of((plane + 2 * pair + 1) * WTILES + i * SUB, SUB)
            block = jnp.concatenate([src[pl.ds(top, SUB), :], src[pl.ds(low, SUB), :]], 0)
            out[pair, i] = block.astype(BF16)
        return carry

    lax.fori_loop(0, pairs, one, 0)


def windows_kernel(orb, vec, energy_ref, psi_any, v_any, pot_any, *refs):
    outs, (planes_ref, more_ref, psi_ref, v_ref, pot_ref, sem) = refs[:-6], refs[-6:]
    chips = orb // 2
    slab = NZ // chips
    depth = v_ref.shape[0]
    chip = lax.axis_index("orb") // 2
    strip = lax.axis_index("vec")
    start = window_start(strip)
    lanes = pl.ds(pl.multiple_of(start * LANES, LANES), WTILES * LANES)
    copies = [
        pltpu.make_async_copy(v_any.at[0], v_ref, sem.at[0]),
        pltpu.make_async_copy(pot_any.at[:, lanes], pot_ref, sem.at[1]),
        pltpu.make_async_copy(psi_any.at[0, :, lanes], psi_ref, sem.at[2]),
    ]
    for copy in copies:
        copy.start()
    for copy in copies:
        copy.wait()
    for n in range(vec + 1):
        for t in range(WTILES):
            row = (n * depth) * WTILES + (t % TILES) * SUB + t // TILES
            if n < vec:
                tile = v_ref[:, tile_lanes(lax.rem(strip + n, vec), t)]
            else:
                tile = pot_ref[:, tile_lanes(strip, t, start)]
            more_ref[pl.ds(row, depth, WTILES), :] = tile.astype(F32)
        pack_planes(more_ref, n * depth, outs[chips + n], depth // 2)
    zero = jnp.zeros((HALO * WTILES, LANES), F32)
    planes_ref[: HALO * WTILES, :] = zero
    planes_ref[(NZ + HALO) * WTILES :, :] = zero
    for t in range(WTILES):
        row = HALO * WTILES + (t % TILES) * SUB + t // TILES
        planes_ref[pl.ds(row, NZ, WTILES), :] = psi_ref[:, tile_lanes(strip, t, start)].astype(F32)
    energy = jnp.full((1, LANES), energy_ref[0], F32)
    high = energy.astype(BF16).astype(F32)
    middle = (energy - high).astype(BF16).astype(F32)
    low = energy - high - middle
    lane = lax.broadcasted_iota(jnp.int32, (1, LANES), 1)
    for at in range(chips):
        row = at * slab * WTILES
        held = planes_ref[row : row + 1, :]
        held = jnp.where(lane == 0, high, jnp.where(lane == 1, middle, jnp.where(lane == 2, low, held)))
        planes_ref[row : row + 1, :] = held
    for shift in range(chips):
        pack_planes(planes_ref, ((chip + shift) % chips) * slab, outs[shift], (slab + 2 * HALO) // 2)


def windows(orbitals, energies, trial, potential, orb, vec):
    chips = orb // 2
    depth = potential.shape[0]
    block = (TILES, 2 * SUB, LANES)
    pairs = (NZ // chips + 2 * HALO) // 2
    outs = [jax.ShapeDtypeStruct((pairs, *block), BF16)] * chips
    outs += [jax.ShapeDtypeStruct((depth // 2, *block), BF16)] * (vec + 1)
    got = pl.pallas_call(
        functools.partial(windows_kernel, orb, vec),
        out_shape=outs,
        in_specs=[pl.BlockSpec(memory_space=pltpu.SMEM)] + [pl.BlockSpec(memory_space=pltpu.HBM)] * 3,
        out_specs=[pl.BlockSpec(memory_space=pltpu.VMEM)] * len(outs),
        scratch_shapes=[
            pltpu.VMEM(((NZ + 2 * HALO) * WTILES, LANES), F32),
            pltpu.VMEM(((vec + 1) * depth * WTILES, LANES), F32),
            pltpu.VMEM((NZ, WTILES * LANES), BF16),
            pltpu.VMEM((depth, NY * NX), BF16),
            pltpu.VMEM((depth, WTILES * LANES), BF16),
            pltpu.SemaphoreType.DMA((3,)),
        ],
        compiler_params=pltpu.CompilerParams(vmem_limit_bytes=24 << 20),
        name="windows",
    )(energies, *(pltpu.with_memory_space_constraint(x, pltpu.HBM) for x in (orbitals, trial, potential)))
    return list(got[:chips]), list(got[chips:])


def edges_kernel(n, parts_and_more, *refs):
    parts, (own_ref, edge_ref) = refs[:n], refs[parts_and_more:]
    core = lax.axis_index("orb") % 2
    first = core * (own_ref.shape[1] - edge_ref.shape[1])
    for i, part in enumerate(parts):
        own_ref[i] = part[...]
        edge_ref[i] = part[pl.ds(first, edge_ref.shape[1])]


def edges(parts, arrived):
    pairs, *block = parts[0].shape
    n = len(parts)
    more = n + len(arrived)
    return pl.pallas_call(
        functools.partial(edges_kernel, n, more),
        out_shape=[
            jax.ShapeDtypeStruct((n, pairs, *block), BF16),
            jax.ShapeDtypeStruct((n, GROUP // 2, *block), BF16),
        ],
        in_specs=[pl.BlockSpec(memory_space=pltpu.VMEM)] * more,
        out_specs=[pl.BlockSpec(memory_space=pltpu.VMEM)] * 2,
        compiler_params=pltpu.CompilerParams(vmem_limit_bytes=24 << 20),
        name="edges",
    )(*parts, *arrived)


def with_edge_kernel(n, own_ref, edge_ref, *refs):
    out_ref = refs[n]
    core = lax.axis_index("orb") % 2
    pairs, edge = own_ref.shape[1], edge_ref.shape[1]
    out_ref[:, pl.ds((1 - core) * edge, pairs)] = own_ref[...]
    out_ref[:, pl.ds(core * pairs, edge)] = edge_ref[...]


def with_edge(own, edge, arrived):
    n, pairs, *block = own.shape
    return pl.pallas_call(
        functools.partial(with_edge_kernel, len(arrived)),
        out_shape=jax.ShapeDtypeStruct((n, pairs + edge.shape[1], *block), own.dtype),
        in_specs=[pl.BlockSpec(memory_space=pltpu.VMEM)] * (2 + len(arrived)),
        out_specs=pl.BlockSpec(memory_space=pltpu.VMEM),
        compiler_params=pltpu.CompilerParams(vmem_limit_bytes=24 << 20),
        name="with_edge",
    )(own, edge, *arrived)


def potential_rows_kernel(vec, n, mine_ref, other_ref, *refs):
    v_ref, d_ref = refs[n:]
    core = lax.axis_index("orb") % 2
    strip = lax.axis_index("vec")
    pairs = mine_ref.shape[1]
    for src, first in ((mine_ref, core * pairs), (other_ref, (1 - core) * pairs)):

        def one(pair, carry, src=src, first=first):
            plane = 2 * (first + pair)
            for n in range(vec + 1):
                rows = to_rows([src[n, pair, i].astype(F32) for i in range(TILES)])
                for zz in range(2):
                    block = jnp.concatenate([rows[i][zz * SUB : (zz + 1) * SUB] for i in range(GROUP)], 0)
                    if n < vec:
                        k = lax.rem(strip - n + vec, vec)
                        v_ref[plane + zz, pl.ds(pl.multiple_of(k * ROWS, ROWS), ROWS), :] = block
                    else:
                        d_ref[plane + zz] = 3.25 + block
            return carry

        lax.fori_loop(0, pairs, one, 0, unroll=True)


def potential_rows(mine, other, vec, arrived):
    planes = 4 * mine.shape[1]
    return pl.pallas_call(
        functools.partial(potential_rows_kernel, vec, len(arrived)),
        out_shape=[
            jax.ShapeDtypeStruct((planes, vec * ROWS, LANES), F32),
            jax.ShapeDtypeStruct((planes, ROWS, LANES), F32),
        ],
        in_specs=[pl.BlockSpec(memory_space=pltpu.VMEM)] * (2 + len(arrived)),
        out_specs=[pl.BlockSpec(memory_space=pltpu.VMEM)] * 2,
        compiler_params=pltpu.CompilerParams(vmem_limit_bytes=24 << 20),
        name="potential_rows",
    )(mine, other, *arrived)


def solve_kernel(vec, first, part, *refs):
    psi_ref, v_ref, d_ref = refs[:3]
    refs = refs[3:]
    sum_ref = None if first else refs[0]
    out_ref, psi_s, h_s, c_s, u_a, u_b = refs[-6:]
    planes = d_ref.shape[0]
    depth = (planes - 2 * GROUP) // 2
    core = lax.axis_index("orb") % 2
    begins = {None: 0, "own": core * depth, "other": (1 - core) * depth}[part]
    count = 2 * depth if part is None else depth
    top = (lax.axis_index("orb") // 2) * 2 * depth - GROUP
    top_row = lax.axis_index("vec") * (ROWS - 2 * GROUP) - GROUP
    lane = lax.broadcasted_iota(jnp.int32, (SUB, LANES), 1)
    group = lax.broadcasted_iota(jnp.int32, (SUB, LANES), 0)
    inside = []
    for i in range(GROUP):
        y = top_row + group * GROUP + i
        inside.append(jnp.where((y >= 0) & (y < NY) & (lane < NX), 0.5, 0.0))
    inside = jnp.concatenate(inside, 0)
    block = psi_ref[0, 0].astype(F32)
    energy = block[0:1, 0:1] + block[0:1, 1:2] + block[0:1, 2:3]
    at = lax.broadcasted_iota(jnp.int32, (2 * LANES, LANES), 0) % LANES
    to = lax.broadcasted_iota(jnp.int32, (2 * LANES, LANES), 1)
    beside = jnp.where((at == to - 1) | (at == to + 1), 1.0, 0.0).astype(BF16)

    def begin(pair, carry):
        rows = to_rows([psi_ref[begins // 2 + pair, i].astype(F32) for i in range(TILES)])
        for zz in range(2):
            w = GROUP - HALO + begins + 2 * pair + zz
            z = top + w
            there = jnp.where((z >= 0) & (z < NZ), 1.0, 0.0)
            psi = jnp.concatenate([rows[i][zz * SUB : (zz + 1) * SUB] for i in range(GROUP)], 0)
            h = inside * there / (d_ref[w] - energy)
            psi_s[w] = SCALES[STEPS - 1] * psi
            h_s[w] = h
            scaled = -2.0 * psi * h
            for k in range(vec):
                rows_k = pl.ds(k * ROWS, ROWS)
                c_s[w, rows_k, :] = scaled * v_ref[w, rows_k, :]
        return carry

    lax.fori_loop(0, (count + 2 * HALO) // 2, begin, 0, unroll=3)

    def stepped(src, w, step):
        u = src[w]
        high, low = split(u)
        x = jnp.dot(jnp.concatenate([high, low], 1), beside, preferred_element_type=F32)
        near = x + (src[w - 1] + src[w + 1])
        own, given, around = COEFFICIENTS[step]
        h = around * h_s[w]
        new = []
        for k in range(vec):
            rows = [u[k * ROWS + i * SUB : k * ROWS + (i + 1) * SUB] for i in range(GROUP)]
            north = jnp.concatenate([pltpu.roll(rows[-1], 1, 0)] + rows[:-1], 0)
            south = jnp.concatenate(rows[1:] + [pltpu.roll(rows[0], SUB - 1, 0)], 0)
            at_k = slice(k * ROWS, (k + 1) * ROWS)
            change = h * (near[at_k] + (north + south))
            if src is c_s:
                new.append((own + given) * u[at_k] + change)
            else:
                new.append((u[at_k] + given * c_s[w, at_k, :]) + change)
        return new

    src, dst = c_s, u_a
    for step in range(1, STEPS - 1):
        low = GROUP - HALO + step

        def middle(p, carry, src=src, dst=dst, step=step, low=low):
            w = begins + low + p
            dst[w] = jnp.concatenate(stepped(src, w, step), 0)
            return carry

        lax.fori_loop(0, count + 2 * (HALO - step), middle, 0, unroll=True)
        src, dst = dst, (u_b if dst is u_a else u_a)

    def end(p, carry, src=src):
        w = GROUP + begins + p
        psi = psi_s[w]
        total = jnp.concatenate([psi * new for new in stepped(src, w, STEPS - 1)], 0)
        if not first:
            total = total + sum_ref[begins + p]
        out_ref[p] = total
        return carry

    lax.fori_loop(0, count, end, 0, unroll=True)


def solve_window(psi, v, d, total, vec, part=None):
    planes = d.shape[0]
    depth = (planes - 2 * GROUP) // 2
    args = (psi, v, d) if total is None else (psi, v, d, total)
    return pl.pallas_call(
        functools.partial(solve_kernel, vec, total is None, part),
        out_shape=jax.ShapeDtypeStruct((2 * depth if part is None else depth, LANES, LANES), F32),
        in_specs=[pl.BlockSpec(memory_space=pltpu.VMEM)] * len(args),
        out_specs=pl.BlockSpec(memory_space=pltpu.VMEM),
        scratch_shapes=[pltpu.VMEM((planes, ROWS, LANES), F32)] * 2
        + [pltpu.VMEM((planes, vec * ROWS, LANES), F32)] * 3,
        compiler_params=pltpu.CompilerParams(vmem_limit_bytes=32 << 20),
        name="solve_window",
    )(*args)


def forward_x_kernel(ndev, basis_ref, own_ref, other_ref, out_ref):
    depth = own_ref.shape[0] // LANES
    inner = depth - depth // TAILS
    rows = out_ref.shape[0] // ndev
    vecrows = LANES // SUB
    basis = (basis_ref[0], basis_ref[1])
    lane = lax.broadcasted_iota(jnp.int32, (NX, LANES), 1)
    pad = jnp.zeros((LANES - (SUB - 2) * vecrows, LANES), F32)
    got = []
    for z in range(depth):
        groups = [pl.ds(z * LANES + g, vecrows, SUB) for g in range(1, SUB - 1)]
        chi = jnp.concatenate([own_ref[g, :] + other_ref[g, :] for g in groups] + [pad], 0)
        got.append(dot3(basis, split(chi), ((1,), (1,))))
    for z in range(inner):
        whole, third = inner + z // TILES, z % TILES
        tail = pltpu.roll(got[whole], LANES - LANES // TAILS * (third + 1), 1)
        row = jnp.where(lane < LANES - LANES // TAILS, got[z], tail)
        for part in range(NX // ndev):
            out_ref[pl.ds(part * inner + z, ndev, rows), :] = row[part * ndev : (part + 1) * ndev]
    for row in range(NX // ndev * inner, rows):
        out_ref[pl.ds(row, ndev, rows), :] = jnp.zeros((ndev, LANES), F32)


def forward_x(own, other, basis, ndev):
    depth = own.shape[0]
    rows = -(-(NX // ndev) * (depth - depth // TAILS) // 8) * 8
    out = pl.pallas_call(
        functools.partial(forward_x_kernel, ndev),
        out_shape=jax.ShapeDtypeStruct((ndev * rows, LANES), F32),
        in_specs=[pl.BlockSpec(memory_space=pltpu.VMEM)] * 3,
        out_specs=pl.BlockSpec(memory_space=pltpu.VMEM),
        compiler_params=pltpu.CompilerParams(vmem_limit_bytes=24 << 20),
        name="forward_x",
    )(basis, own.reshape(-1, LANES), other.reshape(-1, LANES))
    return out.reshape(ndev, rows, LANES)


def spectral_kernel(orb, vec, rows, mux_ref, muzy_ref, wy_ref, kz_ref, kzb_ref, wyb_ref, got_ref, out_ref, tail_ref):
    ndev = orb * vec
    parts = NX // ndev
    me = lax.axis_index("orb") * vec + lax.axis_index("vec")
    quarter = NZ // orb // TAILS
    tails = tail_ref.shape[0] // orb
    tail_ref[...] = jnp.zeros_like(tail_ref)
    lane = lax.broadcasted_iota(jnp.int32, (parts * quarter, LANES), 1)
    for o in range(orb):
        for v in range(vec):
            third = [got_ref[pl.ds((o * vec + v) * rows + p, parts * quarter, TILES), :] for p in range(TILES)]
            tail = pltpu.roll(third[0], LANES // TAILS, 1)
            for p in range(1, TILES):
                tail = jnp.where(lane >= p * LANES // TAILS, pltpu.roll(third[p], (p + 1) * LANES // TAILS, 1), tail)
            tail_ref[o * tails : o * tails + parts * quarter, v * LANES : (v + 1) * LANES] = tail
    x = jnp.concatenate(
        [
            jnp.concatenate([got_ref[(o * vec + v) * rows : (o * vec + v + 1) * rows] for o in range(orb)], 0)
            for v in range(vec)
        ],
        1,
    )
    mm = ((1,), (0,))
    t = dot3(split(jnp.concatenate([x, tail_ref[...]], 0)), (wy_ref[0], wy_ref[1]), mm)
    t = dot3((kz_ref[0], kz_ref[1]), split(t), mm)
    scale = jnp.concatenate(
        [
            math.sqrt(4.0 * math.pi) / jnp.sqrt(muzy_ref[...] + mux_ref[part * ndev + me])
            for part in range(parts)
        ],
        0,
    )
    fields = [t[:, k * LANES : (k + 1) * LANES] * scale for k in range(vec)]
    lane = lax.broadcasted_iota(jnp.int32, (1, LANES), 1)
    gram = jnp.zeros((1, LANES), F32)
    for k in range(vec):
        for l in range(k + 1):
            entry = jnp.sum(jnp.sum(fields[k] * fields[l], axis=0, keepdims=True), axis=1, keepdims=True)
            gram = jnp.where(lane == k * vec + l, entry, gram)
    t = jnp.concatenate(fields, 1)
    t = jnp.concatenate(
        [dot3((kzb_ref[0], kzb_ref[1]), split(t[part * NZ : (part + 1) * NZ]), mm) for part in range(parts)], 0
    )
    t = dot3(split(t), (wyb_ref[0], wyb_ref[1]), mm)
    rows = out_ref.shape[0] // ndev
    zs = NZ // ndev
    for part in range(parts):
        for z in range(zs):
            for yt in range(TILES):
                out_ref[pl.ds((z * parts + part) * TILES + yt, ndev, rows), :] = t[
                    (part * zs + z) * ndev : (part * zs + z + 1) * ndev, yt * LANES : (yt + 1) * LANES
                ]
    out_ref[pl.ds(zs * parts * TILES, ndev, rows), :] = jnp.broadcast_to(gram, (ndev, LANES))


def spectral(got, orb, vec):
    ndev = orb * vec
    parts, zs = NX // ndev, NZ // ndev
    depth = NZ // orb
    quarter = depth // TAILS
    inner = depth - quarter
    strip = ROWS - 2 * GROUP
    rows_in = got.shape[1]
    tails = -(-parts * quarter // 8) * 8
    rows_out = -(-(parts * zs * TILES + 1) // 8) * 8
    sy, sz = np_basis(NY), np_basis(NZ)
    wy = np.zeros((vec, LANES, vec, LANES))
    wyb = np.zeros((vec, LANES, TILES, vec, GROUP, SUB))
    for k in range(vec):
        for i in range(GROUP):
            for g in range(SUB):
                for v in range(vec):
                    if g < SUB - 2:
                        wy[v, (g * vec + k) * GROUP + i, k, :NY] = sy[v * strip + GROUP * g + i]
                for yt in range(TILES):
                    wyb[k, :NY, yt, k, i, g] = sy[yt * ROWS + GROUP * g + i]
    wy = wy.reshape(vec * LANES, vec * LANES)
    wyb = wyb.reshape(vec * LANES, TILES * LANES)
    kz = np.zeros((parts, NZ, orb, rows_in))
    kzt = np.zeros((parts, NZ, orb, tails))
    for part in range(parts):
        for o in range(orb):
            mine = sz[:, o * depth : (o + 1) * depth]
            kz[part, :, o, part * inner : (part + 1) * inner] = mine[:, :inner]
            kzt[part, :, o, part * quarter : (part + 1) * quarter] = mine[:, inner:]
    kz = np.concatenate([kz.reshape(parts * NZ, -1), kzt.reshape(parts * NZ, -1)], 1)
    kzb = np.concatenate([sz[z::zs] for z in range(zs)])
    muzy = np.ones((NZ, LANES), np.float32)
    muzy[:, :NY] = np_eigen(NZ)[:, None] + np_eigen(NY)[None, :]
    mux = np_eigen(NX).astype(np.float32)
    out = pl.pallas_call(
        functools.partial(spectral_kernel, orb, vec, rows_in),
        out_shape=jax.ShapeDtypeStruct((ndev * rows_out, LANES), F32),
        in_specs=[pl.BlockSpec(memory_space=pltpu.SMEM)] + [pl.BlockSpec(memory_space=pltpu.VMEM)] * 6,
        out_specs=pl.BlockSpec(memory_space=pltpu.VMEM),
        scratch_shapes=[pltpu.VMEM((orb * tails, vec * LANES), F32)],
        compiler_params=pltpu.CompilerParams(vmem_limit_bytes=32 << 20),
        name="spectral",
    )(mux, muzy, np_split(wy), np_split(kz), np_split(kzb), np_split(wyb), got.reshape(-1, LANES))
    return out.reshape(ndev, rows_out, LANES)


def back_kernel(ndev, vec, basis_ref, got_ref, factor_ref, *outs):
    parts, zs = NX // ndev, NZ // ndev
    rows = got_ref.shape[0] // ndev
    strip = lax.axis_index("vec")
    basis = (basis_ref[0], basis_ref[1])
    gram = jnp.sum(got_ref[pl.ds(zs * parts * TILES, ndev, rows), :], axis=0, keepdims=True)
    gram = gram / (NZ * NY * NX)
    entry = lambda k, l: gram[:, k * vec + l : k * vec + l + 1]
    lower = [[None] * vec for _ in range(vec)]
    inverse = [[jnp.zeros((1, 1), F32)] * vec for _ in range(vec)]
    for l in range(vec):
        pivot = entry(l, l)
        for m in range(l):
            pivot = pivot - lower[l][m] * lower[l][m]
        lower[l][l] = jnp.sqrt(pivot)
        inverse[l][l] = 1.0 / lower[l][l]
        for k in range(l + 1, vec):
            value = entry(k, l)
            for m in range(l):
                value = value - lower[k][m] * lower[l][m]
            lower[k][l] = value * inverse[l][l]
    for l in range(vec):
        for k in range(l + 1, vec):
            value = lower[k][l] * inverse[l][l]
            for m in range(l + 1, k):
                value = value + lower[k][m] * inverse[m][l]
            inverse[k][l] = -value * inverse[k][k]
    at_row = lax.broadcasted_iota(jnp.int32, (vec, vec), 0)
    at_col = lax.broadcasted_iota(jnp.int32, (vec, vec), 1)
    factor = jnp.zeros((vec, vec), F32)
    for k in range(vec):
        for l in range(k + 1):
            factor = jnp.where((at_row == l) & (at_col == k), lower[k][l], factor)
    factor_ref[...] = factor
    coefficients = []
    for s in range(vec):
        to = lax.rem(strip + s, vec)
        line = []
        for k in range(vec):
            value = inverse[0][k]
            for m in range(1, vec):
                value = jnp.where(to == m, inverse[m][k], value)
            line.append(value)
        coefficients.append(line)
    for z in range(zs):
        for yt in range(TILES):
            x = jnp.concatenate(
                [
                    got_ref[pl.ds((z * parts + part) * TILES + yt, ndev, rows), :]
                    for part in range(parts)
                ],
                0,
            )
            y = dot3(split(x), basis, ((0,), (0,)))
            for s in range(vec):
                mixed = coefficients[s][0] * y[:ROWS]
                for k in range(1, vec):
                    mixed = mixed + coefficients[s][k] * y[k * ROWS : (k + 1) * ROWS]
                tiles = to_tiles([mixed[i * SUB : (i + 1) * SUB] for i in range(GROUP)])
                for i in range(TILES):
                    outs[s][pl.ds((z * TILES + yt) * WTILES + i, SUB, TILES), :] = tiles[i]


def back(got, basis, ndev, vec):
    zs = NZ // ndev
    tiles = NY * NX // LANES
    return pl.pallas_call(
        functools.partial(back_kernel, ndev, vec),
        out_shape=[jax.ShapeDtypeStruct((vec, vec), F32)]
        + [jax.ShapeDtypeStruct((zs * tiles, LANES), F32)] * vec,
        in_specs=[pl.BlockSpec(memory_space=pltpu.VMEM)] * 2,
        out_specs=[pl.BlockSpec(memory_space=pltpu.VMEM)] * (vec + 1),
        compiler_params=pltpu.CompilerParams(vmem_limit_bytes=24 << 20),
        name="back",
    )(basis, got.reshape(-1, LANES))


def assemble_kernel(vec, *refs):
    gots, out_ref = refs[:vec], refs[vec]
    line = lax.axis_index("vec")
    rows = gots[0].shape[0]
    for s in range(vec):
        start = pl.multiple_of(lax.rem(line - s + vec, vec) * rows, 8)
        out_ref[pl.ds(start, rows), :] = gots[s][...]


def assemble(gots):
    vec = len(gots)
    rows = gots[0].shape[0] * vec
    out = pl.pallas_call(
        functools.partial(assemble_kernel, vec),
        out_shape=jax.ShapeDtypeStruct((rows, LANES), F32),
        in_specs=[pl.BlockSpec(memory_space=pltpu.VMEM)] * vec,
        out_specs=pl.BlockSpec(memory_space=pltpu.VMEM),
        compiler_params=pltpu.CompilerParams(vmem_limit_bytes=24 << 20),
        name="assemble",
    )(*gots)
    return out.reshape(1, rows * LANES // (NY * NX), NY * NX)


def swap_cores(x, orb):
    return lax.ppermute(x, "orb", [(o, o ^ 1) for o in range(orb)])


def shift(x, axis, count):
    n = lax.axis_size(axis)
    return lax.ppermute(x, axis, [(i, (i + count) % n) for i in range(n)])


def responses(orbitals, energies, trial_potential, local_potential):
    orb, vec = lax.axis_size("orb"), lax.axis_size("vec")
    chips = orb // 2
    psis, parts = windows(orbitals, energies, trial_potential, local_potential, orb, vec)
    def to_chip(r):
        perm = [(2 * a + c, 2 * ((a + r) % chips) + c) for a in range(chips) for c in range(2)]
        return lax.ppermute(psis[r], "orb", perm)

    order = [1, chips - 1, *range(2, chips - 1)]
    for r in order:
        psis[r] = to_chip(r)
    for n in range(1, vec):
        parts[n] = shift(parts[n], "vec", n)
    arrived = [psis[r] for r in order]
    own, edge = edges(parts, [])
    near = [(o, o + 1) for o in range(1, orb - 1, 2)] + [(o + 1, o) for o in range(1, orb - 1, 2)]
    edge = lax.ppermute(edge, "orb", near + [(0, 0), (orb - 1, orb - 1)])
    mine = with_edge(own, edge, arrived[:2])
    v, d = potential_rows(mine, swap_cores(mine, orb), vec, [])
    total = None
    for r in [0] + order[:-1]:
        total = solve_window(psis[r], v, d, total, vec)
    last = psis[order[-1]]
    other = swap_cores(solve_window(last, v, d, total, vec, "other"), orb)
    return solve_window(last, v, d, total, vec, "own"), other


def block_body(orbitals, energies, trial_potential, local_potential):
    orb, vec = lax.axis_size("orb"), lax.axis_size("vec")
    ndev = orb * vec
    both = ("orb", "vec")
    own, other = responses(orbitals, energies, trial_potential, local_potential)
    sx = np_basis(NX)
    padded = np.zeros((NX, LANES))
    padded[:, :NX] = sx
    sent = forward_x(own, other, np_split(padded * (4.0 / orb)), ndev)
    got = lax.all_to_all(sent, both, 0, 0, tiled=True)
    sent = spectral(got, orb, vec)
    got = lax.all_to_all(sent, both, 0, 0, tiled=True)
    factor, *slots = back(got, np_split(padded), ndev, vec)
    gots = [slots[0]] + [shift(slots[s], "vec", s) for s in range(1, vec)]
    return assemble(gots), factor


def solution(mesh):
    orb, vec = mesh.shape["orb"], mesh.shape["vec"]
    placed = (P("orb", None, None), P("orb"), P("vec", "orb", None), P("orb", None))

    def body(orbitals, energies, trial_potential, local_potential):
        one = orbitals.shape[0] == 1 and trial_potential.shape[0] == 1
        plan = block_body if one and fits(orb, vec, orb, vec) else general_body
        return plan(orbitals, energies, trial_potential, local_potential)

    return jax.shard_map(
        body, mesh=mesh, in_specs=placed, out_specs=(P("vec", "orb", None), P()), check_vma=False
    )
```

```python
import functools
import math

import jax
import jax.numpy as jnp
import ml_dtypes
import numpy as np
from jax import lax
from jax.experimental import pallas as pl
from jax.experimental.pallas import tpu as pltpu
from jax.sharding import PartitionSpec as P

NZ = 96
NY = 96
NX = 96
STEPS = 4

BF16 = jnp.bfloat16
F32 = jnp.float32
LANES = 128
WEIGHTS = [1.0 / (1.0 + 0.8 * math.cos(math.pi * (2 * s + 1) / (2 * STEPS))) for s in range(STEPS)]

SCALES = [WEIGHTS[0]]
for weight_ in WEIGHTS[1:]:
    SCALES.append((1.0 - weight_) * SCALES[-1])
COEFFICIENTS = [None] + [
    (1.0, WEIGHTS[s] / SCALES[s], WEIGHTS[s] * SCALES[s - 1] / SCALES[s]) for s in range(1, STEPS)
]


def neighbours(field):
    depth, flat = field.shape
    zero_plane = jnp.zeros((1, flat), field.dtype)
    total = jnp.concatenate([zero_plane, field[:-1]], 0) + jnp.concatenate(
        [field[1:], zero_plane], 0
    )
    zero_rows = jnp.zeros((depth, NX), field.dtype)
    total = (
        total
        + jnp.concatenate([zero_rows, field[:, :-NX]], 1)
        + jnp.concatenate([field[:, NX:], zero_rows], 1)
    )
    column = jnp.arange(flat) % NX
    zero_col = jnp.zeros((depth, 1), field.dtype)
    left = jnp.concatenate([zero_col, field[:, :-1]], 1) * (column > 0).astype(field.dtype)
    right = jnp.concatenate([field[:, 1:], zero_col], 1) * (column < NX - 1).astype(field.dtype)
    return total + left + right


def solve(psi, perturb, potential, energy):
    diag = 3.25 + potential - energy
    source = -perturb * psi
    answer = jnp.zeros_like(psi)
    for step in range(STEPS):
        weight = 1.0 / (1.0 + 0.8 * jnp.cos(jnp.pi * (2 * step + 1) / (2 * STEPS)))
        applied = diag * answer - 0.5 * neighbours(answer)
        answer = answer + weight * (source - applied) / diag
    return answer


def sine_basis(count):
    index = jnp.arange(count, dtype=jnp.float32) + 1.0
    return jnp.sqrt(2.0 / (count + 1)) * jnp.sin(
        jnp.pi * index[:, None] * index[None, :] / (count + 1)
    )


def eigen_of(position, count):
    return 2.0 - 2.0 * jnp.cos(jnp.pi * (position.astype(jnp.float32) + 1.0) / (count + 1))


def planes(field):
    high = lax.Precision.HIGHEST
    depth = field.shape[0]
    cube = field.reshape(depth, NY, NX)
    cube = jnp.einsum("zyx,cx->zyc", cube, sine_basis(NX), precision=high)
    cube = jnp.einsum("zyc,by->zbc", cube, sine_basis(NY), precision=high)
    return cube.reshape(depth, NY * NX)


def scale_columns(columns, start):
    high = lax.Precision.HIGHEST
    width = columns.shape[1]
    position = start + jnp.arange(width)
    denom = (
        eigen_of(jnp.arange(NZ), NZ)[:, None]
        + eigen_of(position // NX, NY)[None, :]
        + eigen_of(position % NX, NX)[None, :]
    )
    basis = sine_basis(NZ)
    spectral = jnp.dot(basis, columns, precision=high) * (jnp.sqrt(4.0 * jnp.pi) / jnp.sqrt(denom))
    return jnp.dot(basis, spectral, precision=high)


def coulomb_slab(slab):
    columns = lax.all_to_all(planes(slab), "orb", split_axis=1, concat_axis=0, tiled=True)
    scaled = scale_columns(columns, lax.axis_index("orb") * columns.shape[1])
    back = lax.all_to_all(scaled, "orb", split_axis=0, concat_axis=1, tiled=True)
    return planes(back)


def factorize(partial_gram):
    lower = jnp.linalg.cholesky(partial_gram / (NZ * NY * NX))
    inverse = lax.linalg.triangular_solve(
        lower, jnp.eye(lower.shape[0], dtype=jnp.float32), left_side=True, lower=True
    )
    return (lower, inverse)


def general_body(orbitals, energies, trial_potential, local_potential):
    high = lax.Precision.HIGHEST
    depth = local_potential.shape[0]
    plane_cells = local_potential.shape[1]
    vector_slab = trial_potential.reshape(depth, plane_cells)
    perturb_full, potential_full = (
        lax.all_gather(vector_slab, "orb", axis=0, tiled=True),
        lax.all_gather(local_potential, "orb", axis=0, tiled=True),
    )
    perturb = perturb_full.astype(jnp.float32)
    potential = potential_full.astype(jnp.float32)
    weight = 4.0 / (orbitals.shape[0] * lax.axis_size("orb"))
    psi = orbitals[0].astype(jnp.float32)
    partial_value = psi * solve(psi, perturb, potential, energies[0])
    partial_value = partial_value * weight
    slab = lax.psum_scatter(partial_value, "orb", scatter_dimension=0, tiled=True)
    slab = coulomb_slab(slab)
    mine = slab.reshape(1, depth, plane_cells)
    gathered = lax.all_gather(mine, "vec", axis=0, tiled=True)
    flat = gathered.reshape(gathered.shape[0], depth * plane_cells)
    partial_gram = jnp.dot(flat, flat.T, precision=high)
    lower, inverse = factorize(lax.psum(partial_gram, "orb"))
    row = lax.dynamic_slice_in_dim(inverse, lax.axis_index("vec"), 1, 0)
    ortho = jnp.dot(row, flat, precision=high).reshape(1, depth, plane_cells)
    return (ortho, lower.T)


TILES = 3
GROUP = 4
SUB = 8
ROWS = GROUP * SUB
WTILES = TILES * SUB
HALO = STEPS - 1
TAILS = 4


def fits(orb, vec, norb, nv):
    return (
        norb == orb
        and nv == vec
        and orb % 2 == 0
        and NZ % orb == 0
        and NZ // orb >= 4
        and NZ // orb % 2 == 0
        and NY == vec * (ROWS - 2 * GROUP)
        and NY == TILES * ROWS
        and vec * ROWS == LANES
        and NX * GROUP == TILES * LANES
        and NX % (orb * vec) == 0
        and NZ % (orb * vec) == 0
        and STEPS <= GROUP
        and NZ // orb == TAILS * TILES
        and vec == GROUP
    )


def split(x):
    high = x.astype(BF16)
    return high, (x - high.astype(F32)).astype(BF16)


def np_split(x):
    x = np.asarray(x, np.float64)
    high = x.astype(ml_dtypes.bfloat16)
    return np.stack([high, (x - high.astype(np.float64)).astype(ml_dtypes.bfloat16)])


def dot3(a, b, dims):
    one = functools.partial(
        lax.dot_general, dimension_numbers=(dims, ((), ())), preferred_element_type=F32
    )
    return one(a[0], b[0]) + (one(a[0], b[1]) + one(a[1], b[0]))


def np_basis(count):
    index = np.arange(count, dtype=np.float64) + 1.0
    return np.sqrt(2.0 / (count + 1)) * np.sin(np.pi * np.outer(index, index) / (count + 1))


def np_eigen(count):
    return 4.0 * np.sin(np.pi * (np.arange(count, dtype=np.float64) + 1.0) / (2 * (count + 1))) ** 2


def to_rows(tiles):
    lane = lax.broadcasted_iota(jnp.int32, tiles[0].shape, 1)
    a, b, c = tiles
    return [
        a,
        pltpu.roll(jnp.where(lane >= 96, a, b), 32, 1),
        pltpu.roll(jnp.where(lane >= 64, b, c), 64, 1),
        pltpu.roll(c, 96, 1),
    ]


def to_tiles(rows):
    lane = lax.broadcasted_iota(jnp.int32, rows[0].shape, 1)
    r1, r2 = pltpu.roll(rows[1], 96, 1), pltpu.roll(rows[2], 64, 1)
    return [
        jnp.where(lane < 96, rows[0], r1),
        jnp.where(lane < 64, r1, r2),
        jnp.where(lane < 32, r2, pltpu.roll(rows[3], 32, 1)),
    ]


def first_tile(strip):
    return strip * (WTILES - 2 * TILES) - TILES


def window_start(strip):
    return jnp.clip(first_tile(strip), 0, NY * NX // LANES - WTILES)


def tile_lanes(strip, t, start=0):
    tile = jnp.clip(first_tile(strip) + t, 0, NY * NX // LANES - 1) - start
    return pl.ds(pl.multiple_of(tile * LANES, LANES), LANES)


def pack_planes(src, plane, out, pairs):
    def one(pair, carry):
        for i in range(TILES):
            top = pl.multiple_of((plane + 2 * pair) * WTILES + i * SUB, SUB)
            low = pl.multiple_of((plane + 2 * pair + 1) * WTILES + i * SUB, SUB)
            block = jnp.concatenate([src[pl.ds(top, SUB), :], src[pl.ds(low, SUB), :]], 0)
            out[pair, i] = block.astype(BF16)
        return carry

    lax.fori_loop(0, pairs, one, 0)


def windows_kernel(orb, vec, energy_any, psi_any, v_any, pot_any, *refs):
    outs, (planes_ref, more_ref, psi_ref, v_ref, pot_ref, energy_ref, sem) = refs[:-7], refs[-7:]
    chips = orb // 2
    slab = NZ // chips
    depth = v_ref.shape[0]
    chip = lax.axis_index("orb") // 2
    strip = lax.axis_index("vec")
    start = window_start(strip)
    lanes = pl.ds(pl.multiple_of(start * LANES, LANES), WTILES * LANES)
    copies = [
        pltpu.make_async_copy(v_any.at[0], v_ref, sem.at[0]),
        pltpu.make_async_copy(pot_any.at[:, lanes], pot_ref, sem.at[1]),
        pltpu.make_async_copy(psi_any.at[0, :, lanes], psi_ref, sem.at[2]),
        pltpu.make_async_copy(energy_any, energy_ref, sem.at[3]),
    ]
    for copy in copies:
        copy.start()
    for copy in copies[:2]:
        copy.wait()
    for n in range(vec + 1):
        for t in range(WTILES):
            row = (n * depth) * WTILES + (t % TILES) * SUB + t // TILES
            if n < vec:
                tile = v_ref[:, tile_lanes(lax.rem(strip + n, vec), t)]
            else:
                tile = pot_ref[:, tile_lanes(strip, t, start)]
            more_ref[pl.ds(row, depth, WTILES), :] = tile.astype(F32)
        pack_planes(more_ref, n * depth, outs[chips + n], depth // 2)
    zero = jnp.zeros((HALO * WTILES, LANES), F32)
    planes_ref[: HALO * WTILES, :] = zero
    planes_ref[(NZ + HALO) * WTILES :, :] = zero
    for copy in copies[2:]:
        copy.wait()
    for t in range(WTILES):
        row = HALO * WTILES + (t % TILES) * SUB + t // TILES
        planes_ref[pl.ds(row, NZ, WTILES), :] = psi_ref[:, tile_lanes(strip, t, start)].astype(F32)
    energy = jnp.full((1, LANES), energy_ref[0], F32)
    high = energy.astype(BF16).astype(F32)
    middle = (energy - high).astype(BF16).astype(F32)
    low = energy - high - middle
    lane = lax.broadcasted_iota(jnp.int32, (1, LANES), 1)
    for at in range(chips):
        row = at * slab * WTILES
        held = planes_ref[row : row + 1, :]
        held = jnp.where(lane == 0, high, jnp.where(lane == 1, middle, jnp.where(lane == 2, low, held)))
        planes_ref[row : row + 1, :] = held
    for shift in range(chips):
        pack_planes(planes_ref, ((chip + shift) % chips) * slab, outs[shift], (slab + 2 * HALO) // 2)


def windows(orbitals, energies, trial, potential, orb, vec):
    chips = orb // 2
    depth = potential.shape[0]
    block = (TILES, 2 * SUB, LANES)
    pairs = (NZ // chips + 2 * HALO) // 2
    outs = [jax.ShapeDtypeStruct((pairs, *block), BF16)] * chips
    outs += [jax.ShapeDtypeStruct((depth // 2, *block), BF16)] * (vec + 1)
    got = pl.pallas_call(
        functools.partial(windows_kernel, orb, vec),
        out_shape=outs,
        in_specs=[pl.BlockSpec(memory_space=pl.ANY)] + [pl.BlockSpec(memory_space=pltpu.HBM)] * 3,
        out_specs=[pl.BlockSpec(memory_space=pltpu.VMEM)] * len(outs),
        scratch_shapes=[
            pltpu.VMEM(((NZ + 2 * HALO) * WTILES, LANES), F32),
            pltpu.VMEM(((vec + 1) * depth * WTILES, LANES), F32),
            pltpu.VMEM((NZ, WTILES * LANES), BF16),
            pltpu.VMEM((depth, NY * NX), BF16),
            pltpu.VMEM((depth, WTILES * LANES), BF16),
            pltpu.SMEM((1,), F32),
            pltpu.SemaphoreType.DMA((4,)),
        ],
        compiler_params=pltpu.CompilerParams(vmem_limit_bytes=24 << 20),
        name="windows",
    )(energies, *(pltpu.with_memory_space_constraint(x, pltpu.HBM) for x in (orbitals, trial, potential)))
    return list(got[:chips]), list(got[chips:])


def edges_kernel(n, parts_and_more, *refs):
    parts, (own_ref, edge_ref) = refs[:n], refs[parts_and_more:]
    core = lax.axis_index("orb") % 2
    first = core * (own_ref.shape[1] - edge_ref.shape[1])
    for i, part in enumerate(parts):
        own_ref[i] = part[...]
        edge_ref[i] = part[pl.ds(first, edge_ref.shape[1])]


def edges(parts, arrived):
    pairs, *block = parts[0].shape
    n = len(parts)
    more = n + len(arrived)
    return pl.pallas_call(
        functools.partial(edges_kernel, n, more),
        out_shape=[
            jax.ShapeDtypeStruct((n, pairs, *block), BF16),
            jax.ShapeDtypeStruct((n, GROUP // 2, *block), BF16),
        ],
        in_specs=[pl.BlockSpec(memory_space=pltpu.VMEM)] * more,
        out_specs=[pl.BlockSpec(memory_space=pltpu.VMEM)] * 2,
        compiler_params=pltpu.CompilerParams(vmem_limit_bytes=24 << 20),
        name="edges",
    )(*parts, *arrived)


def with_edge_kernel(n, own_ref, edge_ref, *refs):
    out_ref = refs[n]
    core = lax.axis_index("orb") % 2
    pairs, edge = own_ref.shape[1], edge_ref.shape[1]
    out_ref[:, pl.ds((1 - core) * edge, pairs)] = own_ref[...]
    out_ref[:, pl.ds(core * pairs, edge)] = edge_ref[...]


def with_edge(own, edge, arrived):
    n, pairs, *block = own.shape
    return pl.pallas_call(
        functools.partial(with_edge_kernel, len(arrived)),
        out_shape=jax.ShapeDtypeStruct((n, pairs + edge.shape[1], *block), own.dtype),
        in_specs=[pl.BlockSpec(memory_space=pltpu.VMEM)] * (2 + len(arrived)),
        out_specs=pl.BlockSpec(memory_space=pltpu.VMEM),
        compiler_params=pltpu.CompilerParams(vmem_limit_bytes=24 << 20),
        name="with_edge",
    )(own, edge, *arrived)


def potential_rows_kernel(vec, n, mine_ref, other_ref, *refs):
    v_ref, d_ref = refs[n:]
    core = lax.axis_index("orb") % 2
    strip = lax.axis_index("vec")
    pairs = mine_ref.shape[1]
    for src, first in ((mine_ref, core * pairs), (other_ref, (1 - core) * pairs)):

        def one(pair, carry, src=src, first=first):
            plane = 2 * (first + pair)
            for n in range(vec + 1):
                rows = to_rows([src[n, pair, i].astype(F32) for i in range(TILES)])
                for zz in range(2):
                    block = jnp.concatenate([rows[i][zz * SUB : (zz + 1) * SUB] for i in range(GROUP)], 0)
                    if n < vec:
                        k = lax.rem(strip - n + vec, vec)
                        v_ref[plane + zz, pl.ds(pl.multiple_of(k * ROWS, ROWS), ROWS), :] = block
                    else:
                        d_ref[plane + zz] = 3.25 + block
            return carry

        lax.fori_loop(0, pairs, one, 0, unroll=True)


def potential_rows(mine, other, vec, arrived):
    planes = 4 * mine.shape[1]
    return pl.pallas_call(
        functools.partial(potential_rows_kernel, vec, len(arrived)),
        out_shape=[
            jax.ShapeDtypeStruct((planes, vec * ROWS, LANES), F32),
            jax.ShapeDtypeStruct((planes, ROWS, LANES), F32),
        ],
        in_specs=[pl.BlockSpec(memory_space=pltpu.VMEM)] * (2 + len(arrived)),
        out_specs=[pl.BlockSpec(memory_space=pltpu.VMEM)] * 2,
        compiler_params=pltpu.CompilerParams(vmem_limit_bytes=24 << 20),
        name="potential_rows",
    )(mine, other, *arrived)


def solve_kernel(vec, first, part, *refs):
    psi_ref, v_ref, d_ref = refs[:3]
    refs = refs[3:]
    sum_ref = None if first else refs[0]
    out_ref, psi_s, h_s, c_s, u_a, u_b = refs[-6:]
    planes = d_ref.shape[0]
    depth = (planes - 2 * GROUP) // 2
    core = lax.axis_index("orb") % 2
    begins = {None: 0, "own": core * depth, "other": (1 - core) * depth}[part]
    count = 2 * depth if part is None else depth
    top = (lax.axis_index("orb") // 2) * 2 * depth - GROUP
    top_row = lax.axis_index("vec") * (ROWS - 2 * GROUP) - GROUP
    lane = lax.broadcasted_iota(jnp.int32, (SUB, LANES), 1)
    group = lax.broadcasted_iota(jnp.int32, (SUB, LANES), 0)
    inside = []
    for i in range(GROUP):
        y = top_row + group * GROUP + i
        inside.append(jnp.where((y >= 0) & (y < NY) & (lane < NX), 0.5, 0.0))
    inside = jnp.concatenate(inside, 0)
    block = psi_ref[0, 0].astype(F32)
    energy = block[0:1, 0:1] + block[0:1, 1:2] + block[0:1, 2:3]
    at = lax.broadcasted_iota(jnp.int32, (2 * LANES, LANES), 0) % LANES
    to = lax.broadcasted_iota(jnp.int32, (2 * LANES, LANES), 1)
    beside = jnp.where((at == to - 1) | (at == to + 1), 1.0, 0.0).astype(BF16)

    def begin(pair, carry):
        rows = to_rows([psi_ref[begins // 2 + pair, i].astype(F32) for i in range(TILES)])
        for zz in range(2):
            w = GROUP - HALO + begins + 2 * pair + zz
            z = top + w
            there = jnp.where((z >= 0) & (z < NZ), 1.0, 0.0)
            psi = jnp.concatenate([rows[i][zz * SUB : (zz + 1) * SUB] for i in range(GROUP)], 0)
            h = inside * there / (d_ref[w] - energy)
            psi_s[w] = SCALES[STEPS - 1] * psi
            h_s[w] = h
            scaled = -2.0 * psi * h
            for k in range(vec):
                rows_k = pl.ds(k * ROWS, ROWS)
                c_s[w, rows_k, :] = scaled * v_ref[w, rows_k, :]
        return carry

    lax.fori_loop(0, (count + 2 * HALO) // 2, begin, 0, unroll=3)

    def stepped(src, w, step):
        u = src[w]
        high, low = split(u)
        x = jnp.dot(jnp.concatenate([high, low], 1), beside, preferred_element_type=F32)
        near = x + (src[w - 1] + src[w + 1])
        own, given, around = COEFFICIENTS[step]
        h = around * h_s[w]
        new = []
        for k in range(vec):
            rows = [u[k * ROWS + i * SUB : k * ROWS + (i + 1) * SUB] for i in range(GROUP)]
            north = jnp.concatenate([pltpu.roll(rows[-1], 1, 0)] + rows[:-1], 0)
            south = jnp.concatenate(rows[1:] + [pltpu.roll(rows[0], SUB - 1, 0)], 0)
            at_k = slice(k * ROWS, (k + 1) * ROWS)
            change = h * (near[at_k] + (north + south))
            if src is c_s:
                new.append((own + given) * u[at_k] + change)
            else:
                new.append((u[at_k] + given * c_s[w, at_k, :]) + change)
        return new

    src, dst = c_s, u_a
    for step in range(1, STEPS - 1):
        low = GROUP - HALO + step

        def middle(p, carry, src=src, dst=dst, step=step, low=low):
            w = begins + low + p
            dst[w] = jnp.concatenate(stepped(src, w, step), 0)
            return carry

        lax.fori_loop(0, count + 2 * (HALO - step), middle, 0, unroll=True)
        src, dst = dst, (u_b if dst is u_a else u_a)

    def end(p, carry, src=src):
        w = GROUP + begins + p
        psi = psi_s[w]
        total = jnp.concatenate([psi * new for new in stepped(src, w, STEPS - 1)], 0)
        if not first:
            total = total + sum_ref[begins + p]
        out_ref[p] = total
        return carry

    lax.fori_loop(0, count, end, 0, unroll=True)


def solve_window(psi, v, d, total, vec, part=None):
    planes = d.shape[0]
    depth = (planes - 2 * GROUP) // 2
    args = (psi, v, d) if total is None else (psi, v, d, total)
    return pl.pallas_call(
        functools.partial(solve_kernel, vec, total is None, part),
        out_shape=jax.ShapeDtypeStruct((2 * depth if part is None else depth, LANES, LANES), F32),
        in_specs=[pl.BlockSpec(memory_space=pltpu.VMEM)] * len(args),
        out_specs=pl.BlockSpec(memory_space=pltpu.VMEM),
        scratch_shapes=[pltpu.VMEM((planes, ROWS, LANES), F32)] * 2
        + [pltpu.VMEM((planes, vec * ROWS, LANES), F32)] * 3,
        compiler_params=pltpu.CompilerParams(vmem_limit_bytes=32 << 20),
        name="solve_window",
    )(*args)


def forward_x_kernel(ndev, basis_ref, own_ref, other_ref, out_ref):
    depth = own_ref.shape[0] // LANES
    inner = depth - depth // TAILS
    rows = out_ref.shape[0] // ndev
    vecrows = LANES // SUB
    basis = (basis_ref[0], basis_ref[1])
    lane = lax.broadcasted_iota(jnp.int32, (NX, LANES), 1)
    pad = jnp.zeros((LANES - (SUB - 2) * vecrows, LANES), F32)
    got = []
    for z in range(depth):
        groups = [pl.ds(z * LANES + g, vecrows, SUB) for g in range(1, SUB - 1)]
        chi = jnp.concatenate([own_ref[g, :] + other_ref[g, :] for g in groups] + [pad], 0)
        got.append(dot3(basis, split(chi), ((1,), (1,))))
    for z in range(inner):
        whole, third = inner + z // TILES, z % TILES
        tail = pltpu.roll(got[whole], LANES - LANES // TAILS * (third + 1), 1)
        row = jnp.where(lane < LANES - LANES // TAILS, got[z], tail)
        for part in range(NX // ndev):
            out_ref[pl.ds(part * inner + z, ndev, rows), :] = row[part * ndev : (part + 1) * ndev]


def forward_x(own, other, basis, ndev):
    depth = own.shape[0]
    rows = -(-(NX // ndev) * (depth - depth // TAILS) // 4) * 4
    out = pl.pallas_call(
        functools.partial(forward_x_kernel, ndev),
        out_shape=jax.ShapeDtypeStruct((ndev * rows, LANES), F32),
        in_specs=[pl.BlockSpec(memory_space=pltpu.VMEM)] * 3,
        out_specs=pl.BlockSpec(memory_space=pltpu.VMEM),
        compiler_params=pltpu.CompilerParams(vmem_limit_bytes=24 << 20),
        name="forward_x",
    )(basis, own.reshape(-1, LANES), other.reshape(-1, LANES))
    return out.reshape(ndev, rows // 4, 4, LANES)


def spectral_kernel(orb, vec, rows, mux_ref, muzy_ref, wy_ref, kz_ref, kzb_ref, wyb_ref, got_ref, out_ref):
    ndev = orb * vec
    parts = NX // ndev
    me = lax.axis_index("orb") * vec + lax.axis_index("vec")
    inner = NZ // orb - NZ // orb // TAILS
    lane = lax.broadcasted_iota(jnp.int32, (orb, LANES), 1)
    strips = []
    for v in range(vec):
        main = [got_ref[pl.ds(v * rows + r, orb, vec * rows), :] for r in range(parts * inner)]
        tails = []
        for r in range(0, parts * inner, TILES):
            tail = pltpu.roll(main[r], LANES // TAILS, 1)
            for p in range(1, TILES):
                third = pltpu.roll(main[r + p], (p + 1) * LANES // TAILS, 1)
                tail = jnp.where(lane >= p * LANES // TAILS, third, tail)
            tails.append(tail)
        strips.append(jnp.concatenate(main + tails, 0))
    mm = ((1,), (0,))
    t = dot3(split(jnp.concatenate(strips, 1)), (wy_ref[0], wy_ref[1]), mm)
    t = dot3((kz_ref[0], kz_ref[1]), split(t), mm)
    scale = jnp.concatenate(
        [
            math.sqrt(4.0 * math.pi) / jnp.sqrt(muzy_ref[...] + mux_ref[part * ndev + me])
            for part in range(parts)
        ],
        0,
    )
    fields = [t[:, k * LANES : (k + 1) * LANES] * scale for k in range(vec)]
    lane = lax.broadcasted_iota(jnp.int32, (1, LANES), 1)
    gram = jnp.zeros((1, LANES), F32)
    for k in range(vec):
        for l in range(k + 1):
            entry = jnp.sum(jnp.sum(fields[k] * fields[l], axis=0, keepdims=True), axis=1, keepdims=True)
            gram = jnp.where(lane == k * vec + l, entry, gram)
    t = jnp.concatenate(fields, 1)
    t = jnp.concatenate(
        [dot3((kzb_ref[0], kzb_ref[1]), split(t[part * NZ : (part + 1) * NZ]), mm) for part in range(parts)], 0
    )
    t = dot3(split(t), (wyb_ref[0], wyb_ref[1]), mm)
    rows = out_ref.shape[0] // ndev
    zs = NZ // ndev
    for part in range(parts):
        for z in range(zs):
            for yt in range(TILES):
                out_ref[pl.ds((z * parts + part) * TILES + yt, ndev, rows), :] = t[
                    (part * zs + z) * ndev : (part * zs + z + 1) * ndev, yt * LANES : (yt + 1) * LANES
                ]
    out_ref[pl.ds(zs * parts * TILES, ndev, rows), :] = jnp.broadcast_to(gram, (ndev, LANES))


def spectral(got, orb, vec):
    ndev = orb * vec
    parts, zs = NX // ndev, NZ // ndev
    depth = NZ // orb
    quarter = depth // TAILS
    inner = depth - quarter
    strip = ROWS - 2 * GROUP
    rows_in = got.shape[1] * got.shape[2]
    rows_out = -(-(parts * zs * TILES + 1) // 4) * 4
    sy, sz = np_basis(NY), np_basis(NZ)
    wy = np.zeros((vec, LANES, vec, LANES))
    wyb = np.zeros((vec, LANES, TILES, vec, GROUP, SUB))
    for k in range(vec):
        for i in range(GROUP):
            for g in range(SUB):
                for v in range(vec):
                    if g < SUB - 2:
                        wy[v, (g * vec + k) * GROUP + i, k, :NY] = sy[v * strip + GROUP * g + i]
                for yt in range(TILES):
                    wyb[k, :NY, yt, k, i, g] = sy[yt * ROWS + GROUP * g + i]
    wy = wy.reshape(vec * LANES, vec * LANES)
    wyb = wyb.reshape(vec * LANES, TILES * LANES)
    kz = np.zeros((parts, NZ, parts, inner, orb))
    kzt = np.zeros((parts, NZ, parts, quarter, orb))
    for part in range(parts):
        for o in range(orb):
            mine = sz[:, o * depth : (o + 1) * depth]
            kz[part, :, part, :, o] = mine[:, :inner]
            kzt[part, :, part, :, o] = mine[:, inner:]
    kz = np.concatenate([kz.reshape(parts * NZ, -1), kzt.reshape(parts * NZ, -1)], 1)
    kzb = np.concatenate([sz[z::zs] for z in range(zs)])
    muzy = np.ones((NZ, LANES), np.float32)
    muzy[:, :NY] = np_eigen(NZ)[:, None] + np_eigen(NY)[None, :]
    mux = np_eigen(NX).astype(np.float32)
    out = pl.pallas_call(
        functools.partial(spectral_kernel, orb, vec, rows_in),
        out_shape=jax.ShapeDtypeStruct((ndev * rows_out, LANES), F32),
        in_specs=[pl.BlockSpec(memory_space=pltpu.SMEM)] + [pl.BlockSpec(memory_space=pltpu.VMEM)] * 6,
        out_specs=pl.BlockSpec(memory_space=pltpu.VMEM),
        compiler_params=pltpu.CompilerParams(vmem_limit_bytes=32 << 20),
        name="spectral",
    )(mux, muzy, np_split(wy), np_split(kz), np_split(kzb), np_split(wyb), got.reshape(-1, LANES))
    return out.reshape(ndev, rows_out // 4, 4, LANES)


def back_kernel(ndev, vec, basis_ref, got_ref, factor_ref, *outs):
    parts, zs = NX // ndev, NZ // ndev
    rows = got_ref.shape[0] // ndev
    strip = lax.axis_index("vec")
    basis = (basis_ref[0], basis_ref[1])
    gram = jnp.sum(got_ref[pl.ds(zs * parts * TILES, ndev, rows), :], axis=0, keepdims=True)
    gram = gram / (NZ * NY * NX)
    entry = lambda k, l: gram[:, k * vec + l : k * vec + l + 1]
    lower = [[None] * vec for _ in range(vec)]
    inverse = [[jnp.zeros((1, 1), F32)] * vec for _ in range(vec)]
    for l in range(vec):
        pivot = entry(l, l)
        for m in range(l):
            pivot = pivot - lower[l][m] * lower[l][m]
        lower[l][l] = jnp.sqrt(pivot)
        inverse[l][l] = 1.0 / lower[l][l]
        for k in range(l + 1, vec):
            value = entry(k, l)
            for m in range(l):
                value = value - lower[k][m] * lower[l][m]
            lower[k][l] = value * inverse[l][l]
    for l in range(vec):
        for k in range(l + 1, vec):
            value = lower[k][l] * inverse[l][l]
            for m in range(l + 1, k):
                value = value + lower[k][m] * inverse[m][l]
            inverse[k][l] = -value * inverse[k][k]
    at_row = lax.broadcasted_iota(jnp.int32, (vec, vec), 0)
    at_col = lax.broadcasted_iota(jnp.int32, (vec, vec), 1)
    factor = jnp.zeros((vec, vec), F32)
    for k in range(vec):
        for l in range(k + 1):
            factor = jnp.where((at_row == l) & (at_col == k), lower[k][l], factor)
    factor_ref[...] = factor
    coefficients = []
    for s in range(vec):
        to = lax.rem(strip + s, vec)
        line = []
        for k in range(vec):
            value = inverse[0][k]
            for m in range(1, vec):
                value = jnp.where(to == m, inverse[m][k], value)
            line.append(value)
        coefficients.append(line)
    for z in range(zs):
        for yt in range(TILES):
            x = jnp.concatenate(
                [
                    got_ref[pl.ds((z * parts + part) * TILES + yt, ndev, rows), :]
                    for part in range(parts)
                ],
                0,
            )
            y = dot3(split(x), basis, ((0,), (0,)))
            for s in range(vec):
                mixed = coefficients[s][0] * y[:ROWS]
                for k in range(1, vec):
                    mixed = mixed + coefficients[s][k] * y[k * ROWS : (k + 1) * ROWS]
                tiles = to_tiles([mixed[i * SUB : (i + 1) * SUB] for i in range(GROUP)])
                for i in range(TILES):
                    outs[s][pl.ds((z * TILES + yt) * WTILES + i, SUB, TILES), :] = tiles[i]


def back(got, basis, ndev, vec):
    zs = NZ // ndev
    tiles = NY * NX // LANES
    return pl.pallas_call(
        functools.partial(back_kernel, ndev, vec),
        out_shape=[jax.ShapeDtypeStruct((vec, vec), F32)]
        + [jax.ShapeDtypeStruct((zs * tiles, LANES), F32)] * vec,
        in_specs=[pl.BlockSpec(memory_space=pltpu.VMEM)] * 2,
        out_specs=[pl.BlockSpec(memory_space=pltpu.VMEM)] * (vec + 1),
        compiler_params=pltpu.CompilerParams(vmem_limit_bytes=24 << 20),
        name="back",
    )(basis, got.reshape(-1, LANES))


def assemble_kernel(vec, *refs):
    gots, (out_any, sem) = refs[:vec], refs[vec:]
    strip = lax.axis_index("vec")
    rows = gots[0].shape[0]
    copies = []
    for s in range(vec):
        start = pl.multiple_of(lax.rem(strip - s + vec, vec) * rows, 8)
        copies.append(pltpu.make_async_copy(gots[s], out_any.at[pl.ds(start, rows)], sem.at[s]))
    for copy in copies:
        copy.start()
    for copy in copies:
        copy.wait()


def assemble(gots):
    vec = len(gots)
    rows = gots[0].shape[0] * vec
    out = pl.pallas_call(
        functools.partial(assemble_kernel, vec),
        out_shape=jax.ShapeDtypeStruct((rows, LANES), F32),
        in_specs=[pl.BlockSpec(memory_space=pltpu.VMEM)] * vec,
        out_specs=pl.BlockSpec(memory_space=pltpu.HBM),
        scratch_shapes=[pltpu.SemaphoreType.DMA((vec,))],
        compiler_params=pltpu.CompilerParams(vmem_limit_bytes=24 << 20),
        name="assemble",
    )(*gots)
    return out.reshape(1, rows * LANES // (NY * NX), NY * NX)


def swap_cores(x, orb):
    return lax.ppermute(x, "orb", [(o, o ^ 1) for o in range(orb)])


def shift(x, axis, count):
    n = lax.axis_size(axis)
    return lax.ppermute(x, axis, [(i, (i + count) % n) for i in range(n)])


def responses(orbitals, energies, trial_potential, local_potential):
    orb, vec = lax.axis_size("orb"), lax.axis_size("vec")
    chips = orb // 2
    psis, parts = windows(orbitals, energies, trial_potential, local_potential, orb, vec)
    def to_chip(r):
        perm = [(2 * a + c, 2 * ((a + r) % chips) + c) for a in range(chips) for c in range(2)]
        return lax.ppermute(psis[r], "orb", perm)

    order = [1, chips - 1, *range(2, chips - 1)]
    for r in order:
        psis[r] = to_chip(r)
    for n in range(1, vec):
        parts[n] = shift(parts[n], "vec", n)
    arrived = [psis[r] for r in order]
    own, edge = edges(parts, [])
    near = [(o, o + 1) for o in range(1, orb - 1, 2)] + [(o + 1, o) for o in range(1, orb - 1, 2)]
    edge = lax.ppermute(edge, "orb", near + [(0, 0), (orb - 1, orb - 1)])
    mine = with_edge(own, edge, arrived[:2])
    v, d = potential_rows(mine, swap_cores(mine, orb), vec, [])
    total = None
    for r in [0] + order[:-1]:
        total = solve_window(psis[r], v, d, total, vec)
    last = psis[order[-1]]
    other = swap_cores(solve_window(last, v, d, total, vec, "other"), orb)
    return solve_window(last, v, d, total, vec, "own"), other


def block_body(orbitals, energies, trial_potential, local_potential):
    orb, vec = lax.axis_size("orb"), lax.axis_size("vec")
    ndev = orb * vec
    both = ("orb", "vec")
    own, other = responses(orbitals, energies, trial_potential, local_potential)
    sx = np_basis(NX)
    padded = np.zeros((NX, LANES))
    padded[:, :NX] = sx
    sent = forward_x(own, other, np_split(padded * (4.0 / orb)), ndev)
    got = lax.all_to_all(sent, both, 0, 0, tiled=True)
    sent = spectral(got, orb, vec)
    got = lax.all_to_all(sent, both, 0, 0, tiled=True)
    factor, *slots = back(got, np_split(padded), ndev, vec)
    gots = [slots[0]] + [shift(slots[s], "vec", s) for s in range(1, vec)]
    return assemble(gots), factor


def solution(mesh):
    orb, vec = mesh.shape["orb"], mesh.shape["vec"]
    placed = (P("orb", None, None), P("orb"), P("vec", "orb", None), P("orb", None))

    def body(orbitals, energies, trial_potential, local_potential):
        one = orbitals.shape[0] == 1 and trial_potential.shape[0] == 1
        plan = block_body if one and fits(orb, vec, orb, vec) else general_body
        return plan(orbitals, energies, trial_potential, local_potential)

    return jax.shard_map(
        body, mesh=mesh, in_specs=placed, out_specs=(P("vec", "orb", None), P()), check_vma=False
    )
```

```python
import functools
import math

import jax
import jax.numpy as jnp
import ml_dtypes
import numpy as np
from jax import lax
from jax.experimental import pallas as pl
from jax.experimental.pallas import tpu as pltpu
from jax.sharding import PartitionSpec as P

NZ = 96
NY = 96
NX = 96
STEPS = 4

BF16 = jnp.bfloat16
F32 = jnp.float32
LANES = 128
WEIGHTS = [1.0 / (1.0 + 0.8 * math.cos(math.pi * (2 * s + 1) / (2 * STEPS))) for s in range(STEPS)]

SCALES = [WEIGHTS[0]]
for weight_ in WEIGHTS[1:]:
    SCALES.append((1.0 - weight_) * SCALES[-1])
COEFFICIENTS = [None] + [
    (1.0, WEIGHTS[s] / SCALES[s], WEIGHTS[s] * SCALES[s - 1] / SCALES[s]) for s in range(1, STEPS)
]


def neighbours(field):
    depth, flat = field.shape
    zero_plane = jnp.zeros((1, flat), field.dtype)
    total = jnp.concatenate([zero_plane, field[:-1]], 0) + jnp.concatenate(
        [field[1:], zero_plane], 0
    )
    zero_rows = jnp.zeros((depth, NX), field.dtype)
    total = (
        total
        + jnp.concatenate([zero_rows, field[:, :-NX]], 1)
        + jnp.concatenate([field[:, NX:], zero_rows], 1)
    )
    column = jnp.arange(flat) % NX
    zero_col = jnp.zeros((depth, 1), field.dtype)
    left = jnp.concatenate([zero_col, field[:, :-1]], 1) * (column > 0).astype(field.dtype)
    right = jnp.concatenate([field[:, 1:], zero_col], 1) * (column < NX - 1).astype(field.dtype)
    return total + left + right


def solve(psi, perturb, potential, energy):
    diag = 3.25 + potential - energy
    source = -perturb * psi
    answer = jnp.zeros_like(psi)
    for step in range(STEPS):
        weight = 1.0 / (1.0 + 0.8 * jnp.cos(jnp.pi * (2 * step + 1) / (2 * STEPS)))
        applied = diag * answer - 0.5 * neighbours(answer)
        answer = answer + weight * (source - applied) / diag
    return answer


def sine_basis(count):
    index = jnp.arange(count, dtype=jnp.float32) + 1.0
    return jnp.sqrt(2.0 / (count + 1)) * jnp.sin(
        jnp.pi * index[:, None] * index[None, :] / (count + 1)
    )


def eigen_of(position, count):
    return 2.0 - 2.0 * jnp.cos(jnp.pi * (position.astype(jnp.float32) + 1.0) / (count + 1))


def planes(field):
    high = lax.Precision.HIGHEST
    depth = field.shape[0]
    cube = field.reshape(depth, NY, NX)
    cube = jnp.einsum("zyx,cx->zyc", cube, sine_basis(NX), precision=high)
    cube = jnp.einsum("zyc,by->zbc", cube, sine_basis(NY), precision=high)
    return cube.reshape(depth, NY * NX)


def scale_columns(columns, start):
    high = lax.Precision.HIGHEST
    width = columns.shape[1]
    position = start + jnp.arange(width)
    denom = (
        eigen_of(jnp.arange(NZ), NZ)[:, None]
        + eigen_of(position // NX, NY)[None, :]
        + eigen_of(position % NX, NX)[None, :]
    )
    basis = sine_basis(NZ)
    spectral = jnp.dot(basis, columns, precision=high) * (jnp.sqrt(4.0 * jnp.pi) / jnp.sqrt(denom))
    return jnp.dot(basis, spectral, precision=high)


def coulomb_slab(slab):
    columns = lax.all_to_all(planes(slab), "orb", split_axis=1, concat_axis=0, tiled=True)
    scaled = scale_columns(columns, lax.axis_index("orb") * columns.shape[1])
    back = lax.all_to_all(scaled, "orb", split_axis=0, concat_axis=1, tiled=True)
    return planes(back)


def factorize(partial_gram):
    lower = jnp.linalg.cholesky(partial_gram / (NZ * NY * NX))
    inverse = lax.linalg.triangular_solve(
        lower, jnp.eye(lower.shape[0], dtype=jnp.float32), left_side=True, lower=True
    )
    return (lower, inverse)


def general_body(orbitals, energies, trial_potential, local_potential):
    high = lax.Precision.HIGHEST
    depth = local_potential.shape[0]
    plane_cells = local_potential.shape[1]
    vector_slab = trial_potential.reshape(depth, plane_cells)
    perturb_full, potential_full = (
        lax.all_gather(vector_slab, "orb", axis=0, tiled=True),
        lax.all_gather(local_potential, "orb", axis=0, tiled=True),
    )
    perturb = perturb_full.astype(jnp.float32)
    potential = potential_full.astype(jnp.float32)
    weight = 4.0 / (orbitals.shape[0] * lax.axis_size("orb"))
    psi = orbitals[0].astype(jnp.float32)
    partial_value = psi * solve(psi, perturb, potential, energies[0])
    partial_value = partial_value * weight
    slab = lax.psum_scatter(partial_value, "orb", scatter_dimension=0, tiled=True)
    slab = coulomb_slab(slab)
    mine = slab.reshape(1, depth, plane_cells)
    gathered = lax.all_gather(mine, "vec", axis=0, tiled=True)
    flat = gathered.reshape(gathered.shape[0], depth * plane_cells)
    partial_gram = jnp.dot(flat, flat.T, precision=high)
    lower, inverse = factorize(lax.psum(partial_gram, "orb"))
    row = lax.dynamic_slice_in_dim(inverse, lax.axis_index("vec"), 1, 0)
    ortho = jnp.dot(row, flat, precision=high).reshape(1, depth, plane_cells)
    return (ortho, lower.T)


TILES = 3
GROUP = 4
SUB = 8
ROWS = GROUP * SUB
WTILES = TILES * SUB
HALO = STEPS - 1
TAILS = 4


def fits(orb, vec, norb, nv):
    return (
        norb == orb
        and nv == vec
        and orb % 2 == 0
        and NZ % orb == 0
        and NZ // orb >= 4
        and NZ // orb % 2 == 0
        and NY == vec * (ROWS - 2 * GROUP)
        and NY == TILES * ROWS
        and vec * ROWS == LANES
        and NX * GROUP == TILES * LANES
        and NX % (orb * vec) == 0
        and NZ % (orb * vec) == 0
        and STEPS <= GROUP
        and NZ // orb == TAILS * TILES
        and vec == GROUP
    )


def split(x):
    high = x.astype(BF16)
    return high, (x - high.astype(F32)).astype(BF16)


def np_split(x):
    x = np.asarray(x, np.float64)
    high = x.astype(ml_dtypes.bfloat16)
    return np.stack([high, (x - high.astype(np.float64)).astype(ml_dtypes.bfloat16)])


def dot3(a, b, dims):
    one = functools.partial(
        lax.dot_general, dimension_numbers=(dims, ((), ())), preferred_element_type=F32
    )
    if dims[0] == (1,) and a[0].shape[1] == LANES:
        return one(jnp.concatenate([a[0], a[0], a[1]], 1), jnp.concatenate([b[0], b[1], b[0]], dims[1][0]))
    return one(a[0], b[0]) + (one(a[0], b[1]) + one(a[1], b[0]))


def np_basis(count):
    index = np.arange(count, dtype=np.float64) + 1.0
    return np.sqrt(2.0 / (count + 1)) * np.sin(np.pi * np.outer(index, index) / (count + 1))


def np_eigen(count):
    return 4.0 * np.sin(np.pi * (np.arange(count, dtype=np.float64) + 1.0) / (2 * (count + 1))) ** 2


def to_rows(tiles):
    lane = lax.broadcasted_iota(jnp.int32, tiles[0].shape, 1)
    a, b, c = tiles
    return [
        a,
        pltpu.roll(jnp.where(lane >= 96, a, b), 32, 1),
        pltpu.roll(jnp.where(lane >= 64, b, c), 64, 1),
        pltpu.roll(c, 96, 1),
    ]


def to_tiles(rows):
    lane = lax.broadcasted_iota(jnp.int32, rows[0].shape, 1)
    r1, r2 = pltpu.roll(rows[1], 96, 1), pltpu.roll(rows[2], 64, 1)
    return [
        jnp.where(lane < 96, rows[0], r1),
        jnp.where(lane < 64, r1, r2),
        jnp.where(lane < 32, r2, pltpu.roll(rows[3], 32, 1)),
    ]


def first_tile(strip):
    return strip * (WTILES - 2 * TILES) - TILES


def window_start(strip):
    return jnp.clip(first_tile(strip), 0, NY * NX // LANES - WTILES)


def tile_lanes(strip, t, start=0):
    tile = jnp.clip(first_tile(strip) + t, 0, NY * NX // LANES - 1) - start
    return pl.ds(pl.multiple_of(tile * LANES, LANES), LANES)


def pack_planes(src, plane, out, pairs):
    def one(pair, carry):
        for i in range(TILES):
            top = pl.multiple_of((plane + 2 * pair) * WTILES + i * SUB, SUB)
            low = pl.multiple_of((plane + 2 * pair + 1) * WTILES + i * SUB, SUB)
            block = jnp.concatenate([src[pl.ds(top, SUB), :], src[pl.ds(low, SUB), :]], 0)
            out[pair, i] = block.astype(BF16)
        return carry

    lax.fori_loop(0, pairs, one, 0)


def windows_kernel(orb, vec, energy_any, psi_any, v_any, pot_any, *refs):
    outs, (planes_ref, more_ref, psi_ref, v_ref, pot_ref, energy_ref, sem) = refs[:-7], refs[-7:]
    chips = orb // 2
    slab = NZ // chips
    depth = v_ref.shape[0]
    chip = lax.axis_index("orb") // 2
    strip = lax.axis_index("vec")
    start = window_start(strip)
    lanes = pl.ds(pl.multiple_of(start * LANES, LANES), WTILES * LANES)
    copies = [
        pltpu.make_async_copy(v_any.at[0], v_ref, sem.at[0]),
        pltpu.make_async_copy(pot_any.at[:, lanes], pot_ref, sem.at[1]),
        pltpu.make_async_copy(psi_any.at[0, :, lanes], psi_ref, sem.at[2]),
        pltpu.make_async_copy(energy_any, energy_ref, sem.at[3]),
    ]
    for copy in copies:
        copy.start()
    for copy in copies[:2]:
        copy.wait()
    for n in range(vec + 1):
        for t in range(WTILES):
            row = (n * depth) * WTILES + (t % TILES) * SUB + t // TILES
            if n < vec:
                tile = v_ref[:, tile_lanes(lax.rem(strip + n, vec), t)]
            else:
                tile = pot_ref[:, tile_lanes(strip, t, start)]
            more_ref[pl.ds(row, depth, WTILES), :] = tile.astype(F32)
        pack_planes(more_ref, n * depth, outs[chips + n], depth // 2)
    zero = jnp.zeros((HALO * WTILES, LANES), F32)
    planes_ref[: HALO * WTILES, :] = zero
    planes_ref[(NZ + HALO) * WTILES :, :] = zero
    for copy in copies[2:]:
        copy.wait()
    for t in range(WTILES):
        row = HALO * WTILES + (t % TILES) * SUB + t // TILES
        planes_ref[pl.ds(row, NZ, WTILES), :] = psi_ref[:, tile_lanes(strip, t, start)].astype(F32)
    energy = jnp.full((1, LANES), energy_ref[0], F32)
    high = energy.astype(BF16).astype(F32)
    middle = (energy - high).astype(BF16).astype(F32)
    low = energy - high - middle
    lane = lax.broadcasted_iota(jnp.int32, (1, LANES), 1)
    for at in range(chips):
        row = at * slab * WTILES
        held = planes_ref[row : row + 1, :]
        held = jnp.where(lane == 0, high, jnp.where(lane == 1, middle, jnp.where(lane == 2, low, held)))
        planes_ref[row : row + 1, :] = held
    for shift in range(chips):
        pack_planes(planes_ref, ((chip + shift) % chips) * slab, outs[shift], (slab + 2 * HALO) // 2)


def windows(orbitals, energies, trial, potential, orb, vec):
    chips = orb // 2
    depth = potential.shape[0]
    block = (TILES, 2 * SUB, LANES)
    pairs = (NZ // chips + 2 * HALO) // 2
    outs = [jax.ShapeDtypeStruct((pairs, *block), BF16)] * chips
    outs += [jax.ShapeDtypeStruct((depth // 2, *block), BF16)] * (vec + 1)
    got = pl.pallas_call(
        functools.partial(windows_kernel, orb, vec),
        out_shape=outs,
        in_specs=[pl.BlockSpec(memory_space=pl.ANY)] + [pl.BlockSpec(memory_space=pltpu.HBM)] * 3,
        out_specs=[pl.BlockSpec(memory_space=pltpu.VMEM)] * len(outs),
        scratch_shapes=[
            pltpu.VMEM(((NZ + 2 * HALO) * WTILES, LANES), F32),
            pltpu.VMEM(((vec + 1) * depth * WTILES, LANES), F32),
            pltpu.VMEM((NZ, WTILES * LANES), BF16),
            pltpu.VMEM((depth, NY * NX), BF16),
            pltpu.VMEM((depth, WTILES * LANES), BF16),
            pltpu.SMEM((1,), F32),
            pltpu.SemaphoreType.DMA((4,)),
        ],
        compiler_params=pltpu.CompilerParams(vmem_limit_bytes=24 << 20),
        name="windows",
    )(energies, *(pltpu.with_memory_space_constraint(x, pltpu.HBM) for x in (orbitals, trial, potential)))
    return list(got[:chips]), list(got[chips:])


def edges_kernel(n, parts_and_more, *refs):
    parts, (own_ref, edge_ref) = refs[:n], refs[parts_and_more:]
    core = lax.axis_index("orb") % 2
    first = core * (own_ref.shape[1] - edge_ref.shape[1])
    for i, part in enumerate(parts):
        own_ref[i] = part[...]
        edge_ref[i] = part[pl.ds(first, edge_ref.shape[1])]


def edges(parts, arrived):
    pairs, *block = parts[0].shape
    n = len(parts)
    more = n + len(arrived)
    return pl.pallas_call(
        functools.partial(edges_kernel, n, more),
        out_shape=[
            jax.ShapeDtypeStruct((n, pairs, *block), BF16),
            jax.ShapeDtypeStruct((n, GROUP // 2, *block), BF16),
        ],
        in_specs=[pl.BlockSpec(memory_space=pltpu.VMEM)] * more,
        out_specs=[pl.BlockSpec(memory_space=pltpu.VMEM)] * 2,
        compiler_params=pltpu.CompilerParams(vmem_limit_bytes=24 << 20),
        name="edges",
    )(*parts, *arrived)


def with_edge_kernel(n, own_ref, edge_ref, *refs):
    out_ref = refs[n]
    core = lax.axis_index("orb") % 2
    pairs, edge = own_ref.shape[1], edge_ref.shape[1]
    out_ref[:, pl.ds((1 - core) * edge, pairs)] = own_ref[...]
    out_ref[:, pl.ds(core * pairs, edge)] = edge_ref[...]


def with_edge(own, edge, arrived):
    n, pairs, *block = own.shape
    return pl.pallas_call(
        functools.partial(with_edge_kernel, len(arrived)),
        out_shape=jax.ShapeDtypeStruct((n, pairs + edge.shape[1], *block), own.dtype),
        in_specs=[pl.BlockSpec(memory_space=pltpu.VMEM)] * (2 + len(arrived)),
        out_specs=pl.BlockSpec(memory_space=pltpu.VMEM),
        compiler_params=pltpu.CompilerParams(vmem_limit_bytes=24 << 20),
        name="with_edge",
    )(own, edge, *arrived)


def potential_rows_kernel(vec, n, mine_ref, other_ref, *refs):
    v_ref, d_ref = refs[n:]
    core = lax.axis_index("orb") % 2
    strip = lax.axis_index("vec")
    pairs = mine_ref.shape[1]
    for src, first in ((mine_ref, core * pairs), (other_ref, (1 - core) * pairs)):

        def one(pair, carry, src=src, first=first):
            plane = 2 * (first + pair)
            for n in range(vec + 1):
                rows = to_rows([src[n, pair, i].astype(F32) for i in range(TILES)])
                for zz in range(2):
                    block = jnp.concatenate([rows[i][zz * SUB : (zz + 1) * SUB] for i in range(GROUP)], 0)
                    if n < vec:
                        k = lax.rem(strip - n + vec, vec)
                        v_ref[plane + zz, pl.ds(pl.multiple_of(k * ROWS, ROWS), ROWS), :] = block
                    else:
                        d_ref[plane + zz] = 3.25 + block
            return carry

        lax.fori_loop(0, pairs, one, 0, unroll=True)


def potential_rows(mine, other, vec, arrived):
    planes = 4 * mine.shape[1]
    return pl.pallas_call(
        functools.partial(potential_rows_kernel, vec, len(arrived)),
        out_shape=[
            jax.ShapeDtypeStruct((planes, vec * ROWS, LANES), F32),
            jax.ShapeDtypeStruct((planes, ROWS, LANES), F32),
        ],
        in_specs=[pl.BlockSpec(memory_space=pltpu.VMEM)] * (2 + len(arrived)),
        out_specs=[pl.BlockSpec(memory_space=pltpu.VMEM)] * 2,
        compiler_params=pltpu.CompilerParams(vmem_limit_bytes=24 << 20),
        name="potential_rows",
    )(mine, other, *arrived)


def solve_kernel(vec, first, part, *refs):
    psi_ref, v_ref, d_ref = refs[:3]
    refs = refs[3:]
    sum_ref = None if first else refs[0]
    out_ref, psi_s, h_s, c_s, u_a, u_b = refs[-6:]
    planes = d_ref.shape[0]
    depth = (planes - 2 * GROUP) // 2
    core = lax.axis_index("orb") % 2
    begins = {None: 0, "own": core * depth, "other": (1 - core) * depth}[part]
    count = 2 * depth if part is None else depth
    top = (lax.axis_index("orb") // 2) * 2 * depth - GROUP
    top_row = lax.axis_index("vec") * (ROWS - 2 * GROUP) - GROUP
    lane = lax.broadcasted_iota(jnp.int32, (SUB, LANES), 1)
    group = lax.broadcasted_iota(jnp.int32, (SUB, LANES), 0)
    inside = []
    for i in range(GROUP):
        y = top_row + group * GROUP + i
        inside.append(jnp.where((y >= 0) & (y < NY) & (lane < NX), 0.5, 0.0))
    inside = jnp.concatenate(inside, 0)
    block = psi_ref[0, 0].astype(F32)
    energy = block[0:1, 0:1] + block[0:1, 1:2] + block[0:1, 2:3]
    at = lax.broadcasted_iota(jnp.int32, (2 * LANES, LANES), 0) % LANES
    to = lax.broadcasted_iota(jnp.int32, (2 * LANES, LANES), 1)
    beside = jnp.where((at == to - 1) | (at == to + 1), 1.0, 0.0).astype(BF16)

    def begin(pair, carry):
        rows = to_rows([psi_ref[begins // 2 + pair, i].astype(F32) for i in range(TILES)])
        for zz in range(2):
            w = GROUP - HALO + begins + 2 * pair + zz
            z = top + w
            there = jnp.where((z >= 0) & (z < NZ), 1.0, 0.0)
            psi = jnp.concatenate([rows[i][zz * SUB : (zz + 1) * SUB] for i in range(GROUP)], 0)
            h = inside * there / (d_ref[w] - energy)
            psi_s[w] = SCALES[STEPS - 1] * psi
            h_s[w] = h
            scaled = -2.0 * psi * h
            for k in range(vec):
                rows_k = pl.ds(k * ROWS, ROWS)
                c_s[w, rows_k, :] = scaled * v_ref[w, rows_k, :]
        return carry

    lax.fori_loop(0, (count + 2 * HALO) // 2, begin, 0, unroll=True)

    def stepped(src, w, step):
        u = src[w]
        high, low = split(u)
        x = jnp.dot(jnp.concatenate([high, low], 1), beside, preferred_element_type=F32)
        near = x + (src[w - 1] + src[w + 1])
        own, given, around = COEFFICIENTS[step]
        h = around * h_s[w]
        new = []
        for k in range(vec):
            rows = [u[k * ROWS + i * SUB : k * ROWS + (i + 1) * SUB] for i in range(GROUP)]
            north = jnp.concatenate([pltpu.roll(rows[-1], 1, 0)] + rows[:-1], 0)
            south = jnp.concatenate(rows[1:] + [pltpu.roll(rows[0], SUB - 1, 0)], 0)
            at_k = slice(k * ROWS, (k + 1) * ROWS)
            change = h * (near[at_k] + (north + south))
            if src is c_s:
                new.append((own + given) * u[at_k] + change)
            else:
                new.append((u[at_k] + given * c_s[w, at_k, :]) + change)
        return new

    src, dst = c_s, u_a
    for step in range(1, STEPS - 1):
        low = GROUP - HALO + step

        def middle(p, carry, src=src, dst=dst, step=step, low=low):
            w = begins + low + p
            dst[w] = jnp.concatenate(stepped(src, w, step), 0)
            return carry

        lax.fori_loop(0, count + 2 * (HALO - step), middle, 0, unroll=True)
        src, dst = dst, (u_b if dst is u_a else u_a)

    def end(p, carry, src=src):
        w = GROUP + begins + p
        psi = psi_s[w]
        total = jnp.concatenate([psi * new for new in stepped(src, w, STEPS - 1)], 0)
        if not first:
            total = total + sum_ref[begins + p]
        out_ref[p] = total
        return carry

    lax.fori_loop(0, count, end, 0, unroll=True)


def solve_window(psi, v, d, total, vec, part=None):
    planes = d.shape[0]
    depth = (planes - 2 * GROUP) // 2
    args = (psi, v, d) if total is None else (psi, v, d, total)
    return pl.pallas_call(
        functools.partial(solve_kernel, vec, total is None, part),
        out_shape=jax.ShapeDtypeStruct((2 * depth if part is None else depth, LANES, LANES), F32),
        in_specs=[pl.BlockSpec(memory_space=pltpu.VMEM)] * len(args),
        out_specs=pl.BlockSpec(memory_space=pltpu.VMEM),
        scratch_shapes=[pltpu.VMEM((planes, ROWS, LANES), F32)] * 2
        + [pltpu.VMEM((planes, vec * ROWS, LANES), F32)] * 3,
        compiler_params=pltpu.CompilerParams(vmem_limit_bytes=32 << 20),
        name="solve_window",
    )(*args)


def forward_x_kernel(ndev, basis_ref, own_ref, other_ref, out_ref):
    depth = own_ref.shape[0] // LANES
    inner = depth - depth // TAILS
    rows = out_ref.shape[0] // ndev
    vecrows = LANES // SUB
    basis = (basis_ref[0], basis_ref[1])
    lane = lax.broadcasted_iota(jnp.int32, (NX, LANES), 1)
    pad = jnp.zeros((LANES - (SUB - 2) * vecrows, LANES), F32)
    got = []
    for z in range(depth):
        groups = [pl.ds(z * LANES + g, vecrows, SUB) for g in range(1, SUB - 1)]
        chi = jnp.concatenate([own_ref[g, :] + other_ref[g, :] for g in groups] + [pad], 0)
        got.append(dot3(basis, split(chi), ((1,), (1,))))
    for z in range(inner):
        whole, third = inner + z // TILES, z % TILES
        tail = pltpu.roll(got[whole], LANES - LANES // TAILS * (third + 1), 1)
        row = jnp.where(lane < LANES - LANES // TAILS, got[z], tail)
        for part in range(NX // ndev):
            out_ref[pl.ds(part * inner + z, ndev, rows), :] = row[part * ndev : (part + 1) * ndev]


def forward_x(own, other, basis, ndev):
    depth = own.shape[0]
    rows = -(-(NX // ndev) * (depth - depth // TAILS) // 4) * 4
    out = pl.pallas_call(
        functools.partial(forward_x_kernel, ndev),
        out_shape=jax.ShapeDtypeStruct((ndev * rows, LANES), F32),
        in_specs=[pl.BlockSpec(memory_space=pltpu.VMEM)] * 3,
        out_specs=pl.BlockSpec(memory_space=pltpu.VMEM),
        compiler_params=pltpu.CompilerParams(vmem_limit_bytes=24 << 20),
        name="forward_x",
    )(basis, own.reshape(-1, LANES), other.reshape(-1, LANES))
    return out.reshape(ndev, rows // 4, 4, LANES)


def spectral_kernel(orb, vec, rows, mux_ref, muzy_ref, wy_ref, kz_ref, kzb_ref, wyb_ref, got_ref, out_ref):
    ndev = orb * vec
    parts = NX // ndev
    me = lax.axis_index("orb") * vec + lax.axis_index("vec")
    inner = NZ // orb - NZ // orb // TAILS
    lane = lax.broadcasted_iota(jnp.int32, (orb, LANES), 1)
    strips = []
    for v in range(vec):
        main = [got_ref[pl.ds(v * rows + r, orb, vec * rows), :] for r in range(parts * inner)]
        tails = []
        for r in range(0, parts * inner, TILES):
            tail = pltpu.roll(main[r], LANES // TAILS, 1)
            for p in range(1, TILES):
                third = pltpu.roll(main[r + p], (p + 1) * LANES // TAILS, 1)
                tail = jnp.where(lane >= p * LANES // TAILS, third, tail)
            tails.append(tail)
        strips.append(jnp.concatenate(main + tails, 0))
    mm = ((1,), (0,))
    t = dot3(split(jnp.concatenate(strips, 1)), (wy_ref[0], wy_ref[1]), mm)
    t = dot3((kz_ref[0], kz_ref[1]), split(t), mm)
    scale = jnp.concatenate(
        [
            math.sqrt(4.0 * math.pi) / jnp.sqrt(muzy_ref[...] + mux_ref[part * ndev + me])
            for part in range(parts)
        ],
        0,
    )
    fields = [t[:, k * LANES : (k + 1) * LANES] * scale for k in range(vec)]
    lane = lax.broadcasted_iota(jnp.int32, (1, LANES), 1)
    gram = jnp.zeros((1, LANES), F32)
    for k in range(vec):
        for l in range(k + 1):
            entry = jnp.sum(jnp.sum(fields[k] * fields[l], axis=0, keepdims=True), axis=1, keepdims=True)
            gram = jnp.where(lane == k * vec + l, entry, gram)
    t = jnp.concatenate(fields, 1)
    t = jnp.concatenate(
        [dot3((kzb_ref[0], kzb_ref[1]), split(t[part * NZ : (part + 1) * NZ]), mm) for part in range(parts)], 0
    )
    t = dot3(split(t), (wyb_ref[0], wyb_ref[1]), mm)
    rows = out_ref.shape[0] // ndev
    zs = NZ // ndev
    for part in range(parts):
        for z in range(zs):
            for yt in range(TILES):
                out_ref[pl.ds((z * parts + part) * TILES + yt, ndev, rows), :] = t[
                    (part * zs + z) * ndev : (part * zs + z + 1) * ndev, yt * LANES : (yt + 1) * LANES
                ]
    out_ref[pl.ds(zs * parts * TILES, ndev, rows), :] = jnp.broadcast_to(gram, (ndev, LANES))


def spectral(got, orb, vec):
    ndev = orb * vec
    parts, zs = NX // ndev, NZ // ndev
    depth = NZ // orb
    quarter = depth // TAILS
    inner = depth - quarter
    strip = ROWS - 2 * GROUP
    rows_in = got.shape[1] * got.shape[2]
    rows_out = -(-(parts * zs * TILES + 1) // 4) * 4
    sy, sz = np_basis(NY), np_basis(NZ)
    wy = np.zeros((vec, LANES, vec, LANES))
    wyb = np.zeros((vec, LANES, TILES, vec, GROUP, SUB))
    for k in range(vec):
        for i in range(GROUP):
            for g in range(SUB):
                for v in range(vec):
                    if g < SUB - 2:
                        wy[v, (g * vec + k) * GROUP + i, k, :NY] = sy[v * strip + GROUP * g + i]
                for yt in range(TILES):
                    wyb[k, :NY, yt, k, i, g] = sy[yt * ROWS + GROUP * g + i]
    wy = wy.reshape(vec * LANES, vec * LANES)
    wyb = wyb.reshape(vec * LANES, TILES * LANES)
    kz = np.zeros((parts, NZ, parts, inner, orb))
    kzt = np.zeros((parts, NZ, parts, quarter, orb))
    for part in range(parts):
        for o in range(orb):
            mine = sz[:, o * depth : (o + 1) * depth]
            kz[part, :, part, :, o] = mine[:, :inner]
            kzt[part, :, part, :, o] = mine[:, inner:]
    kz = np.concatenate([kz.reshape(parts * NZ, -1), kzt.reshape(parts * NZ, -1)], 1)
    kzb = np.concatenate([sz[z::zs] for z in range(zs)])
    muzy = np.ones((NZ, LANES), np.float32)
    muzy[:, :NY] = np_eigen(NZ)[:, None] + np_eigen(NY)[None, :]
    mux = np_eigen(NX).astype(np.float32)
    out = pl.pallas_call(
        functools.partial(spectral_kernel, orb, vec, rows_in),
        out_shape=jax.ShapeDtypeStruct((ndev * rows_out, LANES), F32),
        in_specs=[pl.BlockSpec(memory_space=pltpu.SMEM)] + [pl.BlockSpec(memory_space=pltpu.VMEM)] * 6,
        out_specs=pl.BlockSpec(memory_space=pltpu.VMEM),
        compiler_params=pltpu.CompilerParams(vmem_limit_bytes=32 << 20),
        name="spectral",
    )(mux, muzy, np_split(wy), np_split(kz), np_split(kzb), np_split(wyb), got.reshape(-1, LANES))
    return out.reshape(ndev, rows_out // 4, 4, LANES)


def back_kernel(ndev, vec, basis_ref, got_ref, factor_ref, *outs):
    parts, zs = NX // ndev, NZ // ndev
    rows = got_ref.shape[0] // ndev
    strip = lax.axis_index("vec")
    basis = (basis_ref[0], basis_ref[1])
    gram = jnp.sum(got_ref[pl.ds(zs * parts * TILES, ndev, rows), :], axis=0, keepdims=True)
    gram = gram / (NZ * NY * NX)
    entry = lambda k, l: gram[:, k * vec + l : k * vec + l + 1]
    lower = [[None] * vec for _ in range(vec)]
    inverse = [[jnp.zeros((1, 1), F32)] * vec for _ in range(vec)]
    for l in range(vec):
        pivot = entry(l, l)
        for m in range(l):
            pivot = pivot - lower[l][m] * lower[l][m]
        lower[l][l] = jnp.sqrt(pivot)
        inverse[l][l] = 1.0 / lower[l][l]
        for k in range(l + 1, vec):
            value = entry(k, l)
            for m in range(l):
                value = value - lower[k][m] * lower[l][m]
            lower[k][l] = value * inverse[l][l]
    for l in range(vec):
        for k in range(l + 1, vec):
            value = lower[k][l] * inverse[l][l]
            for m in range(l + 1, k):
                value = value + lower[k][m] * inverse[m][l]
            inverse[k][l] = -value * inverse[k][k]
    at_row = lax.broadcasted_iota(jnp.int32, (vec, vec), 0)
    at_col = lax.broadcasted_iota(jnp.int32, (vec, vec), 1)
    factor = jnp.zeros((vec, vec), F32)
    for k in range(vec):
        for l in range(k + 1):
            factor = jnp.where((at_row == l) & (at_col == k), lower[k][l], factor)
    factor_ref[...] = factor
    coefficients = []
    for s in range(vec):
        to = lax.rem(strip + s, vec)
        line = []
        for k in range(vec):
            value = inverse[0][k]
            for m in range(1, vec):
                value = jnp.where(to == m, inverse[m][k], value)
            line.append(value)
        coefficients.append(line)
    for z in range(zs):
        for yt in range(TILES):
            x = jnp.concatenate(
                [
                    got_ref[pl.ds((z * parts + part) * TILES + yt, ndev, rows), :]
                    for part in range(parts)
                ],
                0,
            )
            y = dot3(split(x), basis, ((0,), (0,)))
            for s in range(vec):
                mixed = coefficients[s][0] * y[:ROWS]
                for k in range(1, vec):
                    mixed = mixed + coefficients[s][k] * y[k * ROWS : (k + 1) * ROWS]
                tiles = to_tiles([mixed[i * SUB : (i + 1) * SUB] for i in range(GROUP)])
                for i in range(TILES):
                    outs[s][pl.ds((z * TILES + yt) * WTILES + i, SUB, TILES), :] = tiles[i]


def back(got, basis, ndev, vec):
    zs = NZ // ndev
    tiles = NY * NX // LANES
    return pl.pallas_call(
        functools.partial(back_kernel, ndev, vec),
        out_shape=[jax.ShapeDtypeStruct((vec, vec), F32)]
        + [jax.ShapeDtypeStruct((zs * tiles, LANES), F32)] * vec,
        in_specs=[pl.BlockSpec(memory_space=pltpu.VMEM)] * 2,
        out_specs=[pl.BlockSpec(memory_space=pltpu.VMEM)] * (vec + 1),
        compiler_params=pltpu.CompilerParams(vmem_limit_bytes=24 << 20),
        name="back",
    )(basis, got.reshape(-1, LANES))


def assemble_kernel(vec, *refs):
    gots, (out_any, sem) = refs[:vec], refs[vec:]
    strip = lax.axis_index("vec")
    rows = gots[0].shape[0]
    copies = []
    for s in range(vec):
        start = pl.multiple_of(lax.rem(strip - s + vec, vec) * rows, 8)
        copies.append(pltpu.make_async_copy(gots[s], out_any.at[pl.ds(start, rows)], sem.at[s]))
    for copy in copies:
        copy.start()
    for copy in copies:
        copy.wait()


def assemble(gots):
    vec = len(gots)
    rows = gots[0].shape[0] * vec
    out = pl.pallas_call(
        functools.partial(assemble_kernel, vec),
        out_shape=jax.ShapeDtypeStruct((rows, LANES), F32),
        in_specs=[pl.BlockSpec(memory_space=pltpu.VMEM)] * vec,
        out_specs=pl.BlockSpec(memory_space=pltpu.HBM),
        scratch_shapes=[pltpu.SemaphoreType.DMA((vec,))],
        compiler_params=pltpu.CompilerParams(vmem_limit_bytes=24 << 20),
        name="assemble",
    )(*gots)
    return out.reshape(1, rows * LANES // (NY * NX), NY * NX)


def swap_cores(x, orb):
    return lax.ppermute(x, "orb", [(o, o ^ 1) for o in range(orb)])


def shift(x, axis, count):
    n = lax.axis_size(axis)
    return lax.ppermute(x, axis, [(i, (i + count) % n) for i in range(n)])


def responses(orbitals, energies, trial_potential, local_potential):
    orb, vec = lax.axis_size("orb"), lax.axis_size("vec")
    chips = orb // 2
    psis, parts = windows(orbitals, energies, trial_potential, local_potential, orb, vec)
    def to_chip(r):
        perm = [(2 * a + c, 2 * ((a + r) % chips) + c) for a in range(chips) for c in range(2)]
        return lax.ppermute(psis[r], "orb", perm)

    order = [1, chips - 1, *range(2, chips - 1)]
    for r in order:
        psis[r] = to_chip(r)
    for n in range(1, vec):
        parts[n] = shift(parts[n], "vec", n)
    arrived = [psis[r] for r in order]
    own, edge = edges(parts, [])
    near = [(o, o + 1) for o in range(1, orb - 1, 2)] + [(o + 1, o) for o in range(1, orb - 1, 2)]
    edge = lax.ppermute(edge, "orb", near + [(0, 0), (orb - 1, orb - 1)])
    mine = with_edge(own, edge, arrived[:2])
    v, d = potential_rows(mine, swap_cores(mine, orb), vec, [])
    total = None
    for r in [0] + order[:-1]:
        total = solve_window(psis[r], v, d, total, vec)
    last = psis[order[-1]]
    other = swap_cores(solve_window(last, v, d, total, vec, "other"), orb)
    return solve_window(last, v, d, total, vec, "own"), other


def block_body(orbitals, energies, trial_potential, local_potential):
    orb, vec = lax.axis_size("orb"), lax.axis_size("vec")
    ndev = orb * vec
    both = ("orb", "vec")
    own, other = responses(orbitals, energies, trial_potential, local_potential)
    sx = np_basis(NX)
    padded = np.zeros((NX, LANES))
    padded[:, :NX] = sx
    sent = forward_x(own, other, np_split(padded * (4.0 / orb)), ndev)
    got = lax.all_to_all(sent, both, 0, 0, tiled=True)
    sent = spectral(got, orb, vec)
    got = lax.all_to_all(sent, both, 0, 0, tiled=True)
    factor, *slots = back(got, np_split(padded), ndev, vec)
    gots = [slots[0]] + [shift(slots[s], "vec", s) for s in range(1, vec)]
    return assemble(gots), factor


def solution(mesh):
    orb, vec = mesh.shape["orb"], mesh.shape["vec"]
    placed = (P("orb", None, None), P("orb"), P("vec", "orb", None), P("orb", None))

    def body(orbitals, energies, trial_potential, local_potential):
        one = orbitals.shape[0] == 1 and trial_potential.shape[0] == 1
        plan = block_body if one and fits(orb, vec, orb, vec) else general_body
        return plan(orbitals, energies, trial_potential, local_potential)

    return jax.shard_map(
        body, mesh=mesh, in_specs=placed, out_specs=(P("vec", "orb", None), P()), check_vma=False
    )
```

```python
import functools
import math

import jax
import jax.numpy as jnp
import ml_dtypes
import numpy as np
from jax import lax
from jax.experimental import pallas as pl
from jax.experimental.pallas import tpu as pltpu
from jax.sharding import PartitionSpec as P

NZ = 96
NY = 96
NX = 96
STEPS = 4

BF16 = jnp.bfloat16
F32 = jnp.float32
LANES = 128
WEIGHTS = [1.0 / (1.0 + 0.8 * math.cos(math.pi * (2 * s + 1) / (2 * STEPS))) for s in range(STEPS)]

SCALES = [WEIGHTS[0]]
for weight_ in WEIGHTS[1:]:
    SCALES.append((1.0 - weight_) * SCALES[-1])
COEFFICIENTS = [None] + [
    (1.0, WEIGHTS[s] / SCALES[s], WEIGHTS[s] * SCALES[s - 1] / SCALES[s]) for s in range(1, STEPS)
]


def neighbours(field):
    depth, flat = field.shape
    zero_plane = jnp.zeros((1, flat), field.dtype)
    total = jnp.concatenate([zero_plane, field[:-1]], 0) + jnp.concatenate(
        [field[1:], zero_plane], 0
    )
    zero_rows = jnp.zeros((depth, NX), field.dtype)
    total = (
        total
        + jnp.concatenate([zero_rows, field[:, :-NX]], 1)
        + jnp.concatenate([field[:, NX:], zero_rows], 1)
    )
    column = jnp.arange(flat) % NX
    zero_col = jnp.zeros((depth, 1), field.dtype)
    left = jnp.concatenate([zero_col, field[:, :-1]], 1) * (column > 0).astype(field.dtype)
    right = jnp.concatenate([field[:, 1:], zero_col], 1) * (column < NX - 1).astype(field.dtype)
    return total + left + right


def solve(psi, perturb, potential, energy):
    diag = 3.25 + potential - energy
    source = -perturb * psi
    answer = jnp.zeros_like(psi)
    for step in range(STEPS):
        weight = 1.0 / (1.0 + 0.8 * jnp.cos(jnp.pi * (2 * step + 1) / (2 * STEPS)))
        applied = diag * answer - 0.5 * neighbours(answer)
        answer = answer + weight * (source - applied) / diag
    return answer


def sine_basis(count):
    index = jnp.arange(count, dtype=jnp.float32) + 1.0
    return jnp.sqrt(2.0 / (count + 1)) * jnp.sin(
        jnp.pi * index[:, None] * index[None, :] / (count + 1)
    )


def eigen_of(position, count):
    return 2.0 - 2.0 * jnp.cos(jnp.pi * (position.astype(jnp.float32) + 1.0) / (count + 1))


def planes(field):
    high = lax.Precision.HIGHEST
    depth = field.shape[0]
    cube = field.reshape(depth, NY, NX)
    cube = jnp.einsum("zyx,cx->zyc", cube, sine_basis(NX), precision=high)
    cube = jnp.einsum("zyc,by->zbc", cube, sine_basis(NY), precision=high)
    return cube.reshape(depth, NY * NX)


def scale_columns(columns, start):
    high = lax.Precision.HIGHEST
    width = columns.shape[1]
    position = start + jnp.arange(width)
    denom = (
        eigen_of(jnp.arange(NZ), NZ)[:, None]
        + eigen_of(position // NX, NY)[None, :]
        + eigen_of(position % NX, NX)[None, :]
    )
    basis = sine_basis(NZ)
    spectral = jnp.dot(basis, columns, precision=high) * (jnp.sqrt(4.0 * jnp.pi) / jnp.sqrt(denom))
    return jnp.dot(basis, spectral, precision=high)


def coulomb_slab(slab):
    columns = lax.all_to_all(planes(slab), "orb", split_axis=1, concat_axis=0, tiled=True)
    scaled = scale_columns(columns, lax.axis_index("orb") * columns.shape[1])
    back = lax.all_to_all(scaled, "orb", split_axis=0, concat_axis=1, tiled=True)
    return planes(back)


def factorize(partial_gram):
    lower = jnp.linalg.cholesky(partial_gram / (NZ * NY * NX))
    inverse = lax.linalg.triangular_solve(
        lower, jnp.eye(lower.shape[0], dtype=jnp.float32), left_side=True, lower=True
    )
    return (lower, inverse)


def general_body(orbitals, energies, trial_potential, local_potential):
    high = lax.Precision.HIGHEST
    depth = local_potential.shape[0]
    plane_cells = local_potential.shape[1]
    vector_slab = trial_potential.reshape(depth, plane_cells)
    perturb_full, potential_full = (
        lax.all_gather(vector_slab, "orb", axis=0, tiled=True),
        lax.all_gather(local_potential, "orb", axis=0, tiled=True),
    )
    perturb = perturb_full.astype(jnp.float32)
    potential = potential_full.astype(jnp.float32)
    weight = 4.0 / (orbitals.shape[0] * lax.axis_size("orb"))
    psi = orbitals[0].astype(jnp.float32)
    partial_value = psi * solve(psi, perturb, potential, energies[0])
    partial_value = partial_value * weight
    slab = lax.psum_scatter(partial_value, "orb", scatter_dimension=0, tiled=True)
    slab = coulomb_slab(slab)
    mine = slab.reshape(1, depth, plane_cells)
    gathered = lax.all_gather(mine, "vec", axis=0, tiled=True)
    flat = gathered.reshape(gathered.shape[0], depth * plane_cells)
    partial_gram = jnp.dot(flat, flat.T, precision=high)
    lower, inverse = factorize(lax.psum(partial_gram, "orb"))
    row = lax.dynamic_slice_in_dim(inverse, lax.axis_index("vec"), 1, 0)
    ortho = jnp.dot(row, flat, precision=high).reshape(1, depth, plane_cells)
    return (ortho, lower.T)


TILES = 3
GROUP = 4
SUB = 8
ROWS = GROUP * SUB
WTILES = TILES * SUB
HALO = STEPS - 1
TAILS = 4


def fits(orb, vec, norb, nv):
    return (
        norb == orb
        and nv == vec
        and orb % 2 == 0
        and NZ % orb == 0
        and NZ // orb >= 4
        and NZ // orb % 2 == 0
        and NY == vec * (ROWS - 2 * GROUP)
        and NY == TILES * ROWS
        and vec * ROWS == LANES
        and NX * GROUP == TILES * LANES
        and NX % (orb * vec) == 0
        and NZ % (orb * vec) == 0
        and STEPS <= GROUP
        and NZ // orb == TAILS * TILES
        and vec == GROUP
    )


def split(x):
    high = x.astype(BF16)
    return high, (x - high.astype(F32)).astype(BF16)


def np_split(x):
    x = np.asarray(x, np.float64)
    high = x.astype(ml_dtypes.bfloat16)
    return np.stack([high, (x - high.astype(np.float64)).astype(ml_dtypes.bfloat16)])


def dot3(a, b, dims):
    one = functools.partial(
        lax.dot_general, dimension_numbers=(dims, ((), ())), preferred_element_type=F32
    )
    if dims[0] == (1,) and a[0].shape[1] == LANES:
        return one(jnp.concatenate([a[0], a[0], a[1]], 1), jnp.concatenate([b[0], b[1], b[0]], dims[1][0]))
    return one(a[0], b[0]) + (one(a[0], b[1]) + one(a[1], b[0]))


def np_basis(count):
    index = np.arange(count, dtype=np.float64) + 1.0
    return np.sqrt(2.0 / (count + 1)) * np.sin(np.pi * np.outer(index, index) / (count + 1))


def np_eigen(count):
    return 4.0 * np.sin(np.pi * (np.arange(count, dtype=np.float64) + 1.0) / (2 * (count + 1))) ** 2


def to_rows(tiles):
    lane = lax.broadcasted_iota(jnp.int32, tiles[0].shape, 1)
    a, b, c = tiles
    return [
        a,
        pltpu.roll(jnp.where(lane >= 96, a, b), 32, 1),
        pltpu.roll(jnp.where(lane >= 64, b, c), 64, 1),
        pltpu.roll(c, 96, 1),
    ]


def to_tiles(rows):
    lane = lax.broadcasted_iota(jnp.int32, rows[0].shape, 1)
    r1, r2 = pltpu.roll(rows[1], 96, 1), pltpu.roll(rows[2], 64, 1)
    return [
        jnp.where(lane < 96, rows[0], r1),
        jnp.where(lane < 64, r1, r2),
        jnp.where(lane < 32, r2, pltpu.roll(rows[3], 32, 1)),
    ]


def first_tile(strip):
    return strip * (WTILES - 2 * TILES) - TILES


def window_start(strip):
    return jnp.clip(first_tile(strip), 0, NY * NX // LANES - WTILES)


def tile_lanes(strip, t, start=0):
    tile = jnp.clip(first_tile(strip) + t, 0, NY * NX // LANES - 1) - start
    return pl.ds(pl.multiple_of(tile * LANES, LANES), LANES)


def pack_planes(src, plane, out, pairs):
    def one(pair, carry):
        for i in range(TILES):
            top = pl.multiple_of((plane + 2 * pair) * WTILES + i * SUB, SUB)
            low = pl.multiple_of((plane + 2 * pair + 1) * WTILES + i * SUB, SUB)
            block = jnp.concatenate([src[pl.ds(top, SUB), :], src[pl.ds(low, SUB), :]], 0)
            out[pair, i] = block.astype(BF16)
        return carry

    lax.fori_loop(0, pairs, one, 0)


def windows_kernel(orb, vec, energy_any, psi_any, v_any, pot_any, *refs):
    outs, (planes_ref, more_ref, pot_rows_ref, psi_ref, v_ref, pot_ref, energy_ref, sem) = refs[:-8], refs[-8:]
    tiles = NY * NX // LANES
    chips = orb // 2
    slab = NZ // chips
    depth = v_ref.shape[0]
    chip = lax.axis_index("orb") // 2
    strip = lax.axis_index("vec")
    start = window_start(strip)
    lanes = pl.ds(pl.multiple_of(start * LANES, LANES), WTILES * LANES)
    copies = [
        pltpu.make_async_copy(v_any.at[0], v_ref, sem.at[0]),
        pltpu.make_async_copy(pot_any.at[:, lanes], pot_ref, sem.at[1]),
        pltpu.make_async_copy(psi_any.at[0, :, lanes], psi_ref, sem.at[2]),
        pltpu.make_async_copy(energy_any, energy_ref, sem.at[3]),
    ]
    for copy in copies:
        copy.start()
    more_ref[:SUB, :] = jnp.zeros((SUB, LANES), F32)
    more_ref[SUB + depth * tiles :, :] = jnp.zeros((SUB, LANES), F32)
    for copy in copies[:2]:
        copy.wait()
    for tile in range(tiles):
        more_ref[pl.ds(SUB + tile, depth, tiles), :] = v_ref[:, tile * LANES : (tile + 1) * LANES].astype(F32)
    for t in range(WTILES):
        row = (t % TILES) * SUB + t // TILES
        pot_rows_ref[pl.ds(row, depth, WTILES), :] = pot_ref[:, tile_lanes(strip, t, start)].astype(F32)
    for n in range(vec):
        first = SUB + first_tile(lax.rem(strip + n, vec))
        for pair in range(depth // 2):
            for i in range(TILES):
                block = [more_ref[pl.ds(first + i + (2 * pair + zz) * tiles, SUB, TILES), :] for zz in range(2)]
                outs[chips + n][pair, i] = jnp.concatenate(block, 0).astype(BF16)
    pack_planes(pot_rows_ref, 0, outs[chips + vec], depth // 2)
    zero = jnp.zeros((HALO * WTILES, LANES), F32)
    planes_ref[: HALO * WTILES, :] = zero
    planes_ref[(NZ + HALO) * WTILES :, :] = zero
    for copy in copies[2:]:
        copy.wait()
    for t in range(WTILES):
        row = HALO * WTILES + (t % TILES) * SUB + t // TILES
        planes_ref[pl.ds(row, NZ, WTILES), :] = psi_ref[:, tile_lanes(strip, t, start)].astype(F32)
    energy = jnp.full((1, LANES), energy_ref[0], F32)
    high = energy.astype(BF16).astype(F32)
    middle = (energy - high).astype(BF16).astype(F32)
    low = energy - high - middle
    lane = lax.broadcasted_iota(jnp.int32, (1, LANES), 1)
    for at in range(chips):
        row = at * slab * WTILES
        held = planes_ref[row : row + 1, :]
        held = jnp.where(lane == 0, high, jnp.where(lane == 1, middle, jnp.where(lane == 2, low, held)))
        planes_ref[row : row + 1, :] = held
    for shift in range(chips):
        pack_planes(planes_ref, ((chip + shift) % chips) * slab, outs[shift], (slab + 2 * HALO) // 2)


def windows(orbitals, energies, trial, potential, orb, vec):
    chips = orb // 2
    depth = potential.shape[0]
    block = (TILES, 2 * SUB, LANES)
    pairs = (NZ // chips + 2 * HALO) // 2
    outs = [jax.ShapeDtypeStruct((pairs, *block), BF16)] * chips
    outs += [jax.ShapeDtypeStruct((depth // 2, *block), BF16)] * (vec + 1)
    got = pl.pallas_call(
        functools.partial(windows_kernel, orb, vec),
        out_shape=outs,
        in_specs=[pl.BlockSpec(memory_space=pl.ANY)] + [pl.BlockSpec(memory_space=pltpu.HBM)] * 3,
        out_specs=[pl.BlockSpec(memory_space=pltpu.VMEM)] * len(outs),
        scratch_shapes=[
            pltpu.VMEM(((NZ + 2 * HALO) * WTILES, LANES), F32),
            pltpu.VMEM((depth * NY * NX // LANES + 2 * SUB, LANES), F32),
            pltpu.VMEM((depth * WTILES, LANES), F32),
            pltpu.VMEM((NZ, WTILES * LANES), BF16),
            pltpu.VMEM((depth, NY * NX), BF16),
            pltpu.VMEM((depth, WTILES * LANES), BF16),
            pltpu.SMEM((1,), F32),
            pltpu.SemaphoreType.DMA((4,)),
        ],
        compiler_params=pltpu.CompilerParams(vmem_limit_bytes=24 << 20),
        name="windows",
    )(energies, *(pltpu.with_memory_space_constraint(x, pltpu.HBM) for x in (orbitals, trial, potential)))
    return list(got[:chips]), list(got[chips:])


def edges_kernel(n, parts_and_more, *refs):
    parts, (own_ref, edge_ref) = refs[:n], refs[parts_and_more:]
    core = lax.axis_index("orb") % 2
    first = core * (own_ref.shape[1] - edge_ref.shape[1])
    for i, part in enumerate(parts):
        own_ref[i] = part[...]
        edge_ref[i] = part[pl.ds(first, edge_ref.shape[1])]


def edges(parts, arrived):
    pairs, *block = parts[0].shape
    n = len(parts)
    more = n + len(arrived)
    return pl.pallas_call(
        functools.partial(edges_kernel, n, more),
        out_shape=[
            jax.ShapeDtypeStruct((n, pairs, *block), BF16),
            jax.ShapeDtypeStruct((n, GROUP // 2, *block), BF16),
        ],
        in_specs=[pl.BlockSpec(memory_space=pltpu.VMEM)] * more,
        out_specs=[pl.BlockSpec(memory_space=pltpu.VMEM)] * 2,
        compiler_params=pltpu.CompilerParams(vmem_limit_bytes=24 << 20),
        name="edges",
    )(*parts, *arrived)


def with_edge_kernel(n, own_ref, edge_ref, *refs):
    out_ref = refs[n]
    core = lax.axis_index("orb") % 2
    pairs, edge = own_ref.shape[1], edge_ref.shape[1]
    out_ref[:, pl.ds((1 - core) * edge, pairs)] = own_ref[...]
    out_ref[:, pl.ds(core * pairs, edge)] = edge_ref[...]


def with_edge(own, edge, arrived):
    n, pairs, *block = own.shape
    return pl.pallas_call(
        functools.partial(with_edge_kernel, len(arrived)),
        out_shape=jax.ShapeDtypeStruct((n, pairs + edge.shape[1], *block), own.dtype),
        in_specs=[pl.BlockSpec(memory_space=pltpu.VMEM)] * (2 + len(arrived)),
        out_specs=pl.BlockSpec(memory_space=pltpu.VMEM),
        compiler_params=pltpu.CompilerParams(vmem_limit_bytes=24 << 20),
        name="with_edge",
    )(own, edge, *arrived)


def potential_rows_kernel(vec, n, mine_ref, other_ref, *refs):
    v_ref, d_ref = refs[n:]
    core = lax.axis_index("orb") % 2
    strip = lax.axis_index("vec")
    pairs = mine_ref.shape[1]
    for src, first in ((mine_ref, core * pairs), (other_ref, (1 - core) * pairs)):

        def one(pair, carry, src=src, first=first):
            plane = 2 * (first + pair)
            for n in range(vec + 1):
                rows = to_rows([src[n, pair, i].astype(F32) for i in range(TILES)])
                for zz in range(2):
                    block = jnp.concatenate([rows[i][zz * SUB : (zz + 1) * SUB] for i in range(GROUP)], 0)
                    if n < vec:
                        k = lax.rem(strip - n + vec, vec)
                        v_ref[plane + zz, pl.ds(pl.multiple_of(k * ROWS, ROWS), ROWS), :] = block
                    else:
                        d_ref[plane + zz] = 3.25 + block
            return carry

        lax.fori_loop(0, pairs, one, 0, unroll=True)


def potential_rows(mine, other, vec, arrived):
    planes = 4 * mine.shape[1]
    return pl.pallas_call(
        functools.partial(potential_rows_kernel, vec, len(arrived)),
        out_shape=[
            jax.ShapeDtypeStruct((planes, vec * ROWS, LANES), F32),
            jax.ShapeDtypeStruct((planes, ROWS, LANES), F32),
        ],
        in_specs=[pl.BlockSpec(memory_space=pltpu.VMEM)] * (2 + len(arrived)),
        out_specs=[pl.BlockSpec(memory_space=pltpu.VMEM)] * 2,
        compiler_params=pltpu.CompilerParams(vmem_limit_bytes=24 << 20),
        name="potential_rows",
    )(mine, other, *arrived)


def solve_kernel(vec, first, part, *refs):
    psi_ref, v_ref, d_ref = refs[:3]
    refs = refs[3:]
    sum_ref = None if first else refs[0]
    out_ref, psi_s, h_s, c_s, u_a, u_b = refs[-6:]
    planes = d_ref.shape[0]
    depth = (planes - 2 * GROUP) // 2
    core = lax.axis_index("orb") % 2
    begins = {None: 0, "own": core * depth, "other": (1 - core) * depth}[part]
    count = 2 * depth if part is None else depth
    top = (lax.axis_index("orb") // 2) * 2 * depth - GROUP
    top_row = lax.axis_index("vec") * (ROWS - 2 * GROUP) - GROUP
    lane = lax.broadcasted_iota(jnp.int32, (SUB, LANES), 1)
    group = lax.broadcasted_iota(jnp.int32, (SUB, LANES), 0)
    inside = []
    for i in range(GROUP):
        y = top_row + group * GROUP + i
        inside.append(jnp.where((y >= 0) & (y < NY) & (lane < NX), 0.5, 0.0))
    inside = jnp.concatenate(inside, 0)
    block = psi_ref[0, 0].astype(F32)
    energy = block[0:1, 0:1] + block[0:1, 1:2] + block[0:1, 2:3]
    at = lax.broadcasted_iota(jnp.int32, (2 * LANES, LANES), 0) % LANES
    to = lax.broadcasted_iota(jnp.int32, (2 * LANES, LANES), 1)
    beside = jnp.where((at == to - 1) | (at == to + 1), 1.0, 0.0).astype(BF16)

    def begin(pair, carry):
        rows = to_rows([psi_ref[begins // 2 + pair, i].astype(F32) for i in range(TILES)])
        for zz in range(2):
            w = GROUP - HALO + begins + 2 * pair + zz
            z = top + w
            there = jnp.where((z >= 0) & (z < NZ), 1.0, 0.0)
            psi = jnp.concatenate([rows[i][zz * SUB : (zz + 1) * SUB] for i in range(GROUP)], 0)
            h = inside * there / (d_ref[w] - energy)
            psi_s[w] = SCALES[STEPS - 1] * psi
            h_s[w] = h
            scaled = -2.0 * psi * h
            for k in range(vec):
                rows_k = pl.ds(k * ROWS, ROWS)
                c_s[w, rows_k, :] = scaled * v_ref[w, rows_k, :]
        return carry

    lax.fori_loop(0, (count + 2 * HALO) // 2, begin, 0, unroll=True)

    def stepped(src, w, step):
        u = src[w]
        high, low = split(u)
        x = jnp.dot(jnp.concatenate([high, low], 1), beside, preferred_element_type=F32)
        near = x + (src[w - 1] + src[w + 1])
        own, given, around = COEFFICIENTS[step]
        h = around * h_s[w]
        new = []
        for k in range(vec):
            rows = [u[k * ROWS + i * SUB : k * ROWS + (i + 1) * SUB] for i in range(GROUP)]
            north = jnp.concatenate([pltpu.roll(rows[-1], 1, 0)] + rows[:-1], 0)
            south = jnp.concatenate(rows[1:] + [pltpu.roll(rows[0], SUB - 1, 0)], 0)
            at_k = slice(k * ROWS, (k + 1) * ROWS)
            change = h * (near[at_k] + (north + south))
            if src is c_s:
                new.append((own + given) * u[at_k] + change)
            else:
                new.append((u[at_k] + given * c_s[w, at_k, :]) + change)
        return new

    src, dst = c_s, u_a
    for step in range(1, STEPS - 1):
        low = GROUP - HALO + step

        def middle(p, carry, src=src, dst=dst, step=step, low=low):
            w = begins + low + p
            dst[w] = jnp.concatenate(stepped(src, w, step), 0)
            return carry

        lax.fori_loop(0, count + 2 * (HALO - step), middle, 0, unroll=True)
        src, dst = dst, (u_b if dst is u_a else u_a)

    def end(p, carry, src=src):
        w = GROUP + begins + p
        psi = psi_s[w]
        total = jnp.concatenate([psi * new for new in stepped(src, w, STEPS - 1)], 0)
        if not first:
            total = total + sum_ref[begins + p]
        out_ref[p] = total
        return carry

    lax.fori_loop(0, count, end, 0, unroll=True)


def solve_window(psi, v, d, total, vec, part=None):
    planes = d.shape[0]
    depth = (planes - 2 * GROUP) // 2
    args = (psi, v, d) if total is None else (psi, v, d, total)
    return pl.pallas_call(
        functools.partial(solve_kernel, vec, total is None, part),
        out_shape=jax.ShapeDtypeStruct((2 * depth if part is None else depth, LANES, LANES), F32),
        in_specs=[pl.BlockSpec(memory_space=pltpu.VMEM)] * len(args),
        out_specs=pl.BlockSpec(memory_space=pltpu.VMEM),
        scratch_shapes=[pltpu.VMEM((planes, ROWS, LANES), F32)] * 2
        + [pltpu.VMEM((planes, vec * ROWS, LANES), F32)] * 3,
        compiler_params=pltpu.CompilerParams(vmem_limit_bytes=32 << 20),
        name="solve_window",
    )(*args)


def forward_x_kernel(ndev, basis_ref, own_ref, other_ref, out_ref):
    depth = own_ref.shape[0] // LANES
    inner = depth - depth // TAILS
    rows = out_ref.shape[0] // ndev
    vecrows = LANES // SUB
    basis = (basis_ref[0], basis_ref[1])
    lane = lax.broadcasted_iota(jnp.int32, (NX, LANES), 1)
    pad = jnp.zeros((LANES - (SUB - 2) * vecrows, LANES), F32)
    got = []
    for z in range(depth):
        groups = [pl.ds(z * LANES + g, vecrows, SUB) for g in range(1, SUB - 1)]
        chi = jnp.concatenate([own_ref[g, :] + other_ref[g, :] for g in groups] + [pad], 0)
        got.append(dot3(basis, split(chi), ((1,), (1,))))
    for z in range(inner):
        whole, third = inner + z // TILES, z % TILES
        tail = pltpu.roll(got[whole], LANES - LANES // TAILS * (third + 1), 1)
        row = jnp.where(lane < LANES - LANES // TAILS, got[z], tail)
        for part in range(NX // ndev):
            out_ref[pl.ds(part * inner + z, ndev, rows), :] = row[part * ndev : (part + 1) * ndev]


def forward_x(own, other, basis, ndev):
    depth = own.shape[0]
    rows = -(-(NX // ndev) * (depth - depth // TAILS) // 4) * 4
    out = pl.pallas_call(
        functools.partial(forward_x_kernel, ndev),
        out_shape=jax.ShapeDtypeStruct((ndev * rows, LANES), F32),
        in_specs=[pl.BlockSpec(memory_space=pltpu.VMEM)] * 3,
        out_specs=pl.BlockSpec(memory_space=pltpu.VMEM),
        compiler_params=pltpu.CompilerParams(vmem_limit_bytes=24 << 20),
        name="forward_x",
    )(basis, own.reshape(-1, LANES), other.reshape(-1, LANES))
    return out.reshape(ndev, rows // 4, 4, LANES)


def spectral_kernel(orb, vec, rows, mux_ref, muzy_ref, wy_ref, kz_ref, kzb_ref, wyb_ref, got_ref, out_ref):
    ndev = orb * vec
    parts = NX // ndev
    me = lax.axis_index("orb") * vec + lax.axis_index("vec")
    inner = NZ // orb - NZ // orb // TAILS
    lane = lax.broadcasted_iota(jnp.int32, (orb, LANES), 1)
    strips = []
    for v in range(vec):
        main = [got_ref[pl.ds(v * rows + r, orb, vec * rows), :] for r in range(parts * inner)]
        tails = []
        for r in range(0, parts * inner, TILES):
            tail = pltpu.roll(main[r], LANES // TAILS, 1)
            for p in range(1, TILES):
                third = pltpu.roll(main[r + p], (p + 1) * LANES // TAILS, 1)
                tail = jnp.where(lane >= p * LANES // TAILS, third, tail)
            tails.append(tail)
        strips.append(jnp.concatenate(main + tails, 0))
    mm = ((1,), (0,))
    t = dot3(split(jnp.concatenate(strips, 1)), (wy_ref[0], wy_ref[1]), mm)
    t = dot3((kz_ref[0], kz_ref[1]), split(t), mm)
    scale = jnp.concatenate(
        [
            math.sqrt(4.0 * math.pi) / jnp.sqrt(muzy_ref[...] + mux_ref[part * ndev + me])
            for part in range(parts)
        ],
        0,
    )
    fields = [t[:, k * LANES : (k + 1) * LANES] * scale for k in range(vec)]
    lane = lax.broadcasted_iota(jnp.int32, (1, LANES), 1)
    gram = jnp.zeros((1, LANES), F32)
    for k in range(vec):
        for l in range(k + 1):
            entry = jnp.sum(jnp.sum(fields[k] * fields[l], axis=0, keepdims=True), axis=1, keepdims=True)
            gram = jnp.where(lane == k * vec + l, entry, gram)
    t = jnp.concatenate(fields, 1)
    t = jnp.concatenate(
        [dot3((kzb_ref[0], kzb_ref[1]), split(t[part * NZ : (part + 1) * NZ]), mm) for part in range(parts)], 0
    )
    t = dot3(split(t), (wyb_ref[0], wyb_ref[1]), mm)
    rows = out_ref.shape[0] // ndev
    zs = NZ // ndev
    for part in range(parts):
        for z in range(zs):
            for yt in range(TILES):
                out_ref[pl.ds((z * parts + part) * TILES + yt, ndev, rows), :] = t[
                    (part * zs + z) * ndev : (part * zs + z + 1) * ndev, yt * LANES : (yt + 1) * LANES
                ]
    out_ref[pl.ds(zs * parts * TILES, ndev, rows), :] = jnp.broadcast_to(gram, (ndev, LANES))


def spectral(got, orb, vec):
    ndev = orb * vec
    parts, zs = NX // ndev, NZ // ndev
    depth = NZ // orb
    quarter = depth // TAILS
    inner = depth - quarter
    strip = ROWS - 2 * GROUP
    rows_in = got.shape[1] * got.shape[2]
    rows_out = -(-(parts * zs * TILES + 1) // 4) * 4
    sy, sz = np_basis(NY), np_basis(NZ)
    wy = np.zeros((vec, LANES, vec, LANES))
    wyb = np.zeros((vec, LANES, TILES, vec, GROUP, SUB))
    for k in range(vec):
        for i in range(GROUP):
            for g in range(SUB):
                for v in range(vec):
                    if g < SUB - 2:
                        wy[v, (g * vec + k) * GROUP + i, k, :NY] = sy[v * strip + GROUP * g + i]
                for yt in range(TILES):
                    wyb[k, :NY, yt, k, i, g] = sy[yt * ROWS + GROUP * g + i]
    wy = wy.reshape(vec * LANES, vec * LANES)
    wyb = wyb.reshape(vec * LANES, TILES * LANES)
    kz = np.zeros((parts, NZ, parts, inner, orb))
    kzt = np.zeros((parts, NZ, parts, quarter, orb))
    for part in range(parts):
        for o in range(orb):
            mine = sz[:, o * depth : (o + 1) * depth]
            kz[part, :, part, :, o] = mine[:, :inner]
            kzt[part, :, part, :, o] = mine[:, inner:]
    kz = np.concatenate([kz.reshape(parts * NZ, -1), kzt.reshape(parts * NZ, -1)], 1)
    kzb = np.concatenate([sz[z::zs] for z in range(zs)])
    muzy = np.ones((NZ, LANES), np.float32)
    muzy[:, :NY] = np_eigen(NZ)[:, None] + np_eigen(NY)[None, :]
    mux = np_eigen(NX).astype(np.float32)
    out = pl.pallas_call(
        functools.partial(spectral_kernel, orb, vec, rows_in),
        out_shape=jax.ShapeDtypeStruct((ndev * rows_out, LANES), F32),
        in_specs=[pl.BlockSpec(memory_space=pltpu.SMEM)] + [pl.BlockSpec(memory_space=pltpu.VMEM)] * 6,
        out_specs=pl.BlockSpec(memory_space=pltpu.VMEM),
        compiler_params=pltpu.CompilerParams(vmem_limit_bytes=32 << 20),
        name="spectral",
    )(mux, muzy, np_split(wy), np_split(kz), np_split(kzb), np_split(wyb), got.reshape(-1, LANES))
    return out.reshape(ndev, rows_out // 4, 4, LANES)


def back_kernel(ndev, vec, basis_ref, got_ref, factor_ref, *outs):
    parts, zs = NX // ndev, NZ // ndev
    rows = got_ref.shape[0] // ndev
    strip = lax.axis_index("vec")
    basis = (basis_ref[0], basis_ref[1])
    gram = jnp.sum(got_ref[pl.ds(zs * parts * TILES, ndev, rows), :], axis=0, keepdims=True)
    gram = gram / (NZ * NY * NX)
    entry = lambda k, l: gram[:, k * vec + l : k * vec + l + 1]
    lower = [[None] * vec for _ in range(vec)]
    inverse = [[jnp.zeros((1, 1), F32)] * vec for _ in range(vec)]
    for l in range(vec):
        pivot = entry(l, l)
        for m in range(l):
            pivot = pivot - lower[l][m] * lower[l][m]
        lower[l][l] = jnp.sqrt(pivot)
        inverse[l][l] = 1.0 / lower[l][l]
        for k in range(l + 1, vec):
            value = entry(k, l)
            for m in range(l):
                value = value - lower[k][m] * lower[l][m]
            lower[k][l] = value * inverse[l][l]
    for l in range(vec):
        for k in range(l + 1, vec):
            value = lower[k][l] * inverse[l][l]
            for m in range(l + 1, k):
                value = value + lower[k][m] * inverse[m][l]
            inverse[k][l] = -value * inverse[k][k]
    at_row = lax.broadcasted_iota(jnp.int32, (vec, vec), 0)
    at_col = lax.broadcasted_iota(jnp.int32, (vec, vec), 1)
    factor = jnp.zeros((vec, vec), F32)
    for k in range(vec):
        for l in range(k + 1):
            factor = jnp.where((at_row == l) & (at_col == k), lower[k][l], factor)
    factor_ref[...] = factor
    coefficients = []
    for s in range(vec):
        to = lax.rem(strip + s, vec)
        line = []
        for k in range(vec):
            value = inverse[0][k]
            for m in range(1, vec):
                value = jnp.where(to == m, inverse[m][k], value)
            line.append(value)
        coefficients.append(line)
    for z in range(zs):
        for yt in range(TILES):
            x = jnp.concatenate(
                [
                    got_ref[pl.ds((z * parts + part) * TILES + yt, ndev, rows), :]
                    for part in range(parts)
                ],
                0,
            )
            y = dot3(split(x), basis, ((0,), (0,)))
            for s in range(vec):
                mixed = coefficients[s][0] * y[:ROWS]
                for k in range(1, vec):
                    mixed = mixed + coefficients[s][k] * y[k * ROWS : (k + 1) * ROWS]
                tiles = to_tiles([mixed[i * SUB : (i + 1) * SUB] for i in range(GROUP)])
                for i in range(TILES):
                    outs[s][pl.ds((z * TILES + yt) * WTILES + i, SUB, TILES), :] = tiles[i]


def back(got, basis, ndev, vec):
    zs = NZ // ndev
    tiles = NY * NX // LANES
    return pl.pallas_call(
        functools.partial(back_kernel, ndev, vec),
        out_shape=[jax.ShapeDtypeStruct((vec, vec), F32)]
        + [jax.ShapeDtypeStruct((zs * tiles, LANES), F32)] * vec,
        in_specs=[pl.BlockSpec(memory_space=pltpu.VMEM)] * 2,
        out_specs=[pl.BlockSpec(memory_space=pltpu.VMEM)] * (vec + 1),
        compiler_params=pltpu.CompilerParams(vmem_limit_bytes=24 << 20),
        name="back",
    )(basis, got.reshape(-1, LANES))


def assemble_kernel(vec, *refs):
    gots, (out_any, sem) = refs[:vec], refs[vec:]
    strip = lax.axis_index("vec")
    rows = gots[0].shape[0]
    copies = []
    for s in range(vec):
        start = pl.multiple_of(lax.rem(strip - s + vec, vec) * rows, 8)
        copies.append(pltpu.make_async_copy(gots[s], out_any.at[pl.ds(start, rows)], sem.at[s]))
    for copy in copies:
        copy.start()
    for copy in copies:
        copy.wait()


def assemble(gots):
    vec = len(gots)
    rows = gots[0].shape[0] * vec
    out = pl.pallas_call(
        functools.partial(assemble_kernel, vec),
        out_shape=jax.ShapeDtypeStruct((rows, LANES), F32),
        in_specs=[pl.BlockSpec(memory_space=pltpu.VMEM)] * vec,
        out_specs=pl.BlockSpec(memory_space=pltpu.HBM),
        scratch_shapes=[pltpu.SemaphoreType.DMA((vec,))],
        compiler_params=pltpu.CompilerParams(vmem_limit_bytes=24 << 20),
        name="assemble",
    )(*gots)
    return out.reshape(1, rows * LANES // (NY * NX), NY * NX)


def swap_cores(x, orb):
    return lax.ppermute(x, "orb", [(o, o ^ 1) for o in range(orb)])


def shift(x, axis, count):
    n = lax.axis_size(axis)
    return lax.ppermute(x, axis, [(i, (i + count) % n) for i in range(n)])


def responses(orbitals, energies, trial_potential, local_potential):
    orb, vec = lax.axis_size("orb"), lax.axis_size("vec")
    chips = orb // 2
    psis, parts = windows(orbitals, energies, trial_potential, local_potential, orb, vec)
    def to_chip(r):
        perm = [(2 * a + c, 2 * ((a + r) % chips) + c) for a in range(chips) for c in range(2)]
        return lax.ppermute(psis[r], "orb", perm)

    order = [1, chips - 1, *range(2, chips - 1)]
    for r in order:
        psis[r] = to_chip(r)
    for n in range(1, vec):
        parts[n] = shift(parts[n], "vec", n)
    arrived = [psis[r] for r in order]
    own, edge = edges(parts, [])
    near = [(o, o + 1) for o in range(1, orb - 1, 2)] + [(o + 1, o) for o in range(1, orb - 1, 2)]
    edge = lax.ppermute(edge, "orb", near + [(0, 0), (orb - 1, orb - 1)])
    mine = with_edge(own, edge, arrived[:2])
    v, d = potential_rows(mine, swap_cores(mine, orb), vec, [])
    total = None
    for r in [0] + order[:-1]:
        total = solve_window(psis[r], v, d, total, vec)
    last = psis[order[-1]]
    other = swap_cores(solve_window(last, v, d, total, vec, "other"), orb)
    return solve_window(last, v, d, total, vec, "own"), other


def block_body(orbitals, energies, trial_potential, local_potential):
    orb, vec = lax.axis_size("orb"), lax.axis_size("vec")
    ndev = orb * vec
    both = ("orb", "vec")
    own, other = responses(orbitals, energies, trial_potential, local_potential)
    sx = np_basis(NX)
    padded = np.zeros((NX, LANES))
    padded[:, :NX] = sx
    sent = forward_x(own, other, np_split(padded * (4.0 / orb)), ndev)
    got = lax.all_to_all(sent, both, 0, 0, tiled=True)
    sent = spectral(got, orb, vec)
    got = lax.all_to_all(sent, both, 0, 0, tiled=True)
    factor, *slots = back(got, np_split(padded), ndev, vec)
    gots = [slots[0]] + [shift(slots[s], "vec", s) for s in range(1, vec)]
    return assemble(gots), factor


def solution(mesh):
    orb, vec = mesh.shape["orb"], mesh.shape["vec"]
    placed = (P("orb", None, None), P("orb"), P("vec", "orb", None), P("orb", None))

    def body(orbitals, energies, trial_potential, local_potential):
        one = orbitals.shape[0] == 1 and trial_potential.shape[0] == 1
        plan = block_body if one and fits(orb, vec, orb, vec) else general_body
        return plan(orbitals, energies, trial_potential, local_potential)

    return jax.shard_map(
        body, mesh=mesh, in_specs=placed, out_specs=(P("vec", "orb", None), P()), check_vma=False
    )
```

```python
import functools
import math

import jax
import jax.numpy as jnp
import ml_dtypes
import numpy as np
from jax import lax
from jax.experimental import pallas as pl
from jax.experimental.pallas import tpu as pltpu
from jax.sharding import PartitionSpec as P

NZ = 96
NY = 96
NX = 96
STEPS = 4

BF16 = jnp.bfloat16
F32 = jnp.float32
LANES = 128
WEIGHTS = [1.0 / (1.0 + 0.8 * math.cos(math.pi * (2 * s + 1) / (2 * STEPS))) for s in range(STEPS)]

SCALES = [WEIGHTS[0]]
for weight_ in WEIGHTS[1:]:
    SCALES.append((1.0 - weight_) * SCALES[-1])
COEFFICIENTS = [None] + [
    (1.0, WEIGHTS[s] / SCALES[s], WEIGHTS[s] * SCALES[s - 1] / SCALES[s]) for s in range(1, STEPS)
]


def neighbours(field):
    depth, flat = field.shape
    zero_plane = jnp.zeros((1, flat), field.dtype)
    total = jnp.concatenate([zero_plane, field[:-1]], 0) + jnp.concatenate(
        [field[1:], zero_plane], 0
    )
    zero_rows = jnp.zeros((depth, NX), field.dtype)
    total = (
        total
        + jnp.concatenate([zero_rows, field[:, :-NX]], 1)
        + jnp.concatenate([field[:, NX:], zero_rows], 1)
    )
    column = jnp.arange(flat) % NX
    zero_col = jnp.zeros((depth, 1), field.dtype)
    left = jnp.concatenate([zero_col, field[:, :-1]], 1) * (column > 0).astype(field.dtype)
    right = jnp.concatenate([field[:, 1:], zero_col], 1) * (column < NX - 1).astype(field.dtype)
    return total + left + right


def solve(psi, perturb, potential, energy):
    diag = 3.25 + potential - energy
    source = -perturb * psi
    answer = jnp.zeros_like(psi)
    for step in range(STEPS):
        weight = 1.0 / (1.0 + 0.8 * jnp.cos(jnp.pi * (2 * step + 1) / (2 * STEPS)))
        applied = diag * answer - 0.5 * neighbours(answer)
        answer = answer + weight * (source - applied) / diag
    return answer


def sine_basis(count):
    index = jnp.arange(count, dtype=jnp.float32) + 1.0
    return jnp.sqrt(2.0 / (count + 1)) * jnp.sin(
        jnp.pi * index[:, None] * index[None, :] / (count + 1)
    )


def eigen_of(position, count):
    return 2.0 - 2.0 * jnp.cos(jnp.pi * (position.astype(jnp.float32) + 1.0) / (count + 1))


def planes(field):
    high = lax.Precision.HIGHEST
    depth = field.shape[0]
    cube = field.reshape(depth, NY, NX)
    cube = jnp.einsum("zyx,cx->zyc", cube, sine_basis(NX), precision=high)
    cube = jnp.einsum("zyc,by->zbc", cube, sine_basis(NY), precision=high)
    return cube.reshape(depth, NY * NX)


def scale_columns(columns, start):
    high = lax.Precision.HIGHEST
    width = columns.shape[1]
    position = start + jnp.arange(width)
    denom = (
        eigen_of(jnp.arange(NZ), NZ)[:, None]
        + eigen_of(position // NX, NY)[None, :]
        + eigen_of(position % NX, NX)[None, :]
    )
    basis = sine_basis(NZ)
    spectral = jnp.dot(basis, columns, precision=high) * (jnp.sqrt(4.0 * jnp.pi) / jnp.sqrt(denom))
    return jnp.dot(basis, spectral, precision=high)


def coulomb_slab(slab):
    columns = lax.all_to_all(planes(slab), "orb", split_axis=1, concat_axis=0, tiled=True)
    scaled = scale_columns(columns, lax.axis_index("orb") * columns.shape[1])
    back = lax.all_to_all(scaled, "orb", split_axis=0, concat_axis=1, tiled=True)
    return planes(back)


def factorize(partial_gram):
    lower = jnp.linalg.cholesky(partial_gram / (NZ * NY * NX))
    inverse = lax.linalg.triangular_solve(
        lower, jnp.eye(lower.shape[0], dtype=jnp.float32), left_side=True, lower=True
    )
    return (lower, inverse)


def general_body(orbitals, energies, trial_potential, local_potential):
    high = lax.Precision.HIGHEST
    depth = local_potential.shape[0]
    plane_cells = local_potential.shape[1]
    vector_slab = trial_potential.reshape(depth, plane_cells)
    perturb_full, potential_full = (
        lax.all_gather(vector_slab, "orb", axis=0, tiled=True),
        lax.all_gather(local_potential, "orb", axis=0, tiled=True),
    )
    perturb = perturb_full.astype(jnp.float32)
    potential = potential_full.astype(jnp.float32)
    weight = 4.0 / (orbitals.shape[0] * lax.axis_size("orb"))
    psi = orbitals[0].astype(jnp.float32)
    partial_value = psi * solve(psi, perturb, potential, energies[0])
    partial_value = partial_value * weight
    slab = lax.psum_scatter(partial_value, "orb", scatter_dimension=0, tiled=True)
    slab = coulomb_slab(slab)
    mine = slab.reshape(1, depth, plane_cells)
    gathered = lax.all_gather(mine, "vec", axis=0, tiled=True)
    flat = gathered.reshape(gathered.shape[0], depth * plane_cells)
    partial_gram = jnp.dot(flat, flat.T, precision=high)
    lower, inverse = factorize(lax.psum(partial_gram, "orb"))
    row = lax.dynamic_slice_in_dim(inverse, lax.axis_index("vec"), 1, 0)
    ortho = jnp.dot(row, flat, precision=high).reshape(1, depth, plane_cells)
    return (ortho, lower.T)


TILES = 3
GROUP = 4
SUB = 8
ROWS = GROUP * SUB
WTILES = TILES * SUB
HALO = STEPS - 1
TAILS = 4


def fits(orb, vec, norb, nv):
    return (
        norb == orb
        and nv == vec
        and orb % 2 == 0
        and NZ % orb == 0
        and NZ // orb >= 4
        and NZ // orb % 2 == 0
        and NY == vec * (ROWS - 2 * GROUP)
        and NY == TILES * ROWS
        and vec * ROWS == LANES
        and NX * GROUP == TILES * LANES
        and NX % (orb * vec) == 0
        and NZ % (orb * vec) == 0
        and STEPS <= GROUP
        and NZ // orb == TAILS * TILES
        and vec == GROUP
    )


def split(x):
    high = x.astype(BF16)
    return high, (x - high.astype(F32)).astype(BF16)


def np_split(x):
    x = np.asarray(x, np.float64)
    high = x.astype(ml_dtypes.bfloat16)
    return np.stack([high, (x - high.astype(np.float64)).astype(ml_dtypes.bfloat16)])


def dot3(a, b, dims):
    one = functools.partial(
        lax.dot_general, dimension_numbers=(dims, ((), ())), preferred_element_type=F32
    )
    if dims[0] == (1,) and a[0].shape[1] == LANES:
        return one(jnp.concatenate([a[0], a[0], a[1]], 1), jnp.concatenate([b[0], b[1], b[0]], dims[1][0]))
    return one(a[0], b[0]) + (one(a[0], b[1]) + one(a[1], b[0]))


def np_basis(count):
    index = np.arange(count, dtype=np.float64) + 1.0
    return np.sqrt(2.0 / (count + 1)) * np.sin(np.pi * np.outer(index, index) / (count + 1))


def np_eigen(count):
    return 4.0 * np.sin(np.pi * (np.arange(count, dtype=np.float64) + 1.0) / (2 * (count + 1))) ** 2


def to_rows(tiles):
    lane = lax.broadcasted_iota(jnp.int32, tiles[0].shape, 1)
    a, b, c = tiles
    return [
        a,
        pltpu.roll(jnp.where(lane >= 96, a, b), 32, 1),
        pltpu.roll(jnp.where(lane >= 64, b, c), 64, 1),
        pltpu.roll(c, 96, 1),
    ]


def to_tiles(rows):
    lane = lax.broadcasted_iota(jnp.int32, rows[0].shape, 1)
    r1, r2 = pltpu.roll(rows[1], 96, 1), pltpu.roll(rows[2], 64, 1)
    return [
        jnp.where(lane < 96, rows[0], r1),
        jnp.where(lane < 64, r1, r2),
        jnp.where(lane < 32, r2, pltpu.roll(rows[3], 32, 1)),
    ]


def first_tile(strip):
    return strip * (WTILES - 2 * TILES) - TILES


def window_start(strip):
    return jnp.clip(first_tile(strip), 0, NY * NX // LANES - WTILES)


def tile_lanes(strip, t, start=0):
    tile = jnp.clip(first_tile(strip) + t, 0, NY * NX // LANES - 1) - start
    return pl.ds(pl.multiple_of(tile * LANES, LANES), LANES)


def pack_planes(src, plane, out, pairs):
    def one(pair, carry):
        for i in range(TILES):
            top = pl.multiple_of((plane + 2 * pair) * WTILES + i * SUB, SUB)
            low = pl.multiple_of((plane + 2 * pair + 1) * WTILES + i * SUB, SUB)
            block = jnp.concatenate([src[pl.ds(top, SUB), :], src[pl.ds(low, SUB), :]], 0)
            out[pair, i] = block.astype(BF16)
        return carry

    lax.fori_loop(0, pairs, one, 0)


def windows_kernel(orb, vec, energy_any, psi_any, v_any, pot_any, *refs):
    outs, (planes_ref, more_ref, pot_rows_ref, psi_ref, v_ref, pot_ref, energy_ref, sem) = refs[:-8], refs[-8:]
    tiles = NY * NX // LANES
    chips = orb // 2
    slab = NZ // chips
    depth = v_ref.shape[0]
    chip = lax.axis_index("orb") // 2
    strip = lax.axis_index("vec")
    start = window_start(strip)
    lanes = pl.ds(pl.multiple_of(start * LANES, LANES), WTILES * LANES)
    copies = [
        pltpu.make_async_copy(v_any.at[0], v_ref, sem.at[0]),
        pltpu.make_async_copy(pot_any.at[:, lanes], pot_ref, sem.at[1]),
        pltpu.make_async_copy(psi_any.at[0, :, lanes], psi_ref, sem.at[2]),
        pltpu.make_async_copy(energy_any, energy_ref, sem.at[3]),
    ]
    for copy in copies:
        copy.start()
    more_ref[:SUB, :] = jnp.zeros((SUB, LANES), F32)
    more_ref[SUB + depth * tiles :, :] = jnp.zeros((SUB, LANES), F32)
    for copy in copies[:2]:
        copy.wait()
    for tile in range(tiles):
        more_ref[pl.ds(SUB + tile, depth, tiles), :] = v_ref[:, tile * LANES : (tile + 1) * LANES].astype(F32)
    for t in range(WTILES):
        row = (t % TILES) * SUB + t // TILES
        pot_rows_ref[pl.ds(row, depth, WTILES), :] = pot_ref[:, tile_lanes(strip, t, start)].astype(F32)
    for n in range(vec):
        first = SUB + first_tile(lax.rem(strip + n, vec))
        for pair in range(depth // 2):
            for i in range(TILES):
                block = [more_ref[pl.ds(first + i + (2 * pair + zz) * tiles, SUB, TILES), :] for zz in range(2)]
                outs[chips + n][pair, i] = jnp.concatenate(block, 0).astype(BF16)
    pack_planes(pot_rows_ref, 0, outs[chips + vec], depth // 2)
    zero = jnp.zeros((HALO * WTILES, LANES), F32)
    planes_ref[: HALO * WTILES, :] = zero
    planes_ref[(NZ + HALO) * WTILES :, :] = zero
    for copy in copies[2:]:
        copy.wait()
    for t in range(WTILES):
        row = HALO * WTILES + (t % TILES) * SUB + t // TILES
        planes_ref[pl.ds(row, NZ, WTILES), :] = psi_ref[:, tile_lanes(strip, t, start)].astype(F32)
    energy = jnp.full((1, LANES), energy_ref[0], F32)
    high = energy.astype(BF16).astype(F32)
    middle = (energy - high).astype(BF16).astype(F32)
    low = energy - high - middle
    lane = lax.broadcasted_iota(jnp.int32, (1, LANES), 1)
    for at in range(chips):
        row = at * slab * WTILES
        held = planes_ref[row : row + 1, :]
        held = jnp.where(lane == 0, high, jnp.where(lane == 1, middle, jnp.where(lane == 2, low, held)))
        planes_ref[row : row + 1, :] = held
    for shift in range(chips):
        pack_planes(planes_ref, ((chip + shift) % chips) * slab, outs[shift], (slab + 2 * HALO) // 2)


def windows(orbitals, energies, trial, potential, orb, vec):
    chips = orb // 2
    depth = potential.shape[0]
    block = (TILES, 2 * SUB, LANES)
    pairs = (NZ // chips + 2 * HALO) // 2
    outs = [jax.ShapeDtypeStruct((pairs, *block), BF16)] * chips
    outs += [jax.ShapeDtypeStruct((depth // 2, *block), BF16)] * (vec + 1)
    got = pl.pallas_call(
        functools.partial(windows_kernel, orb, vec),
        out_shape=outs,
        in_specs=[pl.BlockSpec(memory_space=pl.ANY)] + [pl.BlockSpec(memory_space=pltpu.HBM)] * 3,
        out_specs=[pl.BlockSpec(memory_space=pltpu.VMEM)] * len(outs),
        scratch_shapes=[
            pltpu.VMEM(((NZ + 2 * HALO) * WTILES, LANES), F32),
            pltpu.VMEM((depth * NY * NX // LANES + 2 * SUB, LANES), F32),
            pltpu.VMEM((depth * WTILES, LANES), F32),
            pltpu.VMEM((NZ, WTILES * LANES), BF16),
            pltpu.VMEM((depth, NY * NX), BF16),
            pltpu.VMEM((depth, WTILES * LANES), BF16),
            pltpu.SMEM((1,), F32),
            pltpu.SemaphoreType.DMA((4,)),
        ],
        compiler_params=pltpu.CompilerParams(vmem_limit_bytes=24 << 20),
        name="windows",
    )(energies, *(pltpu.with_memory_space_constraint(x, pltpu.HBM) for x in (orbitals, trial, potential)))
    return list(got[:chips]), list(got[chips:])


def edges_kernel(n, parts_and_more, *refs):
    parts, (own_ref, edge_ref) = refs[:n], refs[parts_and_more:]
    core = lax.axis_index("orb") % 2
    first = core * (own_ref.shape[1] - edge_ref.shape[1])
    for i, part in enumerate(parts):
        own_ref[i] = part[...]
        edge_ref[i] = part[pl.ds(first, edge_ref.shape[1])]


def edges(parts, arrived):
    pairs, *block = parts[0].shape
    n = len(parts)
    more = n + len(arrived)
    return pl.pallas_call(
        functools.partial(edges_kernel, n, more),
        out_shape=[
            jax.ShapeDtypeStruct((n, pairs, *block), BF16),
            jax.ShapeDtypeStruct((n, GROUP // 2, *block), BF16),
        ],
        in_specs=[pl.BlockSpec(memory_space=pltpu.VMEM)] * more,
        out_specs=[pl.BlockSpec(memory_space=pltpu.VMEM)] * 2,
        compiler_params=pltpu.CompilerParams(vmem_limit_bytes=24 << 20),
        name="edges",
    )(*parts, *arrived)


def with_edge_kernel(n, own_ref, edge_ref, *refs):
    out_ref = refs[n]
    core = lax.axis_index("orb") % 2
    pairs, edge = own_ref.shape[1], edge_ref.shape[1]
    out_ref[:, pl.ds((1 - core) * edge, pairs)] = own_ref[...]
    out_ref[:, pl.ds(core * pairs, edge)] = edge_ref[...]


def with_edge(own, edge, arrived):
    n, pairs, *block = own.shape
    return pl.pallas_call(
        functools.partial(with_edge_kernel, len(arrived)),
        out_shape=jax.ShapeDtypeStruct((n, pairs + edge.shape[1], *block), own.dtype),
        in_specs=[pl.BlockSpec(memory_space=pltpu.VMEM)] * (2 + len(arrived)),
        out_specs=pl.BlockSpec(memory_space=pltpu.VMEM),
        compiler_params=pltpu.CompilerParams(vmem_limit_bytes=24 << 20),
        name="with_edge",
    )(own, edge, *arrived)


def potential_rows_kernel(vec, n, mine_ref, other_ref, *refs):
    v_ref, d_ref = refs[n:]
    core = lax.axis_index("orb") % 2
    strip = lax.axis_index("vec")
    pairs = mine_ref.shape[1]
    for src, first in ((mine_ref, core * pairs), (other_ref, (1 - core) * pairs)):

        def one(pair, carry, src=src, first=first):
            plane = 2 * (first + pair)
            for n in range(vec + 1):
                rows = to_rows([src[n, pair, i].astype(F32) for i in range(TILES)])
                for zz in range(2):
                    block = jnp.concatenate([rows[i][zz * SUB : (zz + 1) * SUB] for i in range(GROUP)], 0)
                    if n < vec:
                        k = lax.rem(strip - n + vec, vec)
                        v_ref[plane + zz, pl.ds(pl.multiple_of(k * ROWS, ROWS), ROWS), :] = block
                    else:
                        d_ref[plane + zz] = 3.25 + block
            return carry

        lax.fori_loop(0, pairs, one, 0, unroll=True)


def potential_rows(mine, other, vec, arrived):
    planes = 4 * mine.shape[1]
    return pl.pallas_call(
        functools.partial(potential_rows_kernel, vec, len(arrived)),
        out_shape=[
            jax.ShapeDtypeStruct((planes, vec * ROWS, LANES), F32),
            jax.ShapeDtypeStruct((planes, ROWS, LANES), F32),
        ],
        in_specs=[pl.BlockSpec(memory_space=pltpu.VMEM)] * (2 + len(arrived)),
        out_specs=[pl.BlockSpec(memory_space=pltpu.VMEM)] * 2,
        compiler_params=pltpu.CompilerParams(vmem_limit_bytes=24 << 20),
        name="potential_rows",
    )(mine, other, *arrived)


def solve_kernel(vec, first, part, *refs):
    psi_ref, v_ref, d_ref = refs[:3]
    refs = refs[3:]
    sum_ref = None if first else refs[0]
    out_ref, psi_s, h_s, c_s, u_a, u_b = refs[-6:]
    planes = d_ref.shape[0]
    depth = (planes - 2 * GROUP) // 2
    core = lax.axis_index("orb") % 2
    begins = {None: 0, "own": core * depth, "other": (1 - core) * depth}[part]
    count = 2 * depth if part is None else depth
    top = (lax.axis_index("orb") // 2) * 2 * depth - GROUP
    top_row = lax.axis_index("vec") * (ROWS - 2 * GROUP) - GROUP
    lane = lax.broadcasted_iota(jnp.int32, (SUB, LANES), 1)
    group = lax.broadcasted_iota(jnp.int32, (SUB, LANES), 0)
    inside = []
    for i in range(GROUP):
        y = top_row + group * GROUP + i
        inside.append(jnp.where((y >= 0) & (y < NY) & (lane < NX), 0.5, 0.0))
    inside = jnp.concatenate(inside, 0)
    block = psi_ref[0, 0].astype(F32)
    energy = block[0:1, 0:1] + block[0:1, 1:2] + block[0:1, 2:3]
    at = lax.broadcasted_iota(jnp.int32, (2 * LANES, LANES), 0) % LANES
    to = lax.broadcasted_iota(jnp.int32, (2 * LANES, LANES), 1)
    beside = jnp.where((at == to - 1) | (at == to + 1), 1.0, 0.0).astype(BF16)

    def begin(pair, carry):
        rows = to_rows([psi_ref[begins // 2 + pair, i].astype(F32) for i in range(TILES)])
        for zz in range(2):
            w = GROUP - HALO + begins + 2 * pair + zz
            z = top + w
            there = jnp.where((z >= 0) & (z < NZ), 1.0, 0.0)
            psi = jnp.concatenate([rows[i][zz * SUB : (zz + 1) * SUB] for i in range(GROUP)], 0)
            h = inside * there / (d_ref[w] - energy)
            psi_s[w] = SCALES[STEPS - 1] * psi
            h_s[w] = h
            scaled = -2.0 * psi * h
            for k in range(vec):
                rows_k = pl.ds(k * ROWS, ROWS)
                c_s[w, rows_k, :] = scaled * v_ref[w, rows_k, :]
        return carry

    lax.fori_loop(0, (count + 2 * HALO) // 2, begin, 0, unroll=True)

    def stepped(src, w, step):
        u = src[w]
        high, low = split(u)
        x = jnp.dot(jnp.concatenate([high, low], 1), beside, preferred_element_type=F32)
        near = x + (src[w - 1] + src[w + 1])
        own, given, around = COEFFICIENTS[step]
        h = around * h_s[w]
        new = []
        for k in range(vec):
            rows = [u[k * ROWS + i * SUB : k * ROWS + (i + 1) * SUB] for i in range(GROUP)]
            north = jnp.concatenate([pltpu.roll(rows[-1], 1, 0)] + rows[:-1], 0)
            south = jnp.concatenate(rows[1:] + [pltpu.roll(rows[0], SUB - 1, 0)], 0)
            at_k = slice(k * ROWS, (k + 1) * ROWS)
            change = h * (near[at_k] + (north + south))
            if src is c_s:
                new.append((own + given) * u[at_k] + change)
            else:
                new.append((u[at_k] + given * c_s[w, at_k, :]) + change)
        return new

    src, dst = c_s, u_a
    for step in range(1, STEPS - 1):
        low = GROUP - HALO + step

        def middle(p, carry, src=src, dst=dst, step=step, low=low):
            w = begins + low + p
            dst[w] = jnp.concatenate(stepped(src, w, step), 0)
            return carry

        lax.fori_loop(0, count + 2 * (HALO - step), middle, 0, unroll=True)
        src, dst = dst, (u_b if dst is u_a else u_a)

    def end(p, carry, src=src):
        w = GROUP + begins + p
        psi = psi_s[w]
        total = jnp.concatenate([psi * new for new in stepped(src, w, STEPS - 1)], 0)
        if not first:
            total = total + sum_ref[begins + p]
        out_ref[p] = total
        return carry

    lax.fori_loop(0, count, end, 0, unroll=True)


def solve_window(psi, v, d, total, vec, part=None):
    planes = d.shape[0]
    depth = (planes - 2 * GROUP) // 2
    args = (psi, v, d) if total is None else (psi, v, d, total)
    return pl.pallas_call(
        functools.partial(solve_kernel, vec, total is None, part),
        out_shape=jax.ShapeDtypeStruct((2 * depth if part is None else depth, LANES, LANES), F32),
        in_specs=[pl.BlockSpec(memory_space=pltpu.VMEM)] * len(args),
        out_specs=pl.BlockSpec(memory_space=pltpu.VMEM),
        scratch_shapes=[pltpu.VMEM((planes, ROWS, LANES), F32)] * 2
        + [pltpu.VMEM((planes, vec * ROWS, LANES), F32)] * 3,
        compiler_params=pltpu.CompilerParams(vmem_limit_bytes=32 << 20),
        name="solve_window",
    )(*args)


def forward_x_kernel(ndev, basis_ref, own_ref, other_ref, out_ref):
    depth = own_ref.shape[0] // LANES
    inner = depth - depth // TAILS
    rows = out_ref.shape[0] // ndev
    vecrows = LANES // SUB
    basis = (basis_ref[0], basis_ref[1])
    lane = lax.broadcasted_iota(jnp.int32, (NX, LANES), 1)
    pad = jnp.zeros((LANES - (SUB - 2) * vecrows, LANES), F32)
    got = []
    for z in range(depth):
        groups = [pl.ds(z * LANES + g, vecrows, SUB) for g in range(1, SUB - 1)]
        chi = jnp.concatenate([own_ref[g, :] + other_ref[g, :] for g in groups] + [pad], 0)
        got.append(dot3(basis, split(chi), ((1,), (1,))))
    for z in range(inner):
        whole, third = inner + z // TILES, z % TILES
        tail = pltpu.roll(got[whole], LANES - LANES // TAILS * (third + 1), 1)
        row = jnp.where(lane < LANES - LANES // TAILS, got[z], tail)
        for part in range(NX // ndev):
            out_ref[pl.ds(part * inner + z, ndev, rows), :] = row[part * ndev : (part + 1) * ndev]


def forward_x(own, other, basis, ndev):
    depth = own.shape[0]
    rows = -(-(NX // ndev) * (depth - depth // TAILS) // 4) * 4
    out = pl.pallas_call(
        functools.partial(forward_x_kernel, ndev),
        out_shape=jax.ShapeDtypeStruct((ndev * rows, LANES), F32),
        in_specs=[pl.BlockSpec(memory_space=pltpu.VMEM)] * 3,
        out_specs=pl.BlockSpec(memory_space=pltpu.VMEM),
        compiler_params=pltpu.CompilerParams(vmem_limit_bytes=24 << 20),
        name="forward_x",
    )(basis, own.reshape(-1, LANES), other.reshape(-1, LANES))
    return out.reshape(ndev, rows // 4, 4, LANES)


def spectral_kernel(orb, vec, rows, mux_ref, muzy_ref, wy_ref, kz_ref, kzb_ref, wyb_ref, got_ref, out_ref):
    ndev = orb * vec
    parts = NX // ndev
    me = lax.axis_index("orb") * vec + lax.axis_index("vec")
    inner = NZ // orb - NZ // orb // TAILS
    lane = lax.broadcasted_iota(jnp.int32, (orb, LANES), 1)
    strips = []
    for v in range(vec):
        main = [got_ref[pl.ds(v * rows + r, orb, vec * rows), :] for r in range(parts * inner)]
        tails = []
        for r in range(0, parts * inner, TILES):
            tail = pltpu.roll(main[r], LANES // TAILS, 1)
            for p in range(1, TILES):
                third = pltpu.roll(main[r + p], (p + 1) * LANES // TAILS, 1)
                tail = jnp.where(lane >= p * LANES // TAILS, third, tail)
            tails.append(tail)
        strips.append(jnp.concatenate(main + tails, 0))
    mm = ((1,), (0,))
    t = dot3(split(jnp.concatenate(strips, 1)), (wy_ref[0], wy_ref[1]), mm)
    t = dot3((kz_ref[0], kz_ref[1]), split(t), mm)
    scale = jnp.concatenate(
        [
            math.sqrt(4.0 * math.pi) / jnp.sqrt(muzy_ref[...] + mux_ref[part * ndev + me])
            for part in range(parts)
        ],
        0,
    )
    fields = [t[:, k * LANES : (k + 1) * LANES] * scale for k in range(vec)]
    lane = lax.broadcasted_iota(jnp.int32, (1, LANES), 1)
    gram = jnp.zeros((1, LANES), F32)
    for k in range(vec):
        for l in range(k + 1):
            entry = jnp.sum(jnp.sum(fields[k] * fields[l], axis=0, keepdims=True), axis=1, keepdims=True)
            gram = jnp.where(lane == k * vec + l, entry, gram)
    t = jnp.concatenate(fields, 1)
    t = jnp.concatenate(
        [dot3((kzb_ref[0], kzb_ref[1]), split(t[part * NZ : (part + 1) * NZ]), mm) for part in range(parts)], 0
    )
    t = dot3(split(t), (wyb_ref[0], wyb_ref[1]), mm)
    rows = out_ref.shape[0] // ndev
    zs = NZ // ndev
    for part in range(parts):
        for z in range(zs):
            for yt in range(TILES):
                out_ref[pl.ds((z * parts + part) * TILES + yt, ndev, rows), :] = t[
                    (part * zs + z) * ndev : (part * zs + z + 1) * ndev, yt * LANES : (yt + 1) * LANES
                ]
    out_ref[pl.ds(zs * parts * TILES, ndev, rows), :] = jnp.broadcast_to(gram, (ndev, LANES))


def spectral(got, orb, vec):
    ndev = orb * vec
    parts, zs = NX // ndev, NZ // ndev
    depth = NZ // orb
    quarter = depth // TAILS
    inner = depth - quarter
    strip = ROWS - 2 * GROUP
    rows_in = got.shape[1] * got.shape[2]
    rows_out = -(-(parts * zs * TILES + 1) // 4) * 4
    sy, sz = np_basis(NY), np_basis(NZ)
    wy = np.zeros((vec, LANES, vec, LANES))
    wyb = np.zeros((vec, LANES, TILES, vec, GROUP, SUB))
    for k in range(vec):
        for i in range(GROUP):
            for g in range(SUB):
                for v in range(vec):
                    if g < SUB - 2:
                        wy[v, (g * vec + k) * GROUP + i, k, :NY] = sy[v * strip + GROUP * g + i]
                for yt in range(TILES):
                    wyb[k, :NY, yt, k, i, g] = sy[yt * ROWS + GROUP * g + i]
    wy = wy.reshape(vec * LANES, vec * LANES)
    wyb = wyb.reshape(vec * LANES, TILES * LANES)
    kz = np.zeros((parts, NZ, parts, inner, orb))
    kzt = np.zeros((parts, NZ, parts, quarter, orb))
    for part in range(parts):
        for o in range(orb):
            mine = sz[:, o * depth : (o + 1) * depth]
            kz[part, :, part, :, o] = mine[:, :inner]
            kzt[part, :, part, :, o] = mine[:, inner:]
    kz = np.concatenate([kz.reshape(parts * NZ, -1), kzt.reshape(parts * NZ, -1)], 1)
    kzb = np.concatenate([sz[z::zs] for z in range(zs)])
    muzy = np.ones((NZ, LANES), np.float32)
    muzy[:, :NY] = np_eigen(NZ)[:, None] + np_eigen(NY)[None, :]
    mux = np_eigen(NX).astype(np.float32)
    out = pl.pallas_call(
        functools.partial(spectral_kernel, orb, vec, rows_in),
        out_shape=jax.ShapeDtypeStruct((ndev * rows_out, LANES), F32),
        in_specs=[pl.BlockSpec(memory_space=pltpu.SMEM)] + [pl.BlockSpec(memory_space=pltpu.VMEM)] * 6,
        out_specs=pl.BlockSpec(memory_space=pltpu.VMEM),
        compiler_params=pltpu.CompilerParams(vmem_limit_bytes=32 << 20),
        name="spectral",
    )(mux, muzy, np_split(wy), np_split(kz), np_split(kzb), np_split(wyb), got.reshape(-1, LANES))
    return out.reshape(ndev, rows_out // 4, 4, LANES)


def back_kernel(ndev, vec, basis_ref, got_ref, factor_ref, *outs):
    parts, zs = NX // ndev, NZ // ndev
    rows = got_ref.shape[0] // ndev
    strip = lax.axis_index("vec")
    basis = (basis_ref[0], basis_ref[1])
    gram = jnp.sum(got_ref[pl.ds(zs * parts * TILES, ndev, rows), :], axis=0, keepdims=True)
    gram = gram / (NZ * NY * NX)
    entry = lambda k, l: gram[:, k * vec + l : k * vec + l + 1]
    lower = [[None] * vec for _ in range(vec)]
    inverse = [[jnp.zeros((1, 1), F32)] * vec for _ in range(vec)]
    for l in range(vec):
        pivot = entry(l, l)
        for m in range(l):
            pivot = pivot - lower[l][m] * lower[l][m]
        lower[l][l] = jnp.sqrt(pivot)
        inverse[l][l] = 1.0 / lower[l][l]
        for k in range(l + 1, vec):
            value = entry(k, l)
            for m in range(l):
                value = value - lower[k][m] * lower[l][m]
            lower[k][l] = value * inverse[l][l]
    for l in range(vec):
        for k in range(l + 1, vec):
            value = lower[k][l] * inverse[l][l]
            for m in range(l + 1, k):
                value = value + lower[k][m] * inverse[m][l]
            inverse[k][l] = -value * inverse[k][k]
    at_row = lax.broadcasted_iota(jnp.int32, (vec, vec), 0)
    at_col = lax.broadcasted_iota(jnp.int32, (vec, vec), 1)
    factor = jnp.zeros((vec, vec), F32)
    for k in range(vec):
        for l in range(k + 1):
            factor = jnp.where((at_row == l) & (at_col == k), lower[k][l], factor)
    factor_ref[...] = factor
    coefficients = []
    for s in range(vec):
        to = lax.rem(strip + s, vec)
        line = []
        for k in range(vec):
            value = inverse[0][k]
            for m in range(1, vec):
                value = jnp.where(to == m, inverse[m][k], value)
            line.append(value)
        coefficients.append(line)
    for z in range(zs):
        columns = [
            jnp.concatenate(
                [got_ref[pl.ds((z * parts + part) * TILES + yt, ndev, rows), :] for part in range(parts)], 0
            )
            for yt in range(TILES)
        ]
        fields = dot3(split(jnp.concatenate(columns, 1)), basis, ((0,), (0,)))
        for yt in range(TILES):
            y = fields[yt * LANES : (yt + 1) * LANES]
            for s in range(vec):
                mixed = coefficients[s][0] * y[:ROWS]
                for k in range(1, vec):
                    mixed = mixed + coefficients[s][k] * y[k * ROWS : (k + 1) * ROWS]
                tiles = to_tiles([mixed[i * SUB : (i + 1) * SUB] for i in range(GROUP)])
                for i in range(TILES):
                    outs[s][pl.ds((z * TILES + yt) * WTILES + i, SUB, TILES), :] = tiles[i]


def back(got, basis, ndev, vec):
    zs = NZ // ndev
    tiles = NY * NX // LANES
    return pl.pallas_call(
        functools.partial(back_kernel, ndev, vec),
        out_shape=[jax.ShapeDtypeStruct((vec, vec), F32)]
        + [jax.ShapeDtypeStruct((zs * tiles, LANES), F32)] * vec,
        in_specs=[pl.BlockSpec(memory_space=pltpu.VMEM)] * 2,
        out_specs=[pl.BlockSpec(memory_space=pltpu.VMEM)] * (vec + 1),
        compiler_params=pltpu.CompilerParams(vmem_limit_bytes=24 << 20),
        name="back",
    )(basis, got.reshape(-1, LANES))


def assemble_kernel(vec, *refs):
    gots, (out_any, sem) = refs[:vec], refs[vec:]
    strip = lax.axis_index("vec")
    rows = gots[0].shape[0]
    copies = []
    for s in range(vec):
        start = pl.multiple_of(lax.rem(strip - s + vec, vec) * rows, 8)
        copies.append(pltpu.make_async_copy(gots[s], out_any.at[pl.ds(start, rows)], sem.at[s]))
    for copy in copies:
        copy.start()
    for copy in copies:
        copy.wait()


def assemble(gots):
    vec = len(gots)
    rows = gots[0].shape[0] * vec
    out = pl.pallas_call(
        functools.partial(assemble_kernel, vec),
        out_shape=jax.ShapeDtypeStruct((rows, LANES), F32),
        in_specs=[pl.BlockSpec(memory_space=pltpu.VMEM)] * vec,
        out_specs=pl.BlockSpec(memory_space=pltpu.HBM),
        scratch_shapes=[pltpu.SemaphoreType.DMA((vec,))],
        compiler_params=pltpu.CompilerParams(vmem_limit_bytes=24 << 20),
        name="assemble",
    )(*gots)
    return out.reshape(1, rows * LANES // (NY * NX), NY * NX)


def swap_cores(x, orb):
    return lax.ppermute(x, "orb", [(o, o ^ 1) for o in range(orb)])


def shift(x, axis, count):
    n = lax.axis_size(axis)
    return lax.ppermute(x, axis, [(i, (i + count) % n) for i in range(n)])


def responses(orbitals, energies, trial_potential, local_potential):
    orb, vec = lax.axis_size("orb"), lax.axis_size("vec")
    chips = orb // 2
    psis, parts = windows(orbitals, energies, trial_potential, local_potential, orb, vec)
    def to_chip(r):
        perm = [(2 * a + c, 2 * ((a + r) % chips) + c) for a in range(chips) for c in range(2)]
        return lax.ppermute(psis[r], "orb", perm)

    order = [1, chips - 1, *range(2, chips - 1)]
    for r in order:
        psis[r] = to_chip(r)
    for n in range(1, vec):
        parts[n] = shift(parts[n], "vec", n)
    arrived = [psis[r] for r in order]
    own, edge = edges(parts, [])
    near = [(o, o + 1) for o in range(1, orb - 1, 2)] + [(o + 1, o) for o in range(1, orb - 1, 2)]
    edge = lax.ppermute(edge, "orb", near + [(0, 0), (orb - 1, orb - 1)])
    mine = with_edge(own, edge, arrived[:2])
    v, d = potential_rows(mine, swap_cores(mine, orb), vec, [])
    total = None
    for r in [0] + order[:-1]:
        total = solve_window(psis[r], v, d, total, vec)
    last = psis[order[-1]]
    other = swap_cores(solve_window(last, v, d, total, vec, "other"), orb)
    return solve_window(last, v, d, total, vec, "own"), other


def block_body(orbitals, energies, trial_potential, local_potential):
    orb, vec = lax.axis_size("orb"), lax.axis_size("vec")
    ndev = orb * vec
    both = ("orb", "vec")
    own, other = responses(orbitals, energies, trial_potential, local_potential)
    sx = np_basis(NX)
    padded = np.zeros((NX, LANES))
    padded[:, :NX] = sx
    sent = forward_x(own, other, np_split(padded * (4.0 / orb)), ndev)
    got = lax.all_to_all(sent, both, 0, 0, tiled=True)
    sent = spectral(got, orb, vec)
    got = lax.all_to_all(sent, both, 0, 0, tiled=True)
    factor, *slots = back(got, np_split(padded), ndev, vec)
    gots = [slots[0]] + [shift(slots[s], "vec", s) for s in range(1, vec)]
    return assemble(gots), factor


def solution(mesh):
    orb, vec = mesh.shape["orb"], mesh.shape["vec"]
    placed = (P("orb", None, None), P("orb"), P("vec", "orb", None), P("orb", None))

    def body(orbitals, energies, trial_potential, local_potential):
        one = orbitals.shape[0] == 1 and trial_potential.shape[0] == 1
        plan = block_body if one and fits(orb, vec, orb, vec) else general_body
        return plan(orbitals, energies, trial_potential, local_potential)

    return jax.shard_map(
        body, mesh=mesh, in_specs=placed, out_specs=(P("vec", "orb", None), P()), check_vma=False
    )
```
